32 devices in a mesh: dp: 8 (over z, y), ctx: 2 (over x), tp: 2 (over core).
Axes of the slice: x: 2, y: 2, z: 4, core: 2. Of those that a mesh axis runs over, the one named last changes fastest.
Arguments:
- hidden_in: bfloat16 [8192, 1024], P(('dp', 'ctx')), may hold values from -6 to 6
- encoder_states: bfloat16 [4096, 1024], P(('dp', 'ctx')), may hold values from -6 to 6
- out_grad: bfloat16 [8192, 1024], P(('dp', 'ctx')), may hold values from -6 to 6
- target_ids: int32 [8, 1024], P('dp'), may hold values from 0 to 3, never falling along the last dimension, each value on 1 to 800 neighbouring positions
- source_ids: int32 [8, 512], P('dp'), may hold values from 0 to 3, never falling along the last dimension, each value on 1 to 400 neighbouring positions
- self_in: bfloat16 [3, 1024, 1024], P(None, 'dp', 'tp'), may hold values from -0.1875 to 0.1875
- self_out: bfloat16 [1024, 1024], P('tp', 'dp'), may hold values from -1.5 to 1.5
- cross_in: bfloat16 [3, 1024, 1024], P(None, 'dp', 'tp'), may hold values from -0.1875 to 0.1875
- cross_out: bfloat16 [1024, 1024], P('tp', 'dp'), may hold values from -1.5 to 1.5
- ffn_in: bfloat16 [1024, 8192], P('dp', 'tp'), may hold values from -0.1875 to 0.1875
- ffn_out: bfloat16 [8192, 1024], P('tp', 'dp'), may hold values from -0.0625 to 0.0625
- norm_gain: bfloat16 [3, 1024], P(None, 'dp'), may hold values from 0.25 to 1.75
- norm_bias: bfloat16 [3, 1024], P(None, 'dp'), may hold values from -3 to 3
Outputs:
- out_hidden: bfloat16 [8192, 1024], P(('dp', 'ctx'))
- grad_hidden: float32 [8192, 1024], P(('dp', 'ctx'))
- grad_encoder: float32 [4096, 1024], P(('dp', 'ctx'))
- grad_self_in: float32 [3, 1024, 1024], P(None, 'dp', 'tp')
- grad_self_out: float32 [1024, 1024], P('tp', 'dp')
- grad_cross_in: float32 [3, 1024, 1024], P(None, 'dp', 'tp')
- grad_cross_out: float32 [1024, 1024], P('tp', 'dp')
- grad_ffn_in: float32 [1024, 8192], P('dp', 'tp')
- grad_ffn_out: float32 [8192, 1024], P('tp', 'dp')
- grad_norm_gain: float32 [3, 1024], P(None, 'dp')
- grad_norm_bias: float32 [3, 1024], P(None, 'dp')
The draws below stay inside these ranges and needn't reach their ends.
Inputs may be any that keep to these rules, and one draw needn't show every extreme that they name: `target_ids`: along each sequence the ids never fall; each of the 4 documents holds 1 to 800 decoder positions, and one holds exactly 800. `source_ids`: along each sequence the ids never fall; each of the 4 documents holds 1 to 400 encoder positions, and one holds exactly 400.
All inputs are finite; a program needn't handle non-finite values.
Results may differ from the reference program's by a relative error of at most 0.018.
Values may be sent and summed in bfloat16 or wider, within the bound.
No kernel may reach another device: no remote copies, remote signals or barrier semaphores. Data moves between devices by JAX's collectives and lax.ppermute only.
A program may use at most 256 MiB of HBM per device.

```python
import math
import jax
import jax.numpy as jnp
import numpy as np
from jax import lax

D = 1024
HEADS = 16
HEAD_DIM = 64
FF = 8192
SEQ_LEN = 1024
SRC_LEN = 512
SEQS = 8
TOKENS = 8192
SRC_TOKENS = 4096
DOCS = 4
DOC_MOST = 800
SRC_MOST = 400


def spiked(array, key, source, target, parts, factor):
    owner, partner = [(jnp.arange(array.shape[dim]) // (array.shape[dim] // parts)).reshape([-1 if axis == dim else 1 for axis in range(array.ndim)]) for dim in (source, target)]
    chosen = jax.random.permutation(key, parts)[partner]
    strong = (owner == chosen) | (owner == (partner + parts // 2) % parts)
    return jnp.where(strong, factor * array, array)


def levels(stream_key, extent, cuts, smallest, top_value):
    def one(position, parts):
        draws = jax.random.uniform(jax.random.fold_in(jax.random.fold_in(stream_key, 6), position), (parts,), jnp.float32, smallest / len(cuts), top_value / len(cuts))
        return jnp.repeat(jnp.exp(draws), extent[position] // parts).reshape((-1,) + (1,) * (len(extent) - position - 1))

    loudness = one(*cuts[0])
    for cut in cuts[1:]:
        loudness = loudness * one(*cut)
    return loudness


def split_up(number_of, total, reach, skew):
    portions = [(1 << 20) // math.isqrt(rank ** skew) + 1 for rank in range(2, number_of + 1)]
    rest, holding = total - reach - (number_of - 1), [1] * (number_of - 1)
    while rest > 0:
        movable = [i for i in range(number_of - 1) if holding[i] < reach]
        pool, left = sum([portions[i] for i in movable]), rest
        for i in movable:
            more = min(reach - holding[i], max(1, left * portions[i] // pool), rest)
            holding[i] = holding[i] + more
            rest = rest - more
    return np.array([reach] + holding)


def ragged(key, amount, total, limit, lean):
    if amount == 2:
        one = jax.random.randint(key, (), max(1, total - limit), min(limit, total - 1) + 1)
        return jnp.stack([one, total - one])
    tallies = jnp.asarray(split_up(amount, total, limit, lean), jnp.int32)
    twos = (amount - 1) // 2
    donor, sink = tallies[1:1 + 2 * twos:2], tallies[2:2 + 2 * twos:2]
    room = jnp.minimum(donor - 1, limit - sink)
    passed = jax.random.randint(jax.random.fold_in(key, 1), (twos,), 0, 1 << 20) % (room + 1)
    tallies = tallies.at[1:1 + 2 * twos:2].set(donor - passed).at[2:2 + 2 * twos:2].set(sink + passed)
    return tallies[jax.random.permutation(jax.random.fold_in(key, 2), amount)]


def bell_draw(rng, shape, scale, limit, cuts=(), kind=jnp.bfloat16):
    values = jax.random.normal(rng, shape, jnp.float32) * scale
    if len(cuts) > 0:
        values = levels(rng, shape, cuts, -0.22, 0.18) * values
    return jnp.clip(values, min=-limit, max=limit).astype(kind)


def bell_draw_with(stream_key, shape, deviation, bound, pieces, heavy, kind=jnp.bfloat16):
    entries = deviation * jax.random.normal(stream_key, shape, jnp.float32)
    if pieces:
        entries = entries * levels(stream_key, shape, pieces, -0.22, 0.18)
    return jnp.clip(spiked(entries, jax.random.fold_in(stream_key, 3), *heavy), -bound, bound).astype(kind)


def setup_inputs(seed: int = 0) -> dict:
    key_list = jax.random.split(jax.random.key(seed), 14)
    return {
        "hidden_in": bell_draw(key_list[0], (TOKENS, D), 1.0, 6.0, ((0, 16),)),
        "encoder_states": bell_draw(key_list[1], (SRC_TOKENS, D), 1.0, 6.0, ((0, 16),)),
        "out_grad": bell_draw_with(key_list[2], (TOKENS, D), 1.0, 6.0, ((0, 16),), (0, 1, 16, 2.0)),
        "target_ids": jax.vmap(lambda own: jnp.searchsorted(jnp.cumsum(ragged(own, DOCS, SEQ_LEN, DOC_MOST, 1)), jnp.arange(SEQ_LEN), side="right"))(jax.random.split(key_list[3], SEQS)).reshape((SEQS, SEQ_LEN)).astype(jnp.int32),
        "source_ids": jax.vmap(lambda own: jnp.searchsorted(jnp.cumsum(ragged(own, DOCS, SRC_LEN, SRC_MOST, 1)), jnp.arange(SRC_LEN), side="right"))(jax.random.split(key_list[4], SEQS)).reshape((SEQS, SRC_LEN)).astype(jnp.int32),
        "self_in": bell_draw(key_list[5], (3, D, D), D ** -0.5, 0.1875, ((1, 8), (2, 2))),
        "self_out": bell_draw(key_list[6], (D, D), (D // 64) ** -0.5, 1.5, ((0, 2), (1, 8))),
        "cross_in": bell_draw(key_list[7], (3, D, D), D ** -0.5, 0.1875, ((1, 8), (2, 2))),
        "cross_out": bell_draw(key_list[8], (D, D), (D // 64) ** -0.5, 1.5, ((0, 2), (1, 8))),
        "ffn_in": bell_draw(key_list[9], (D, FF), D ** -0.5, 0.1875, ((0, 8), (1, 2))),
        "ffn_out": bell_draw(key_list[10], (FF, D), FF ** -0.5, 0.0625, ((0, 2), (1, 8))),
        "norm_gain": jnp.clip(1.0 + 0.15 * jax.random.normal(key_list[11], (3, D), jnp.float32), 0.25, 1.75).astype(jnp.bfloat16),
        "norm_bias": bell_draw(key_list[12], (3, D), 0.5, 3.0, ((1, 8),)),
    }


@jax.custom_vjp
def low(v):
    return lax.optimization_barrier(v.astype(jnp.bfloat16)).astype(jnp.float32)

@jax.custom_vjp
def low_back(v):
    return v

def low_keep(v):
    return (low(v), None)

def low_pass(kept, grad):
    return (grad,)

def back_keep(v):
    return (v, None)

def back_low(kept, grad):
    return (low(grad),)
low.defvjp(low_keep, low_pass)
low_back.defvjp(back_keep, back_low)
epsilon = 1e-05
masked_score = -1000000000.0
highest = lax.Precision.HIGHEST

def rounded(values):
    return low(low_back(values))

def product(left, right):
    return jnp.dot(left, right, precision=highest)

def layer_norm(values, gain, shift):
    centre = lax.optimization_barrier(jnp.mean(values, axis=-1, keepdims=True))
    centred = values - centre
    spread = lax.optimization_barrier(jnp.mean(centred * centred, axis=-1, keepdims=True))
    return centred * lax.rsqrt(spread + epsilon) * gain + shift

def attention(queries, key_rows, value_rows, allowed):
    query_count = queries.shape[0]
    key_count = key_rows.shape[0]
    query_heads = queries.reshape(query_count, HEADS, HEAD_DIM)
    key_heads = key_rows.reshape(key_count, HEADS, HEAD_DIM)
    value_heads = value_rows.reshape(key_count, HEADS, HEAD_DIM)
    scores = jnp.einsum('qhd,khd->hqk', query_heads, key_heads, precision=highest)
    scores = low_back(scores * HEAD_DIM ** (-0.5))
    scores = jnp.where(allowed[None], scores, masked_score)
    peak = lax.optimization_barrier(jnp.max(scores, axis=-1, keepdims=True))
    expo = jnp.exp(scores - peak)
    probs = low(expo / lax.optimization_barrier(jnp.sum(expo, axis=-1, keepdims=True)))
    mixed = jnp.einsum('hqk,khd->qhd', probs, value_heads, precision=highest)
    return rounded(mixed.reshape(query_count, HEADS * HEAD_DIM))

def gelu_tanh(values):
    return jax.nn.gelu(values, approximate=True)

def one_sequence(hidden, source, target_row, source_row, weights):
    self_w, self_o, cross_w, cross_o, up_w, down_w, gains, biases = weights
    length = hidden.shape[0]
    places = jnp.arange(length, dtype=jnp.int32)
    self_allowed = (target_row[:, None] == target_row[None, :]) & (places[None, :] <= places[:, None])
    cross_allowed = target_row[:, None] == source_row[None, :]
    normed = low(layer_norm(hidden, gains[0], biases[0]))
    queries = rounded(product(normed, self_w[0]))
    key_rows = rounded(product(normed, self_w[1]))
    value_rows = rounded(product(normed, self_w[2]))
    first = hidden + low_back(product(attention(queries, key_rows, value_rows, self_allowed), self_o))
    normed = low(layer_norm(first, gains[1], biases[1]))
    queries = rounded(product(normed, cross_w[0]))
    key_rows = rounded(product(source, cross_w[1]))
    value_rows = rounded(product(source, cross_w[2]))
    second = first + low_back(product(attention(queries, key_rows, value_rows, cross_allowed), cross_o))
    normed = low(layer_norm(second, gains[2], biases[2]))
    activated = low(gelu_tanh(low_back(product(normed, up_w))))
    return second + low_back(product(activated, down_w))

def reference(hidden_in, encoder_states, out_grad, target_ids, source_ids, self_in, self_out, cross_in, cross_out, ffn_in, ffn_out, norm_gain, norm_bias):
    seq_count = target_ids.shape[0]
    length = target_ids.shape[1]
    src_length = source_ids.shape[1]
    width = hidden_in.shape[1]
    weights = tuple((item.astype(jnp.float32) for item in (self_in, self_out, cross_in, cross_out, ffn_in, ffn_out, norm_gain, norm_bias)))
    hidden_seqs = hidden_in.astype(jnp.float32).reshape(seq_count, length, width)
    source_seqs = encoder_states.astype(jnp.float32).reshape(seq_count, src_length, width)
    block = jax.checkpoint(one_sequence)

    def forward(hidden_all, source_all, params):

        def step(carry, item):
            return (carry, block(item[0], item[1], item[2], item[3], params))
        unused, outputs = lax.scan(step, jnp.zeros((), jnp.float32), (hidden_all, source_all, target_ids, source_ids))
        return outputs
    outputs, pullback = jax.vjp(forward, hidden_seqs, source_seqs, weights)
    grad_hidden, grad_source, grads = pullback(out_grad.astype(jnp.float32).reshape(seq_count, length, width))
    return (outputs.reshape(seq_count * length, width).astype(jnp.bfloat16), grad_hidden.reshape(seq_count * length, width), grad_source.reshape(seq_count * src_length, width), grads[0], grads[1], grads[2], grads[3], grads[4], grads[5], grads[6], grads[7])
```

```python
import functools

import jax
import jax.numpy as jnp
import numpy as np
from jax import lax
from jax.experimental import pallas as pl
from jax.experimental.pallas import tpu as pltpu
from jax.sharding import PartitionSpec as P

HEAD_DIM = 64
SCALE = HEAD_DIM**-0.5
EPSILON = 1e-05
MASKED = -1000000000.0
RING_MOST = 8

f32 = jnp.float32
bf16 = jnp.bfloat16
hold = lax.optimization_barrier


def product(left, right):
    return jnp.dot(left, right, preferred_element_type=f32)


def left_product(left, right):
    return lax.dot_general(left, right, (((0,), (0,)), ((), ())), preferred_element_type=f32)


def right_product(left, right):
    return lax.dot_general(left, right, (((1,), (1,)), ((), ())), preferred_element_type=f32)


def norm_forward(values, gain, shift):
    centre = jnp.mean(values, axis=-1, keepdims=True)
    centred = values - centre
    factor = lax.rsqrt(jnp.mean(centred * centred, axis=-1, keepdims=True) + EPSILON)
    normal = centred * factor
    return normal * gain + shift, normal, factor


def norm_backward(grad_norm, normal, factor, gain):
    scaled = grad_norm * gain
    inner = (
        scaled
        - jnp.mean(scaled, axis=-1, keepdims=True)
        - normal * jnp.mean(scaled * normal, axis=-1, keepdims=True)
    )
    return factor * inner


def norm_sums(grad_norm, normal):
    return jnp.stack([jnp.sum(grad_norm * normal, axis=0), jnp.sum(grad_norm, axis=0)])


def split_heads(values):
    return values.reshape(values.shape[0], values.shape[1] // HEAD_DIM, HEAD_DIM)


def masked_scores(queries, keys, allowed):
    scores = jnp.einsum(
        "qhd,khd->hqk", split_heads(queries), split_heads(keys), preferred_element_type=f32
    )
    return jnp.where(allowed[None], scores * SCALE, MASKED)


def attend_forward(queries, keys, values, allowed):
    scores = masked_scores(queries, keys, allowed)
    peak = jnp.max(scores, axis=-1, keepdims=True)
    expo = jnp.exp(scores - peak)
    total = jnp.sum(expo, axis=-1, keepdims=True)
    probs = (expo / total).astype(bf16)
    mixed = jnp.einsum("hqk,khd->qhd", probs, split_heads(values), preferred_element_type=f32)
    return mixed.reshape(queries.shape).astype(bf16), peak + jnp.log(total)


def attend_backward(grad_mixed, queries, keys, values, allowed, log_total):
    scores = masked_scores(queries, keys, allowed)
    probs = jnp.exp(scores - log_total)
    grad_heads = split_heads(grad_mixed)
    grad_values = jnp.einsum(
        "hqk,qhd->khd", probs.astype(bf16), grad_heads, preferred_element_type=f32
    )
    grad_probs = jnp.einsum(
        "qhd,khd->hqk", grad_heads, split_heads(values), preferred_element_type=f32
    )
    grad_scores = probs * (grad_probs - jnp.sum(probs * grad_probs, axis=-1, keepdims=True))
    grad_scores = grad_scores.astype(bf16)
    grad_queries = jnp.einsum(
        "hqk,khd->qhd", grad_scores, split_heads(keys), preferred_element_type=f32
    )
    grad_keys = jnp.einsum(
        "hqk,qhd->khd", grad_scores, split_heads(queries), preferred_element_type=f32
    )
    return (
        (grad_queries * SCALE).reshape(queries.shape).astype(bf16),
        (grad_keys * SCALE).reshape(keys.shape).astype(bf16),
        grad_values.reshape(values.shape).astype(bf16),
    )


def gelu_tanh(values):
    return jax.nn.gelu(values, approximate=True)


def move_blocks(array, places):
    rows, columns = array.shape
    count = places.shape[0]
    width = columns // count

    def body(places_ref, in_ref, out_ref):
        out_ref[...] = in_ref[...]

    return pl.pallas_call(
        body,
        grid_spec=pltpu.PrefetchScalarGridSpec(
            num_scalar_prefetch=1,
            grid=(count,),
            in_specs=[pl.BlockSpec((rows, width), lambda k, places_ref: (0, places_ref[k]))],
            out_specs=pl.BlockSpec((rows, width), lambda k, places_ref: (0, k)),
        ),
        out_shape=jax.ShapeDtypeStruct(array.shape, array.dtype),
    )(places, array)


def swap(values, axis):
    return lax.ppermute(values, axis, [(0, 1), (1, 0)])


class Ring:
    def __init__(self, size):
        self.size = size
        self.short = size <= RING_MOST and size % 2 == 0
        half = size // 2
        if self.short:
            self.order = [2 * p if p < half else 2 * (size - 1 - p) + 1 for p in range(size)]
        else:
            self.order = list(range(size))
        position = np.zeros(size, np.int32)
        position[self.order] = np.arange(size)
        there = np.zeros((size, size), np.int32)
        back = np.zeros((size, size), np.int32)
        for device in range(size):
            for k in range(size):
                place = self.order[(position[device] + k) % size] if self.short else k
                there[device, k] = place
                back[device, place] = k
        self.there, self.back = there, back

    def places(self, table):
        return lax.dynamic_index_in_dim(jnp.asarray(table), lax.axis_index("dp"), 0, False)

    def into(self, array):
        return move_blocks(array, self.places(self.there)) if self.short else array

    def out_of(self, array):
        return move_blocks(array, self.places(self.back)) if self.short else array

    def send(self, values, step):
        size, order = self.size, self.order
        pairs = [(order[p], order[(p + step) % size]) for p in range(size)]
        return lax.ppermute(values, "dp", pairs)

    def gather(self, shard):
        if not self.short:
            return lax.all_gather(shard, "dp", axis=1, tiled=True)
        size = self.size
        cut = shard.shape[-1] // 2
        ahead = behind = shard
        from_ahead, from_behind = [], []
        for _ in range(size // 2 - 1):
            ahead = self.send(ahead, -1)
            behind = self.send(behind, 1)
            from_ahead.append(ahead)
            from_behind.append(behind)
        far = [self.send(ahead[..., :cut], -1), self.send(behind[..., cut:], 1)]
        middle = jnp.concatenate(far, -1)
        return jnp.concatenate([shard] + from_ahead + [middle] + from_behind[::-1], 1)

    def scatter(self, full):
        size = self.size
        if not self.short:
            return lax.psum_scatter(full.astype(bf16), "dp", scatter_dimension=1, tiled=True).astype(f32)
        rows = full.shape[1] // size
        half = size // 2
        blocks = [full[:, k * rows : (k + 1) * rows].astype(f32) for k in range(size)]
        cut = full.shape[-1] // 2
        ahead = self.send(blocks[half][..., :cut].astype(bf16), 1)
        behind = self.send(blocks[half][..., cut:].astype(bf16), -1)
        for k in range(half - 1, 0, -1):
            up, down = blocks[k], blocks[size - k]
            if k == half - 1:
                up = jnp.concatenate([up[..., :cut] + ahead.astype(f32), up[..., cut:]], -1)
                down = jnp.concatenate([down[..., :cut], down[..., cut:] + behind.astype(f32)], -1)
            else:
                up = up + ahead.astype(f32)
                down = down + behind.astype(f32)
            ahead = self.send(up.astype(bf16), 1)
            behind = self.send(down.astype(bf16), -1)
        return blocks[0] + (ahead.astype(f32) + behind.astype(f32))

    def scatter_few(self, full):
        size = self.size
        if not self.short:
            return lax.psum_scatter(full, "dp", scatter_dimension=1, tiled=True)
        width = full.shape[1] // size
        blocks = [full[:, k * width : (k + 1) * width] for k in range(size)]
        parts = [blocks[0]] + [self.send(blocks[k], k) for k in range(1, size)]
        return sum(parts[1:], parts[0])


def per_device(
    ring,
    hidden_in,
    encoder_states,
    out_grad,
    target_ids,
    source_ids,
    self_in,
    self_out,
    cross_in,
    cross_out,
    ffn_in,
    ffn_out,
    norm_gain,
    norm_bias,
):
    ctx = lax.axis_index("ctx")
    core = lax.axis_index("tp")
    rows = hidden_in.shape[0]
    source_rows = encoder_states.shape[0]

    def own_half(array, axis, place=ctx):
        half = array.shape[axis] // 2
        return lax.dynamic_slice_in_dim(array, place * half, half, axis)

    def both_rows(own):
        part = own_half(own, 0, core)
        got = swap(part, "ctx")
        rest = swap(got, "tp")
        low = jnp.where(core == 0, got, rest)
        high = jnp.where(core == 0, rest, got)
        return jnp.concatenate([own, low, high], 0)

    def turned(values):
        half = values.shape[0] // 2
        return jnp.concatenate([values[half:], values[:half]], 0)

    def core_sum(partial):
        part = hold(partial.astype(bf16))
        return part.astype(f32) + swap(part, "tp").astype(f32)

    def row_sum(partial):
        count = partial.shape[0] // 2
        low = hold(partial.astype(bf16))
        mine, theirs = low[:count], low[count:]
        keep = own_half(theirs, 0, core)
        give = own_half(theirs, 0, 1 - core)
        summed = (keep.astype(f32) + swap(give, "tp").astype(f32)).astype(bf16)
        got = swap(summed, "ctx")
        rest = swap(got, "tp")
        far = jnp.concatenate([jnp.where(core == 0, got, rest), jnp.where(core == 0, rest, got)], 0)
        near = mine.astype(f32) + swap(mine, "tp").astype(f32)
        return near + far.astype(f32)

    def both_columns(part):
        part = hold(part.astype(bf16))
        other = swap(part, "ctx")
        low = jnp.where(ctx == 0, part, other)
        high = jnp.where(ctx == 0, other, part)
        return jnp.concatenate([low, high], -1).astype(f32)

    first_shard = own_half(self_in, 2)
    cross_half = own_half(cross_in, 2)
    out_halves = jnp.stack([own_half(self_out, 0).T, own_half(cross_out, 0).T])
    key_shard = cross_half[1:]
    third_shard = jnp.concatenate([out_halves[:1], cross_half[:1], out_halves[1:]], 0)
    up_shard = own_half(ffn_in, 1)[None]
    down_shard = own_half(ffn_out, 0).T[None]

    vectors = jnp.concatenate([norm_gain, norm_bias], 0)
    vectors = lax.all_gather(vectors, "dp", axis=1, tiled=True).astype(f32)
    vectors = jnp.concatenate([vectors, jnp.zeros((2, vectors.shape[1]), f32)], 0)
    vectors = ring.into(vectors)
    gains, biases = vectors[0:3, None, :], vectors[3:6, None, :]

    hidden = both_rows(ring.into(hidden_in))
    first_w = ring.gather(first_shard)
    key_shard, first_w = hold((key_shard, first_w))
    third_shard, key_shard = hold((third_shard, key_shard))
    third_w = ring.gather(third_shard)
    key_w = ring.gather(key_shard)
    third_w = jnp.concatenate([third_w, swap(third_w, "ctx")], -1)
    up_shard, down_shard, third_w = hold((up_shard, down_shard, third_w))
    up_w = ring.gather(up_shard)[0]
    down_w = ring.gather(down_shard)[0]
    source = both_rows(ring.into(encoder_states))
    out_cot = both_rows(ring.into(out_grad))

    def both_order(vector):
        half = vector.shape[0] // 2
        return jnp.concatenate(
            [
                lax.dynamic_slice_in_dim(vector, ctx * half, half),
                lax.dynamic_slice_in_dim(vector, (1 - ctx) * half, half),
            ]
        )

    target_row = both_order(target_ids[0])
    source_row = both_order(source_ids[0])
    place = both_order(jnp.arange(2 * rows, dtype=jnp.int32))
    self_allowed = (target_row[:, None] == target_row[None, :]) & (place[None, :] <= place[:, None])
    cross_allowed = target_row[:rows, None] == source_row[None, :]

    start_rows = hidden.astype(f32)
    normed, normal_one, factor_one = norm_forward(start_rows, gains[0], biases[0])
    input_one = normed.astype(bf16)
    queries = product(input_one, first_w[0]).astype(bf16)
    keys = product(input_one, first_w[1]).astype(bf16)
    values = product(input_one, first_w[2]).astype(bf16)
    mixed, total_one = attend_forward(queries, keys, values, self_allowed)
    mixed_one = jnp.concatenate([mixed[:rows], swap(mixed[rows:], "ctx")], 1)
    self_o, cross_q, cross_o = third_w[0], third_w[1], third_w[2]
    first_rows = start_rows[:rows] + core_sum(right_product(mixed_one, self_o))

    key_cross = product(source, key_w[0]).astype(bf16)
    value_cross = product(source, key_w[1]).astype(bf16)
    pair = jnp.concatenate([key_cross, value_cross], 1)
    other = swap(turned(pair), "ctx")
    width = key_cross.shape[1]
    key_cross = jnp.concatenate([key_cross, other[:, :width]], 1)
    value_cross = jnp.concatenate([value_cross, other[:, width:]], 1)
    normed, normal_two, factor_two = norm_forward(first_rows, gains[1], biases[1])
    input_two = normed.astype(bf16)
    cross_queries = product(input_two, cross_q).astype(bf16)
    mixed_two, total_two = attend_forward(cross_queries, key_cross, value_cross, cross_allowed)
    second_rows = first_rows + core_sum(right_product(mixed_two, cross_o))

    normed, normal_three, factor_three = norm_forward(second_rows, gains[2], biases[2])
    input_three = both_rows(normed.astype(bf16))
    activated, gelu_pull = jax.vjp(gelu_tanh, product(input_three, up_w))
    activated = activated.astype(bf16)
    grad_up = gelu_pull(product(out_cot, down_w))[0].astype(bf16)
    grad_norm = row_sum(right_product(grad_up, up_w))
    result = (second_rows + row_sum(right_product(activated, down_w))).astype(bf16)
    grad_up_w = left_product(input_three, grad_up)
    grad_down_w = left_product(out_cot, activated)
    up_sum = ring.scatter(grad_up_w[None])
    down_sum = ring.scatter(grad_down_w[None])

    grad_rows = out_cot[:rows].astype(f32)
    sums_three = norm_sums(grad_norm, normal_three)
    grad_second = grad_rows + norm_backward(grad_norm, normal_three, factor_three, gains[2])

    grad_branch = grad_second.astype(bf16)
    grad_cross_o = left_product(grad_branch, mixed_two)
    grad_mixed = product(grad_branch, cross_o).astype(bf16)
    grad_cq, grad_ck, grad_cv = attend_backward(
        grad_mixed, cross_queries, key_cross, value_cross, cross_allowed, total_two
    )
    grad_norm = core_sum(right_product(grad_cq, cross_q))
    grad_cross_q = left_product(input_two, grad_cq)
    given = swap(turned(jnp.concatenate([grad_ck[:, width:], grad_cv[:, width:]], 1)), "ctx")
    grad_ck = (grad_ck[:, :width].astype(f32) + given[:, :width].astype(f32)).astype(bf16)
    grad_cv = (grad_cv[:, :width].astype(f32) + given[:, width:].astype(f32)).astype(bf16)
    grad_key_w = jnp.stack([left_product(source, grad_ck), left_product(source, grad_cv)])
    grad_source = row_sum(right_product(grad_ck, key_w[0]) + right_product(grad_cv, key_w[1]))

    sums_two = norm_sums(grad_norm, normal_two)
    grad_first = grad_second + norm_backward(grad_norm, normal_two, factor_two, gains[1])

    grad_branch = grad_first.astype(bf16)
    grad_self_o = left_product(grad_branch, mixed_one)
    grad_mixed = product(grad_branch, self_o).astype(bf16)
    head_width = mixed.shape[1]
    grad_mixed = jnp.concatenate(
        [grad_mixed[:, :head_width], swap(grad_mixed[:, head_width:], "ctx")], 0
    )
    grad_q, grad_k, grad_v = attend_backward(
        grad_mixed, queries, keys, values, self_allowed, total_one
    )
    grad_first_w = jnp.stack(
        [left_product(input_one, grad_q), left_product(input_one, grad_k), left_product(input_one, grad_v)]
    )
    first_sum = ring.scatter(grad_first_w)
    partial = (
        right_product(grad_q, first_w[0])
        + right_product(grad_k, first_w[1])
        + right_product(grad_v, first_w[2])
    )
    sums_one = norm_sums(partial, normal_one)
    grad_norm = row_sum(partial)
    grad_input = grad_first + norm_backward(
        grad_norm, normal_one[:rows], factor_one[:rows], gains[0]
    )

    third = jnp.stack([grad_self_o, grad_cross_q, grad_cross_o])
    cut = third.shape[2] // 2
    third = third[..., :cut] + swap(third[..., cut:].astype(bf16), "ctx").astype(f32)
    third_sum = ring.scatter(third)
    key_sum = ring.scatter(grad_key_w)

    sums_one = sums_one + swap(sums_one, "tp")
    sums = jnp.concatenate([sums_one, sums_two, sums_three, jnp.zeros_like(sums_one)], 0)
    sums = ring.scatter_few(sums + swap(sums, "ctx"))
    grad_gains = jnp.stack([sums[0], sums[2], sums[4]])
    grad_biases = jnp.stack([sums[1], sums[3], sums[5]])

    first_out = both_columns(first_sum)
    third_out = both_columns(third_sum)
    key_out = both_columns(key_sum)
    return (
        ring.out_of(result),
        ring.out_of(grad_input),
        ring.out_of(grad_source),
        first_out,
        third_out[0].T,
        jnp.concatenate([third_out[1:2], key_out], 0),
        third_out[2].T,
        both_columns(up_sum)[0],
        both_columns(down_sum)[0].T,
        grad_gains,
        grad_biases,
    )


def solution(mesh):
    return jax.shard_map(
        functools.partial(per_device, Ring(mesh.shape["dp"])),
        mesh=mesh,
        in_specs=(
            P(("dp", "ctx"), None),
            P(("dp", "ctx"), None),
            P(("dp", "ctx"), None),
            P("dp", None),
            P("dp", None),
            P(None, "dp", "tp"),
            P("tp", "dp"),
            P(None, "dp", "tp"),
            P("tp", "dp"),
            P("dp", "tp"),
            P("tp", "dp"),
            P(None, "dp"),
            P(None, "dp"),
        ),
        out_specs=(
            P(("dp", "ctx"), None),
            P(("dp", "ctx"), None),
            P(("dp", "ctx"), None),
            P(None, "dp", "tp"),
            P("tp", "dp"),
            P(None, "dp", "tp"),
            P("tp", "dp"),
            P("dp", "tp"),
            P("tp", "dp"),
            P(None, "dp"),
            P(None, "dp"),
        ),
        check_vma=False,
    )
```

```python
import functools

import jax
import jax.numpy as jnp
import numpy as np
from jax import lax
from jax.experimental import pallas as pl
from jax.experimental.pallas import tpu as pltpu
from jax.sharding import PartitionSpec as P

HEAD_DIM = 64
EPSILON = 1e-05
RING_MOST = 8
SCORE_SCALE = HEAD_DIM**-0.5 * 1.4426950408889634
MASKED = -1e30
TILE = 256
QUAD = 256
FFN_ROWS = 512
FFN_CHUNKS = 2
VMEM = 52 << 20

f32 = jnp.float32
bf16 = jnp.bfloat16
hold = lax.optimization_barrier


def nn(left, right):
    return jnp.dot(left, right, preferred_element_type=f32)


def tn(left, right):
    return lax.dot_general(left, right, (((0,), (0,)), ((), ())), preferred_element_type=f32)


def nt(left, right):
    return lax.dot_general(left, right, (((1,), (1,)), ((), ())), preferred_element_type=f32)


def cost(flops):
    return pl.CostEstimate(flops=int(flops), bytes_accessed=0, transcendentals=0)


def only_head(values, head):
    lane = lax.broadcasted_iota(jnp.int32, values.shape, 1) // HEAD_DIM
    return jnp.where(lane == head, values, jnp.zeros_like(values))


def attend_forward_kernel(
    need, q_ref, k_ref, v_ref, qid_ref, qat_ref, kid_ref, kat_ref, o_ref, lse_ref, s_ref, vt_ref
):
    step = pl.program_id(0)
    width = q_ref.shape[1]
    tiles = k_ref.shape[0] // TILE
    heads = width // HEAD_DIM
    per = QUAD // HEAD_DIM

    @pl.when(step == 0)
    def _():
        for t in range(tiles):
            vt_ref[:, t * TILE : (t + 1) * TILE] = v_ref[t * TILE : (t + 1) * TILE, :].T

    s_ref[...] = jnp.full_like(s_ref, MASKED)
    for t in range(tiles):

        @pl.when(need[step * tiles + t] != 0)
        def _():
            span = slice(t * TILE, (t + 1) * TILE)
            allowed = (kid_ref[span, :] == qid_ref[...]) & (kat_ref[span, :] <= qat_ref[...])
            for h in range(heads):
                lanes = slice(h // per * QUAD, (h // per + 1) * QUAD)
                scores = nt(k_ref[span, lanes], only_head(q_ref[:, lanes], h % per)) * SCORE_SCALE
                s_ref[h, span, :] = jnp.where(allowed, scores, MASKED)

    for h in range(heads):
        scores = s_ref[h]
        peak = jnp.max(scores, axis=0, keepdims=True)
        expo = jnp.exp2(scores - peak)
        total = jnp.sum(expo, axis=0, keepdims=True)
        lse_ref[h : h + 1, :] = peak + jnp.log2(total)
        out = nn(vt_ref[h * HEAD_DIM : (h + 1) * HEAD_DIM, :], expo.astype(bf16))
        s_ref[h, 0:HEAD_DIM, :] = out * (1.0 / total)
    for g in range(heads // per):
        out = jnp.concatenate([s_ref[g * per + i, 0:HEAD_DIM, :] for i in range(per)], 0)
        o_ref[:, g * QUAD : (g + 1) * QUAD] = out.T.astype(bf16)


def attend_forward(q, k, v, seen, width):
    query_id, query_at, key_id, key_at, need = seen
    rows, keys, heads = q[0].shape[0], k[0].shape[0], width // HEAD_DIM
    col = lambda i, need: (0, i)
    return pl.pallas_call(
        attend_forward_kernel,
        grid_spec=pltpu.PrefetchScalarGridSpec(
            num_scalar_prefetch=1,
            grid=(rows // TILE,),
            in_specs=[
                pl.BlockSpec((TILE, width), lambda i, need: (i, q[1])),
                pl.BlockSpec((keys, width), lambda i, need: (0, k[1])),
                pl.BlockSpec((keys, width), lambda i, need: (0, v[1])),
                pl.BlockSpec((1, TILE), col),
                pl.BlockSpec((1, TILE), col),
                pl.BlockSpec((keys, 1), lambda i, need: (0, 0)),
                pl.BlockSpec((keys, 1), lambda i, need: (0, 0)),
            ],
            out_specs=[
                pl.BlockSpec((TILE, width), lambda i, need: (i, 0)),
                pl.BlockSpec((heads, TILE), col),
            ],
            scratch_shapes=[
                pltpu.VMEM((heads, keys, TILE), f32),
                pltpu.VMEM((width, keys), bf16),
            ],
        ),
        out_shape=[
            jax.ShapeDtypeStruct((rows, width), bf16),
            jax.ShapeDtypeStruct((heads, rows), f32),
        ],
        compiler_params=pltpu.CompilerParams(vmem_limit_bytes=VMEM),
        cost_estimate=cost(1e8),
        name="attend_forward",
    )(need, q[0], k[0], v[0], query_id, query_at, key_id, key_at)


def attend_backward_kernel(
    need,
    q_ref,
    k_ref,
    v_ref,
    o_ref,
    g_ref,
    lse_ref,
    qid_ref,
    qat_ref,
    kid_ref,
    kat_ref,
    gq_ref,
    gk_ref,
    gv_ref,
    gk_acc,
    gv_acc,
    gq_acc,
):
    step = pl.program_id(0)
    width = q_ref.shape[1]
    tiles = k_ref.shape[0] // TILE
    per = QUAD // HEAD_DIM

    @pl.when(step == 0)
    def _():
        gk_acc[...] = jnp.zeros_like(gk_acc)
        gv_acc[...] = jnp.zeros_like(gv_acc)

    gq_acc[...] = jnp.zeros_like(gq_acc)
    both = g_ref[...].astype(f32) * o_ref[...].astype(f32)
    heads = lse_ref.shape[0]
    pick = lax.broadcasted_iota(jnp.int32, (heads, width), 0) == (
        lax.broadcasted_iota(jnp.int32, (heads, width), 1) // HEAD_DIM
    )
    inner = lax.dot_general(
        pick.astype(f32),
        both,
        (((1,), (1,)), ((), ())),
        precision=lax.Precision.HIGHEST,
        preferred_element_type=f32,
    )
    for t in range(tiles):

        @pl.when(need[step * tiles + t] != 0)
        def _():
            span = slice(t * TILE, (t + 1) * TILE)
            allowed = (kid_ref[span, :] == qid_ref[...]) & (kat_ref[span, :] <= qat_ref[...])
            for g in range(width // QUAD):
                lanes = slice(g * QUAD, (g + 1) * QUAD)
                kq, vq, qq, gg = k_ref[span, lanes], v_ref[span, lanes], q_ref[:, lanes], g_ref[:, lanes]
                gk, gv, gq = gk_acc[span, lanes], gv_acc[span, lanes], gq_acc[:, lanes]
                for i in range(per):
                    h = g * per + i
                    qh, gh = only_head(qq, i), only_head(gg, i)
                    scores = jnp.where(allowed, nt(kq, qh) * SCORE_SCALE, MASKED)
                    probs = jnp.exp2(scores - lse_ref[h : h + 1, :])
                    grad = (probs * (nt(vq, gh) - inner[h : h + 1, :])).astype(bf16)
                    gv = gv + nn(probs.astype(bf16), gh)
                    gk = gk + nn(grad, qh)
                    gq = gq + tn(grad, only_head(kq, i))
                gk_acc[span, lanes] = gk
                gv_acc[span, lanes] = gv
                gq_acc[:, lanes] = gq

    gq_ref[...] = (gq_acc[...] * HEAD_DIM**-0.5).astype(bf16)

    @pl.when(step == pl.num_programs(0) - 1)
    def _():
        gk_ref[...] = (gk_acc[...] * HEAD_DIM**-0.5).astype(bf16)
        gv_ref[...] = gv_acc[...].astype(bf16)


def attend_backward(g, q, k, v, o, lse, seen, width):
    query_id, query_at, key_id, key_at, need = seen
    rows, keys, heads = q[0].shape[0], k[0].shape[0], width // HEAD_DIM
    row = lambda i, need: (i, 0)
    col = lambda i, need: (0, i)
    full = lambda i, need: (0, 0)
    return pl.pallas_call(
        attend_backward_kernel,
        grid_spec=pltpu.PrefetchScalarGridSpec(
            num_scalar_prefetch=1,
            grid=(rows // TILE,),
            in_specs=[
                pl.BlockSpec((TILE, width), lambda i, need: (i, q[1])),
                pl.BlockSpec((keys, width), lambda i, need: (0, k[1])),
                pl.BlockSpec((keys, width), lambda i, need: (0, v[1])),
                pl.BlockSpec((TILE, width), row),
                pl.BlockSpec((TILE, width), row),
                pl.BlockSpec((heads, TILE), col),
                pl.BlockSpec((1, TILE), col),
                pl.BlockSpec((1, TILE), col),
                pl.BlockSpec((keys, 1), full),
                pl.BlockSpec((keys, 1), full),
            ],
            out_specs=[
                pl.BlockSpec((TILE, width), row),
                pl.BlockSpec((keys, width), full),
                pl.BlockSpec((keys, width), full),
            ],
            scratch_shapes=[
                pltpu.VMEM((keys, width), f32),
                pltpu.VMEM((keys, width), f32),
                pltpu.VMEM((TILE, width), f32),
            ],
        ),
        out_shape=[
            jax.ShapeDtypeStruct((rows, width), bf16),
            jax.ShapeDtypeStruct((keys, width), bf16),
            jax.ShapeDtypeStruct((keys, width), bf16),
        ],
        compiler_params=pltpu.CompilerParams(vmem_limit_bytes=VMEM),
        cost_estimate=cost(1e8),
        name="attend_backward",
    )(need, q[0], k[0], v[0], o, g, lse, query_id, query_at, key_id, key_at)


def seen_by(query_id, query_at, key_id, key_at):
    qi, qa, ki, ka = (item.reshape(-1, TILE) for item in (query_id, query_at, key_id, key_at))
    need = (qi[:, None, 0] <= ki[None, :, -1]) & (ki[None, :, 0] <= qi[:, None, -1])
    need &= ka[None, :, 0] <= qa[:, None, -1]
    return (
        query_id[None, :],
        query_at[None, :],
        key_id[:, None],
        key_at[:, None],
        need.astype(jnp.int32).reshape(-1),
    )


def gelu_pair(u):
    c = 0.7978845608028654
    square = u * u
    t = jnp.tanh(u * (c + (c * 0.044715) * square))
    half = 0.5 + 0.5 * t
    slope = half + 0.5 * u * (1.0 - t * t) * (c + (3 * c * 0.044715) * square)
    return u * half, slope


def start_pieces(places, refs, scratch, sems):
    copies = []
    for n, ((row, col), ref) in enumerate(zip(places, refs)):
        _, r, c = ref.shape
        copies.append(
            pltpu.make_async_copy(ref, scratch.at[:, pl.ds(row, r), pl.ds(col, c)], sems.at[n])
        )
        copies[-1].start()
    return copies


def copy_pieces(places, refs, scratch, sems):
    for copy in start_pieces(places, refs, scratch, sems):
        copy.wait()


def ffn_first_kernel(places, add, *refs):
    if add:
        a_ref, g_ref, before, *refs = refs
    else:
        a_ref, g_ref, *refs = refs
    pieces, (act_ref, gu_ref, gn_ref, w, sems) = refs[: len(places)], refs[len(places) :]

    @pl.when(pl.program_id(0) == 0)
    def _():
        copy_pieces(places, pieces, w, sems)

    a, g = a_ref[...], g_ref[...]
    total = before[...] if add else jnp.zeros(gn_ref.shape, f32)
    for j in range(act_ref.shape[1] // TILE):
        span = slice(j * TILE, (j + 1) * TILE)
        act, slope = gelu_pair(nn(a, w[0, :, span]))
        act_ref[:, span] = act.astype(bf16)
        gu = (nn(g, w[1, :, span]) * slope).astype(bf16)
        gu_ref[:, span] = gu
        total = total + nt(gu, w[0, :, span])
    gn_ref[...] = total.astype(gn_ref.dtype)


def ffn_first(a, g, shards, cols, before=None):
    places, arrays = shards
    rows, width = a.shape
    row = lambda i: (i, 0)
    wide = pl.BlockSpec((FFN_ROWS, width), row)
    narrow = pl.BlockSpec((FFN_ROWS, cols), row)
    ins = [a, g] + ([] if before is None else [before])
    return pl.pallas_call(
        functools.partial(ffn_first_kernel, places, before is not None),
        grid=(rows // FFN_ROWS,),
        in_specs=[wide] * len(ins) + [pl.BlockSpec(memory_space=pl.ANY)] * len(arrays),
        out_specs=[narrow, narrow, wide],
        out_shape=[
            jax.ShapeDtypeStruct((rows, cols), bf16),
            jax.ShapeDtypeStruct((rows, cols), bf16),
            jax.ShapeDtypeStruct((rows, width), f32 if before is None else bf16),
        ],
        scratch_shapes=[
            pltpu.VMEM((2, width, cols), bf16),
            pltpu.SemaphoreType.DMA((len(arrays),)),
        ],
        compiler_params=pltpu.CompilerParams(vmem_limit_bytes=VMEM),
        cost_estimate=cost(1e8),
        name="ffn_first",
    )(*ins, *arrays)


def ffn_second_kernel(places, add, *refs):
    a_ref, g_ref, act_ref, gu_ref, *refs = refs
    if add:
        before, *refs = refs
    pieces, (dw_ref, out_ref, w, sems) = refs[: len(places)], refs[len(places) :]
    step = pl.program_id(0)

    @pl.when(step == 0)
    def _():
        copy_pieces(places, [ref.at[1:2] for ref in pieces], w, sems)

    dw_ref[0] = nn(a_ref[...].T, gu_ref[...]).astype(bf16)
    dw_ref[1] = nn(g_ref[...].T, act_ref[...]).astype(bf16)
    tile = out_ref.shape[0]
    out = nt(act_ref[pl.ds(pl.multiple_of(step * tile, tile), tile), :], w[0])
    if add:
        out = out + before[...]
    out_ref[...] = out.astype(out_ref.dtype)


def ffn_second(a, g, act, gu, shards, before=None):
    places, arrays = shards
    rows, width = a.shape
    cols = act.shape[1]
    steps = 4
    row = lambda i: (i, 0)
    full = pl.BlockSpec((rows, cols), lambda i: (0, 0))
    wide = pl.BlockSpec((rows, width // steps), lambda i: (0, i))
    out_wide = pl.BlockSpec((rows // steps, width), row)
    more = [] if before is None else [before]
    return pl.pallas_call(
        functools.partial(ffn_second_kernel, places, before is not None),
        grid=(steps,),
        in_specs=[wide, wide, full, full]
        + [out_wide] * len(more)
        + [pl.BlockSpec(memory_space=pl.ANY)] * len(arrays),
        out_specs=[pl.BlockSpec((2, width // steps, cols), lambda i: (0, i, 0)), out_wide],
        out_shape=[
            jax.ShapeDtypeStruct((2, width, cols), bf16),
            jax.ShapeDtypeStruct((rows, width), f32 if before is None else bf16),
        ],
        scratch_shapes=[
            pltpu.VMEM((1, width, cols), bf16),
            pltpu.SemaphoreType.DMA((len(arrays),)),
        ],
        compiler_params=pltpu.CompilerParams(vmem_limit_bytes=VMEM),
        cost_estimate=cost(1e8),
        name="ffn_second",
    )(a, g, act, gu, *more, *arrays)


def normalized(values):
    centre = jnp.mean(values, axis=-1, keepdims=True)
    centred = values - centre
    factor = lax.rsqrt(jnp.mean(centred * centred, axis=-1, keepdims=True) + EPSILON)
    return centred * factor, factor


def norm_backward(grad_norm, normal, factor, gain):
    scaled = grad_norm * gain
    inner = (
        scaled
        - jnp.mean(scaled, axis=-1, keepdims=True)
        - normal * jnp.mean(scaled * normal, axis=-1, keepdims=True)
    )
    return factor * inner


def kernel_call(body, ins, outs, scalars=None, scratch=(), name=None, spaces=None):
    spaces = spaces or {}
    specs = [pl.BlockSpec(memory_space=spaces.get(n, pltpu.VMEM)) for n in range(len(ins))]
    out_specs = [pl.BlockSpec(memory_space=spaces.get(("out", n), pltpu.VMEM)) for n in range(len(outs))]
    if scalars is not None:
        specs = [pl.BlockSpec(memory_space=pltpu.SMEM)] + specs
        ins = [scalars] + list(ins)
    return pl.pallas_call(
        body,
        in_specs=specs,
        out_specs=out_specs,
        out_shape=[jax.ShapeDtypeStruct(*out) for out in outs],
        scratch_shapes=list(scratch),
        compiler_params=pltpu.CompilerParams(vmem_limit_bytes=VMEM),
        cost_estimate=cost(1e8),
        name=name,
    )(*ins)


def tiles_of(rows, most=256):
    tile = min(rows, most)
    return [slice(n, n + tile) for n in range(0, rows, tile)]


def first_project(scalars, own, got, rest, shards, columns):
    places, pieces = shards
    rows, width = own.shape
    total = pieces[0].shape[2]

    def body(scalars_ref, own_ref, got_ref, rest_ref, *refs):
        pieces, (qkv_ref, low_ref, normal_ref, vectors_ref, w, sems) = refs[: len(places)], refs[len(places) :]
        core = scalars_ref[1]
        copies = start_pieces(places, pieces, w, sems)
        sources = [(own_ref, part, part) for part in tiles_of(rows)]
        half = rows // 2
        for ref, far in ((got_ref, core), (rest_ref, 1 - core)):
            for part in tiles_of(half):
                at = pl.multiple_of(rows + far * half + part.start, 128)
                sources.append((ref, part, pl.ds(at, part.stop - part.start)))
        for ref, part, at in sources:
            normal_ref[at, :] = normalized(ref[part, :].astype(f32))[0].astype(bf16)
        for copy in copies:
            copy.wait()
        vectors_ref[...] = w[0, :, columns:].astype(f32).T[:8]
        gain, bias = vectors_ref[0:1, :], vectors_ref[3:4, :]
        for ref, part, at in sources:
            normal = normalized(ref[part, :].astype(f32))[0]
            low = (normal * gain + bias).astype(bf16)
            low_ref[at, :] = low
            qkv_ref[at, :] = nn(low, w[0, :, :columns]).astype(bf16)

    outs = [
        ((2 * rows, columns), bf16),
        ((2 * rows, width), bf16),
        ((2 * rows, width), bf16),
        ((8, width), f32),
    ]
    scratch = [pltpu.VMEM((1, width, total), bf16), pltpu.SemaphoreType.DMA((len(places),))]
    spaces = {3 + n: pl.ANY for n in range(len(places))}
    return kernel_call(body, [own, got, rest, *pieces], outs, scalars, scratch, "first_project", spaces)


def join_pieces(shards, widths):
    places, pieces = shards
    depth = max(row + piece.shape[1] for (row, _), piece in zip(places, pieces))
    starts = np.cumsum([0] + widths)

    def plan():
        for (row, col), n in zip(places, range(len(pieces))):
            _, r, c = pieces[n].shape
            for o, (start, wide) in enumerate(zip(starts, widths)):
                low, high = max(col, start), min(col + c, start + wide)
                if low < high:
                    yield n, o, row, r, low - col, low - start, high - low

    moves = list(plan())

    def body(*refs):
        ins, outs, sems = refs[: len(pieces)], refs[len(pieces) : -1], refs[-1]
        copies = []
        for m, (n, o, row, r, source, target, wide) in enumerate(moves):
            copies.append(
                pltpu.make_async_copy(
                    ins[n].at[0, :, pl.ds(source, wide)],
                    outs[o].at[pl.ds(row, r), pl.ds(target, wide)],
                    sems.at[m],
                )
            )
            copies[-1].start()
        for copy in copies:
            copy.wait()

    spaces = {n: pl.ANY for n in range(len(pieces))}
    outs = [((int(depth), wide), bf16) for wide in widths]
    scratch = [pltpu.SemaphoreType.DMA((len(moves),))]
    return kernel_call(body, pieces, outs, None, scratch, "join_pieces", spaces)


def branch_norm(before, branch, got, vectors, which, weights=None):
    rows, width = before.shape

    def body(before_ref, branch_ref, got_ref, vectors_ref, *refs):
        if weights is None:
            out_ref, low_ref = refs
        else:
            w_ref, out_ref, low_ref, product_ref = refs
        gain, bias = vectors_ref[which : which + 1, :], vectors_ref[3 + which : 4 + which, :]
        for part in tiles_of(rows, 128):
            out = before_ref[part, :].astype(f32) + (
                branch_ref[part, :].astype(f32) + got_ref[part, :].astype(f32)
            )
            out_ref[part, :] = out
            low_ref[part, :] = (normalized(out)[0] * gain + bias).astype(bf16)
        if weights is not None:
            product_ref[...] = nn(low_ref[...], w_ref[...]).astype(bf16)

    outs = [((rows, width), f32), ((rows, width), bf16)]
    ins = [before, branch, got, vectors]
    if weights is not None:
        ins.append(weights)
        outs.append(((rows, weights.shape[1]), bf16))
    return kernel_call(body, ins, outs, name="branch_norm")


def norm_back(scalars, first, second, split, above, values, vectors, which, weights):
    rows, width = values.shape

    def body(scalars_ref, first_ref, second_ref, above_ref, values_ref, vectors_ref, w_ref, *outs):
        product_ref, low_ref, out_ref, sums_ref = outs
        gain = vectors_ref[which : which + 1, :]
        core = scalars_ref[1]
        totals = [jnp.zeros((8, width), f32)] * 2
        half = rows // 2

        def tile(grad, at, size):
            normal, factor = normalized(values_ref[at, :].astype(f32))
            out = above_ref[at, :].astype(f32) + norm_backward(grad, normal, factor, gain)
            out_ref[at, :] = out
            low_ref[at, :] = out.astype(bf16)
            eight = lambda item: jnp.sum(item.reshape(size // 8, 8, width), axis=0)
            totals[0] = totals[0] + eight(grad * normal)
            totals[1] = totals[1] + eight(grad)

        if split:
            for ref, far in ((first_ref, core), (second_ref, 1 - core)):
                for part in tiles_of(half, 128):
                    size = part.stop - part.start
                    at = pl.ds(pl.multiple_of(far * half + part.start, 128), size)
                    tile(ref[part, :].astype(f32), at, size)
        else:
            for part in tiles_of(rows, 128):
                grad = first_ref[part, :].astype(f32) + second_ref[part, :].astype(f32)
                tile(grad, part, part.stop - part.start)
        sums_ref[0:1, :] = jnp.sum(totals[0], axis=0, keepdims=True)
        sums_ref[1:2, :] = jnp.sum(totals[1], axis=0, keepdims=True)
        product_ref[...] = nn(low_ref[...], w_ref[...]).astype(bf16)

    outs = [
        ((rows, weights.shape[1]), bf16),
        ((rows, width), bf16),
        ((rows, width), f32),
        ((2, width), f32),
    ]
    ins = [first, second, above, values, vectors, weights]
    return kernel_call(body, ins, outs, scalars, name="norm_back")


def last_norm_back(scalars, first, second, above, values, vectors, places):
    rows, width = values.shape
    count = places.shape[0]
    block = width // count

    def body(scalars_ref, first_ref, second_ref, above_ref, values_ref, vectors_ref, places_ref, out_ref):
        core = scalars_ref[1]
        half = rows // 2
        for ref, far in ((first_ref, core), (second_ref, 1 - core)):
            for part in tiles_of(half, 128):
                size = part.stop - part.start
                at = pl.ds(pl.multiple_of(far * half + part.start, 128), size)
                normal, factor = normalized(values_ref[at, :].astype(f32))
                grad = norm_backward(ref[part, :].astype(f32), normal, factor, vectors_ref[0:1, :])
                out = above_ref[at, :] + grad
                if block % 128:
                    out_ref[at, :] = out
                else:
                    for k in range(count):
                        to = pl.ds(pl.multiple_of(places_ref[k] * block, 128), block)
                        out_ref[at, to] = out[:, k * block : (k + 1) * block]

    ins = [first, second, above, values, vectors, places]
    outs = [((rows, width), f32)]
    return kernel_call(body, ins, outs, scalars, name="last_norm_back", spaces={5: pltpu.SMEM})[0]


def first_partial(grad_parts, weights, normal):
    gq, gk, gv = grad_parts
    rows, cols = gq.shape
    width = normal.shape[1]
    tile = 256

    def body(gq_ref, gk_ref, gv_ref, w_ref, normal_ref, out_ref, qkv_ref, sums_ref):
        both = jnp.concatenate([gq_ref[...], gk_ref[...], gv_ref[...]], 1)
        qkv_ref[...] = both
        grad = nt(both, w_ref[...])
        out_ref[...] = grad.astype(bf16)
        sums = [jnp.sum(grad * normal_ref[...].astype(f32), 0, keepdims=True), jnp.sum(grad, 0, keepdims=True)]
        step = pl.program_id(0)
        for n, item in enumerate(sums):
            sums_ref[n : n + 1, :] = jnp.where(step == 0, item, sums_ref[n : n + 1, :] + item)

    row = lambda i: (i, 0)
    full = lambda i: (0, 0)
    narrow = pl.BlockSpec((tile, cols), row)
    wide = pl.BlockSpec((tile, width), row)
    return pl.pallas_call(
        body,
        grid=(rows // tile,),
        in_specs=[narrow, narrow, narrow, pl.BlockSpec((width, 3 * cols), full), wide],
        out_specs=[wide, pl.BlockSpec((tile, 3 * cols), row), pl.BlockSpec((2, width), full)],
        out_shape=[
            jax.ShapeDtypeStruct((rows, width), bf16),
            jax.ShapeDtypeStruct((rows, 3 * cols), bf16),
            jax.ShapeDtypeStruct((2, width), f32),
        ],
        compiler_params=pltpu.CompilerParams(vmem_limit_bytes=VMEM),
        cost_estimate=cost(1e8),
        name="first_partial",
    )(gq, gk, gv, weights, normal)


def first_shards(scalars, self_in, gain, bias):
    count, rows, columns = self_in.shape
    half = columns // 2

    def body(scalars_ref, w_ref, gain_ref, bias_ref, out_ref, table):
        at = pl.ds(pl.multiple_of(scalars_ref[0] * half, 128), half)
        for n in range(count):
            out_ref[0, :, n * half : (n + 1) * half] = w_ref[n, :, at]
        table[...] = jnp.zeros_like(table)
        table[0:3, 0:rows] = gain_ref[...].astype(f32)
        table[3:6, 0:rows] = bias_ref[...].astype(f32)
        out_ref[0, :, count * half :] = table[...].T[0:rows].astype(bf16)

    outs = [((1, rows, count * half + 128), bf16)]
    scratch = [pltpu.VMEM((128, 128), f32)]
    return kernel_call(body, [self_in, gain, bias], outs, scalars, scratch, "first_shards")[0]


def other_shards(scalars, self_out, cross_in, cross_out, ffn_in, ffn_out, chunks):
    _, rows, columns = cross_in.shape
    half = columns // 2
    units = ffn_in.shape[1] // 2 // chunks

    def body(scalars_ref, so_ref, cross_ref, co_ref, in_ref, out_ref, second_ref, *ffn_refs):
        ctx = scalars_ref[0]
        mine = pl.multiple_of(ctx * half, 128)
        theirs = pl.multiple_of((1 - ctx) * half, 128)
        place = 0
        for n in (1, 2):
            second_ref[0, :, place : place + half] = cross_ref[n, :, pl.ds(mine, half)]
            place += half
        for ref in (so_ref, None, co_ref):
            for at in (mine, theirs):
                if ref is None:
                    item = cross_ref[0, :, pl.ds(at, half)]
                else:
                    item = ref[pl.ds(at, half), :].T
                second_ref[0, :, place : place + half] = item
                place += half
        for n in range(chunks):
            at = pl.ds(pl.multiple_of(ctx * (units * chunks) + n * units, 128), units)
            ffn_refs[n][0] = in_ref[:, at]
            ffn_refs[n][1] = out_ref[at, :].T

    outs = [((1, rows, 2 * half + 3 * columns), bf16)] + [((2, rows, units), bf16)] * chunks
    ins = [self_out, cross_in, cross_out, ffn_in, ffn_out]
    return kernel_call(body, ins, outs, scalars, name="other_shards")


def ffn_results(scalars, mine, theirs):
    _, rows, units = mine[0].shape
    chunks = len(mine)

    def body(scalars_ref, *refs):
        in_ref, out_ref = refs[-2:]
        ctx = scalars_ref[0]
        for place, refs_ in ((ctx, refs[:chunks]), (1 - ctx, refs[chunks : 2 * chunks])):
            for n, ref in enumerate(refs_):
                at = pl.ds(pl.multiple_of(place * (units * chunks) + n * units, 128), units)
                in_ref[:, at] = ref[0].astype(f32)
                out_ref[at, :] = ref[1].astype(f32).T

    whole = 2 * chunks * units
    outs = [((rows, whole), f32), ((whole, rows), f32)]
    return kernel_call(body, [*mine, *theirs], outs, scalars, name="ffn_results")


def first_results(scalars, mine, theirs, half):
    _, rows, columns = mine.shape
    count = (columns - 128) // half

    def body(scalars_ref, mine_ref, theirs_ref, out_ref, sums_ref):
        ctx = scalars_ref[0]
        for place, ref in ((ctx, mine_ref), (1 - ctx, theirs_ref)):
            at = pl.ds(pl.multiple_of(place * half, 128), half)
            for n in range(count):
                out_ref[n, :, at] = ref[0, :, n * half : (n + 1) * half].astype(f32)
        sums_ref[...] = mine_ref[0, :, count * half :].astype(f32) + theirs_ref[0, :, count * half :].astype(f32)

    outs = [((count, rows, 2 * half), f32), ((rows, 128), f32)]
    return kernel_call(body, [mine, theirs], outs, scalars, name="first_results")


def second_results(scalars, mine, theirs, half):
    _, rows, _ = mine.shape

    def body(scalars_ref, mine_ref, theirs_ref, so_ref, cross_ref, co_ref):
        ctx = scalars_ref[0]
        here = pl.multiple_of(ctx * half, 128)
        there = pl.multiple_of((1 - ctx) * half, 128)
        for at, ref in ((here, mine_ref), (there, theirs_ref)):
            for n in range(2):
                cross_ref[n + 1, :, pl.ds(at, half)] = ref[0, :, n * half : (n + 1) * half].astype(f32)
        for n, ref in enumerate((so_ref, None, co_ref)):
            start = 2 * half + 2 * n * half
            for at, a, b in ((here, start, start + half), (there, start + half, start)):
                item = mine_ref[0, :, a : a + half].astype(f32) + theirs_ref[0, :, b : b + half].astype(f32)
                if ref is None:
                    cross_ref[0, :, pl.ds(at, half)] = item
                else:
                    ref[pl.ds(at, half), :] = item.T

    outs = [((2 * half, rows), f32), ((3, rows, 2 * half), f32), ((2 * half, rows), f32)]
    return kernel_call(body, [mine, theirs], outs, scalars, name="second_results")


def move_blocks(arrays, places):
    count = places.shape[0]

    def body(places_ref, *refs):
        half = len(refs) // 2
        for in_ref, out_ref in zip(refs[:half], refs[half:]):
            width = in_ref.shape[1] // count
            for k in range(count):
                start = pl.multiple_of(places_ref[k] * width, width)
                out_ref[:, k * width : (k + 1) * width] = in_ref[:, pl.ds(start, width)]

    return pl.pallas_call(
        body,
        in_specs=[pl.BlockSpec(memory_space=pltpu.SMEM)]
        + [pl.BlockSpec(memory_space=pltpu.VMEM)] * len(arrays),
        out_specs=[pl.BlockSpec(memory_space=pltpu.VMEM)] * len(arrays),
        out_shape=[jax.ShapeDtypeStruct(a.shape, a.dtype) for a in arrays],
        compiler_params=pltpu.CompilerParams(vmem_limit_bytes=VMEM),
        cost_estimate=cost(1e8),
        name="move_blocks",
    )(places, *arrays)


def swap(values, axis):
    return lax.ppermute(values, axis, [(0, 1), (1, 0)])


class Ring:
    def __init__(self, size):
        self.size = size
        self.short = size <= RING_MOST and size % 2 == 0
        half = size // 2
        if self.short:
            self.order = [2 * p if p < half else 2 * (size - 1 - p) + 1 for p in range(size)]
        else:
            self.order = list(range(size))
        position = np.zeros(size, np.int32)
        position[self.order] = np.arange(size)
        there = np.zeros((size, size), np.int32)
        back = np.zeros((size, size), np.int32)
        for device in range(size):
            for k in range(size):
                place = self.order[(position[device] + k) % size] if self.short else k
                there[device, k] = place
                back[device, place] = k
        self.there, self.back = there, back

    def places(self, table):
        return lax.dynamic_index_in_dim(jnp.asarray(table), lax.axis_index("dp"), 0, False)

    def into(self, *arrays):
        return move_blocks(arrays, self.places(self.there)) if self.short else arrays

    def out_of(self, *arrays):
        return move_blocks(arrays, self.places(self.back)) if self.short else arrays

    def send(self, values, step):
        size, order = self.size, self.order
        pairs = [(order[p], order[(p + step) % size]) for p in range(size)]
        return lax.ppermute(values, "dp", pairs)

class Order:
    def __init__(self):
        self.mark = None

    def pin(self, *arrays):
        if self.mark is not None:
            _, arrays = hold((self.mark, arrays))
        return arrays if len(arrays) > 1 else arrays[0]

    def ran(self, result):
        self.mark = result
        return result

    def step(self, run, *arrays):
        if self.mark is not None:
            _, arrays = hold((self.mark, arrays))
        return self.ran(run(*arrays))


def middle_cut(columns):
    return columns // 2 // 128 * 128


class Gather:
    def __init__(self, ring, order, shard):
        self.ring, self.order, self.shard = ring, order, shard
        self.places, self.arrays = [(0, 0)], [shard]
        self.hop = 0
        if not ring.short:
            self.arrays = [lax.all_gather(shard, "dp", axis=1, tiled=True)]

    def advance(self):
        ring, size, rows = self.ring, self.ring.size, self.shard.shape[1]
        if not ring.short or self.hop > size // 2:
            return
        if self.hop == 0:
            self.ahead = self.behind = self.order.pin(self.shard)
        else:
            self.ahead, self.behind = self.order.ran(self.order.pin(self.ahead, self.behind))
            if self.hop < size // 2:
                self.places += [(self.hop * rows, 0), ((size - self.hop) * rows, 0)]
            else:
                cut = middle_cut(self.shard.shape[2])
                self.places += [(size // 2 * rows, 0), (size // 2 * rows, cut)]
            self.arrays += [self.ahead, self.behind]
        self.hop += 1
        if self.hop == size // 2:
            cut = middle_cut(self.shard.shape[2])
            self.ahead, self.behind = self.ahead[..., :cut], self.behind[..., cut:]
        if self.hop <= size // 2:
            self.ahead = ring.send(self.ahead, -1)
            self.behind = ring.send(self.behind, 1)

    def pieces(self):
        return self.places, self.arrays


def ring_add(full, ahead, behind, hop, size):
    count, rows, columns = full.shape
    rows = rows // size
    last = hop == 0
    cut = ahead.shape[2]

    def body(up_ref, down_ref, ahead_ref, behind_ref, *out_refs):
        if last:
            out = up_ref[...].astype(f32) + (ahead_ref[...].astype(f32) + behind_ref[...].astype(f32))
            out_refs[0][...] = out.astype(bf16)
            return
        up_out, down_out = out_refs
        if cut < columns:
            up_out[..., :cut] = (up_ref[..., :cut].astype(f32) + ahead_ref[...].astype(f32)).astype(bf16)
            up_out[..., cut:] = up_ref[..., cut:]
            down_out[..., :cut] = down_ref[..., :cut]
            down_out[..., cut:] = (down_ref[..., cut:].astype(f32) + behind_ref[...].astype(f32)).astype(bf16)
        else:
            up_out[...] = (up_ref[...].astype(f32) + ahead_ref[...].astype(f32)).astype(bf16)
            down_out[...] = (down_ref[...].astype(f32) + behind_ref[...].astype(f32)).astype(bf16)

    block = (count, rows, columns)
    moved = [pl.BlockSpec(item.shape, lambda i: (0, 0, 0)) for item in (ahead, behind)]
    outs = 1 if last else 2
    return pl.pallas_call(
        body,
        grid=(1,),
        in_specs=[
            pl.BlockSpec(block, lambda i: (0, hop, 0)),
            pl.BlockSpec(block, lambda i: (0, (size - hop) % size, 0)),
            *moved,
        ],
        out_specs=[pl.BlockSpec(block, lambda i: (0, 0, 0))] * outs,
        out_shape=[jax.ShapeDtypeStruct(block, bf16)] * outs,
        compiler_params=pltpu.CompilerParams(vmem_limit_bytes=VMEM),
        cost_estimate=cost(1e8),
        name="ring_add",
    )(full, full, ahead, behind)


class Scatter:
    def __init__(self, ring, order, full):
        self.ring, self.order, self.full, self.hop = ring, order, full, ring.size // 2
        if not ring.short:
            self.result = lax.psum_scatter(full, "dp", scatter_dimension=1, tiled=True)
            self.hop = -1

    def advance(self):
        ring, size = self.ring, self.ring.size
        if self.hop < 0:
            return
        if self.hop == size // 2:
            rows, cut = self.full.shape[1] // size, middle_cut(self.full.shape[2])
            start = self.hop * rows
            far = self.order.pin(self.full)[:, start : start + rows]
            self.ahead, self.behind = far[..., :cut], far[..., cut:]
        else:
            run = functools.partial(ring_add, hop=self.hop, size=size)
            out = self.order.step(run, self.full, self.ahead, self.behind)
            if self.hop == 0:
                self.result, self.hop = out[0], -1
                return
            self.ahead, self.behind = out
        self.hop -= 1
        self.ahead = ring.send(self.ahead, 1)
        self.behind = ring.send(self.behind, -1)


def per_device(
    ring,
    hidden_in,
    encoder_states,
    out_grad,
    target_ids,
    source_ids,
    self_in,
    self_out,
    cross_in,
    cross_out,
    ffn_in,
    ffn_out,
    norm_gain,
    norm_bias,
):
    ctx = lax.axis_index("ctx")
    core = lax.axis_index("tp")
    scalars = jnp.stack([ctx, core]).astype(jnp.int32)
    rows, width = hidden_in.shape
    source_rows = encoder_states.shape[0]
    inner = self_in.shape[2]
    half = inner // 2
    units = ffn_in.shape[1] // 2 // FFN_CHUNKS
    order = Order()

    def part(array, axis, place):
        count = array.shape[axis] // 2
        return lax.dynamic_slice_in_dim(array, place * count, count, axis)

    def ordered(mine, theirs, axis, place=ctx):
        first = place == 0
        return jnp.concatenate(
            [jnp.where(first, mine, theirs), jnp.where(first, theirs, mine)], axis
        )

    def relative(array, axis):
        return jnp.concatenate([part(array, axis, ctx), part(array, axis, 1 - ctx)], axis)

    def turned(values):
        count = values.shape[0] // 2
        return jnp.concatenate([values[count:], values[:count]], 0)

    def with_other_rows(own, got, rest):
        return jnp.concatenate([own, ordered(got, rest, 0, core)], 0)

    def pair_sum(low, other):
        return low.astype(f32) + other.astype(f32)

    def give_rows(low):
        count = low.shape[0] // 2
        return jnp.concatenate([part(low[:count], 0, 1 - core), part(low[count:], 0, 1 - core)], 0)

    def keep_rows(low, taken):
        count = low.shape[0] // 2
        kept = jnp.concatenate([part(low[:count], 0, core), part(low[count:], 0, core)], 0)
        total = kept.astype(f32) + taken.astype(f32)
        return total[: count // 2], total[count // 2 :].astype(bf16)

    def low_product(a, b):
        return nt(a, b).astype(bf16)

    def grad_product(a, b):
        return tn(a, b).astype(bf16)

    def make_seen(target_ids, source_ids):
        target = relative(target_ids[0], 0)
        place = relative(jnp.arange(2 * rows, dtype=jnp.int32), 0)
        sources = relative(source_ids[0], 0)
        nowhere = jnp.zeros_like(sources)
        return (
            seen_by(target, place, target, place),
            seen_by(target[:rows], jnp.zeros_like(target[:rows]), sources, nowhere),
        )

    first = Gather(ring, order, order.ran(first_shards(scalars, self_in, norm_gain, norm_bias)))
    first.advance()
    (hidden_own,) = order.step(ring.into, hidden_in)
    hidden_got = swap(part(hidden_own, 0, core), "ctx")
    second_shard, *ffn_shards = order.step(
        lambda *arrays: other_shards(scalars, *arrays, FFN_CHUNKS),
        self_out,
        cross_in,
        cross_out,
        ffn_in,
        ffn_out,
    )
    second = Gather(ring, order, second_shard)
    ffn = [Gather(ring, order, shard) for shard in ffn_shards]
    first.advance()
    self_seen, cross_seen = order.step(make_seen, target_ids, source_ids)
    first.advance()
    second.advance()
    hidden_got = order.ran(order.pin(hidden_got))
    hidden_rest = swap(hidden_got, "tp")
    cotangent, states = order.step(ring.into, out_grad, encoder_states)
    given_got = swap(part(jnp.concatenate([cotangent, states], 0), 0, core), "ctx")
    first.advance()
    hidden_got, hidden_rest = order.ran(order.pin(hidden_got, hidden_rest))
    first.advance()

    places, pieces = first.pieces()
    qkv, input_one, normal_one, vectors = order.step(
        lambda *arrays: first_project(scalars, *arrays[:3], (places, arrays[3:]), 3 * half),
        hidden_own,
        hidden_got,
        hidden_rest,
        *pieces,
    )
    second.advance()
    mixed, total_one = order.step(
        lambda qkv: attend_forward((qkv, 0), (qkv, 1), (qkv, 2), self_seen, half), qkv
    )
    mixed_got = swap(mixed[rows:], "ctx")
    second.advance()
    given_got = order.ran(order.pin(given_got))
    given_rest = swap(given_got, "tp")
    mixed_one = order.step(lambda a, b: jnp.concatenate([a[:rows], b], 1), mixed, mixed_got)

    def sort_given(cotangent, states, got, rest):
        taken = ordered(got, rest, 0, core)
        return (
            jnp.concatenate([cotangent, taken[:rows]], 0),
            jnp.concatenate([states, taken[rows:]], 0),
        )

    out_cot, source = order.step(sort_given, cotangent, states, given_got, given_rest)
    second.advance()
    ffn[0].advance()
    first_w = order.step(
        lambda *arrays: join_pieces((places, arrays), [3 * half, 128])[0], *pieces
    )
    second.advance()
    second_places, pieces = second.pieces()
    widths = [2 * half, inner, inner, inner]
    key_w, self_o, cross_q, cross_o = order.step(
        lambda *arrays: join_pieces((second_places, arrays), widths), *pieces
    )
    branch = order.step(low_product, mixed_one, self_o)
    branch_got = swap(branch, "tp")

    kv = order.step(lambda a, b: nn(a, b).astype(bf16), source, key_w)
    kv_got = swap(turned(kv), "ctx")
    first_rows, input_two, cross_queries = order.step(
        lambda *arrays: branch_norm(*arrays[:-1], 1, arrays[-1]),
        hidden_own,
        branch,
        branch_got,
        vectors,
        cross_q,
    )
    ffn[0].advance()
    ffn[1].advance()
    key_cross, value_cross = order.step(
        lambda kv, other: (
            jnp.concatenate([kv[:, :half], other[:, :half]], 1),
            jnp.concatenate([kv[:, half:], other[:, half:]], 1),
        ),
        kv,
        kv_got,
    )
    mixed_two, total_two = order.step(
        lambda q, k, v: attend_forward((q, 0), (k, 0), (v, 0), cross_seen, inner),
        cross_queries,
        key_cross,
        value_cross,
    )
    branch = order.step(low_product, mixed_two, cross_o)
    branch_got = swap(branch, "tp")
    ffn[0].advance()
    second_rows, input_own = order.step(
        lambda *arrays: branch_norm(*arrays, 2), first_rows, branch, branch_got, vectors
    )
    input_got = swap(part(input_own, 0, core), "ctx")
    ffn[1].advance()
    input_got = order.ran(order.pin(input_got))
    input_rest = swap(input_got, "tp")
    ffn[0].advance()
    input_three = order.step(with_other_rows, input_own, input_got, input_rest)
    ffn[1].advance()
    ffn[0].advance()

    ffn_places, first_half = ffn[0].pieces()
    act, grad_up, grad_norm = order.step(
        lambda a, g, *arrays: ffn_first(a, g, (ffn_places, arrays), units),
        input_three,
        out_cot,
        *first_half,
    )
    ffn[1].advance()
    grad_w, result = order.step(
        lambda a, g, act, gu: ffn_second(a, g, act, gu, (ffn_places, first_half), None),
        input_three,
        out_cot,
        act,
        grad_up,
    )
    scatters = [Scatter(ring, order, grad_w)]
    scatters[0].advance()
    ffn[1].advance()
    _, second_half = ffn[1].pieces()
    act, grad_up, grad_norm = order.step(
        lambda a, g, before, *arrays: ffn_first(a, g, (ffn_places, arrays), units, before),
        input_three,
        out_cot,
        grad_norm,
        *second_half,
    )
    taken = swap(give_rows(grad_norm), "tp")
    scatters[0].advance()
    near, far = order.step(keep_rows, grad_norm, taken)
    far_got = swap(far, "ctx")
    grad_w, result = order.step(
        lambda a, g, act, gu, before: ffn_second(
            a, g, act, gu, (ffn_places, second_half), before
        ),
        input_three,
        out_cot,
        act,
        grad_up,
        result,
    )
    scatters.append(Scatter(ring, order, grad_w))
    scatters[1].advance()
    done = order.step(pair_sum, near, far_got)
    done_got = swap(done, "tp")
    scatters[0].advance()

    grad_mixed, grad_branch, grad_second, sums_three = order.step(
        lambda *arrays: norm_back(scalars, arrays[0], arrays[1], True, *arrays[2:5], 2, arrays[5]),
        done,
        done_got,
        cotangent,
        second_rows,
        vectors,
        cross_o,
    )

    grad_cq, grad_ck, grad_cv = order.step(
        lambda g, o: attend_backward(
            g, (cross_queries, 0), (key_cross, 0), (value_cross, 0), o, total_two, cross_seen, inner
        ),
        grad_mixed,
        mixed_two,
    )
    branch = order.step(low_product, grad_cq, cross_q)
    branch_got = swap(branch, "tp")
    scatters[1].advance()
    given = swap(turned(jnp.concatenate([grad_ck[:, half:], grad_cv[:, half:]], 1)), "ctx")
    grad_cross_o = order.step(grad_product, grad_branch, mixed_two)
    grad_cross_q = order.step(grad_product, input_two, grad_cq)
    grad_mixed, grad_branch, grad_first, sums_two = order.step(
        lambda *arrays: norm_back(scalars, arrays[0], arrays[1], False, *arrays[2:5], 1, arrays[5]),
        branch,
        branch_got,
        grad_second,
        first_rows,
        vectors,
        self_o,
    )
    mixed_got = swap(grad_mixed[:, half:], "ctx")
    scatters[0].advance()
    grad_kv = order.step(
        lambda a, b, c: pair_sum(jnp.concatenate([a[:, :half], b[:, :half]], 1), c).astype(bf16),
        grad_ck,
        grad_cv,
        given,
    )
    grad_key_w, source_low = order.step(
        lambda a, b, w: (grad_product(a, b), low_product(b, w)), source, grad_kv, key_w
    )
    source_got = swap(source_low[source_rows:], "ctx")
    grad_self_o = order.step(grad_product, grad_branch, mixed_one)
    scatters[1].advance()
    grad_third = order.step(
        lambda *parts: jnp.concatenate(parts, 1)[None],
        grad_key_w,
        grad_self_o,
        grad_cross_q,
        grad_cross_o,
    )
    second_scatter = Scatter(ring, order, grad_third)

    grad_mixed = order.step(
        lambda a, b: jnp.concatenate([a[:, :half], b], 0), grad_mixed, mixed_got
    )
    scatters[0].advance()
    ffn_mine = [scatters[0].result]
    ffn_got = [swap(ffn_mine[0], "ctx")]
    grad_parts = order.step(
        lambda g, o: attend_backward(
            g, (qkv, 0), (qkv, 1), (qkv, 2), o, total_one, self_seen, half
        ),
        grad_mixed,
        mixed,
    )
    scatters[1].advance()
    partial, grad_qkv, sums_one = order.step(
        lambda q, k, v, w, normal: first_partial((q, k, v), w, normal),
        *grad_parts,
        first_w,
        normal_one,
    )
    taken = swap(give_rows(partial), "tp")

    def first_grad(low, grad_qkv, one, two, three):
        sums = jnp.concatenate([one, 0.5 * two, 0.5 * three], 0).astype(bf16).T
        sums = jnp.pad(sums, ((0, 0), (0, 128 - sums.shape[1])))
        return jnp.concatenate([grad_product(low, grad_qkv), sums], 1)[None]

    first_scatter = Scatter(
        ring, order, order.step(first_grad, input_one, grad_qkv, sums_one, sums_two, sums_three)
    )
    first_scatter.advance()
    second_scatter.advance()
    near, far = order.step(keep_rows, partial, taken)
    far_got = swap(far, "ctx")
    scatters[1].advance()
    ffn_mine.append(scatters[1].result)
    ffn_got.append(swap(ffn_mine[1], "ctx"))
    first_scatter.advance()
    low = order.step(
        lambda a, b: pair_sum(a, b).astype(bf16), result[:rows], swap(result[rows:], "ctx")
    )
    result_low, result_got = low, swap(low, "tp")
    second_scatter.advance()
    low = order.step(
        lambda a, b: pair_sum(a, b).astype(bf16), source_low[:source_rows], source_got
    )
    source_low, source_got = low, swap(low, "tp")
    first_scatter.advance()
    done = order.step(pair_sum, near, far_got)
    done_got = swap(done, "tp")
    second_scatter.advance()
    first_scatter.advance()
    grad_source, result = order.step(
        lambda a, b, c, d, e: (pair_sum(a, b), (c + pair_sum(d, e)).astype(bf16)),
        source_low,
        source_got,
        second_rows,
        result_low,
        result_got,
    )
    result, grad_source = order.step(ring.out_of, result, grad_source)
    second_scatter.advance()
    grad_input = order.step(
        lambda *arrays: last_norm_back(scalars, *arrays, ring.places(ring.there)),
        done,
        done_got,
        grad_first,
        hidden_own,
        vectors,
    )
    first_scatter.advance()
    first_mine = first_scatter.result
    first_other = swap(first_mine, "ctx")

    grad_ffn_in, grad_ffn_out = order.step(
        lambda *items: ffn_results(scalars, items[:FFN_CHUNKS], items[FFN_CHUNKS:]),
        *ffn_mine,
        *ffn_got,
    )
    second_scatter.advance()
    second_mine = second_scatter.result
    second_other = swap(second_mine, "ctx")
    grad_self_in, sums = order.step(
        lambda a, b: first_results(scalars, a, b, half), first_mine, first_other
    )
    sums_got = swap(sums, "tp")
    grad_self_out, grad_cross_in, grad_cross_out = order.step(
        lambda a, b: second_results(scalars, a, b, half), second_mine, second_other
    )
    sums = (sums + sums_got)[:, :6].T
    return (
        result,
        grad_input,
        grad_source,
        grad_self_in,
        grad_self_out,
        grad_cross_in,
        grad_cross_out,
        grad_ffn_in,
        grad_ffn_out,
        jnp.stack([sums[0], sums[2], sums[4]]),
        jnp.stack([sums[1], sums[3], sums[5]]),
    )


def solution(mesh):
    return jax.shard_map(
        functools.partial(per_device, Ring(mesh.shape["dp"])),
        mesh=mesh,
        in_specs=(
            P(("dp", "ctx"), None),
            P(("dp", "ctx"), None),
            P(("dp", "ctx"), None),
            P("dp", None),
            P("dp", None),
            P(None, "dp", "tp"),
            P("tp", "dp"),
            P(None, "dp", "tp"),
            P("tp", "dp"),
            P("dp", "tp"),
            P("tp", "dp"),
            P(None, "dp"),
            P(None, "dp"),
        ),
        out_specs=(
            P(("dp", "ctx"), None),
            P(("dp", "ctx"), None),
            P(("dp", "ctx"), None),
            P(None, "dp", "tp"),
            P("tp", "dp"),
            P(None, "dp", "tp"),
            P("tp", "dp"),
            P("dp", "tp"),
            P("tp", "dp"),
            P(None, "dp"),
            P(None, "dp"),
        ),
        check_vma=False,
    )
```

```python
import functools

import jax
import jax.numpy as jnp
import numpy as np
from jax import lax
from jax.experimental import pallas as pl
from jax.experimental.pallas import tpu as pltpu
from jax.sharding import PartitionSpec as P

HEAD_DIM = 64
EPSILON = 1e-05
RING_MOST = 8
SCORE_SCALE = HEAD_DIM**-0.5 * 1.4426950408889634
MASKED = -1e30
TILE = 256
QUAD = 256
FFN_TILE = 1024
FFN_STEPS = 4
FFN_CHUNKS = 1
VMEM = 52 << 20

f32 = jnp.float32
bf16 = jnp.bfloat16
hold = lax.optimization_barrier


def nn(left, right):
    return jnp.dot(left, right, preferred_element_type=f32)


def tn(left, right):
    return lax.dot_general(left, right, (((0,), (0,)), ((), ())), preferred_element_type=f32)


def nt(left, right):
    return lax.dot_general(left, right, (((1,), (1,)), ((), ())), preferred_element_type=f32)


def cost(flops):
    return pl.CostEstimate(flops=int(flops), bytes_accessed=0, transcendentals=0)


def head_stack(values):
    lane = lax.broadcasted_iota(jnp.int32, values.shape, 1) // HEAD_DIM
    return jnp.concatenate(
        [jnp.where(lane == h, values, jnp.zeros_like(values)) for h in range(QUAD // HEAD_DIM)], 0
    )


def attend_forward_kernel(need, q_ref, *refs):
    groups = q_ref.shape[1] // QUAD
    k_refs, v_refs, refs = refs[:groups], refs[groups : 2 * groups], refs[2 * groups :]
    lo_ref, hi_ref, code_ref = refs[:3]
    o_ref, lse_ref, s_ref, vt_ref, qs_ref, peak_ref, total_ref, out_ref, codes_ref = refs[-9:]
    step = pl.program_id(0)
    tiles = k_refs[0].shape[0] // TILE
    per = QUAD // HEAD_DIM

    @pl.when(step == 0)
    def _():
        for t in range(tiles):
            for g in range(groups):
                span = slice(t * TILE, (t + 1) * TILE)
                vt_ref[g * QUAD : (g + 1) * QUAD, span] = v_refs[g][span, :].T
        turn_codes(code_ref, codes_ref)

    peak_ref[...] = jnp.full_like(peak_ref, MASKED)
    total_ref[...] = jnp.zeros_like(total_ref)
    out_ref[...] = jnp.zeros_like(out_ref)
    for g in range(groups):
        qs_ref[g] = head_stack(q_ref[:, g * QUAD : (g + 1) * QUAD])
    for t in range(tiles):

        @pl.when(need[step * tiles + t] != 0)
        def _():
            span = slice(t * TILE, (t + 1) * TILE)
            code = codes_ref[span, :]
            allowed = (code >= lo_ref[...]) & (code <= hi_ref[...])
            for g in range(groups):
                scores = nt(k_refs[g][span, :], qs_ref[g])
                for i in range(per):
                    lanes = slice(i * TILE, (i + 1) * TILE)
                    item = jnp.where(allowed, scores[:, lanes] * SCORE_SCALE, MASKED)
                    s_ref[t, g, :, lanes] = item
                    peak_ref[g : g + 1, lanes] = jnp.maximum(
                        peak_ref[g : g + 1, lanes], jnp.max(item, axis=0, keepdims=True)
                    )

    for t in range(tiles):

        @pl.when(need[step * tiles + t] != 0)
        def _():
            span = slice(t * TILE, (t + 1) * TILE)
            for g in range(groups):
                for i in range(per):
                    lanes = slice(i * TILE, (i + 1) * TILE)
                    h = g * per + i
                    expo = jnp.exp2(s_ref[t, g, :, lanes] - peak_ref[g : g + 1, lanes])
                    total_ref[g : g + 1, lanes] += jnp.sum(expo, axis=0, keepdims=True)
                    out_ref[h] += nn(vt_ref[h * HEAD_DIM : (h + 1) * HEAD_DIM, span], expo.astype(bf16))

    for g in range(groups):
        items = []
        for i in range(per):
            lanes = slice(i * TILE, (i + 1) * TILE)
            h = g * per + i
            total = total_ref[g : g + 1, lanes]
            lse_ref[h : h + 1, :] = peak_ref[g : g + 1, lanes] + jnp.log2(total)
            items.append(out_ref[h] * (1.0 / total))
        o_ref[:, g * QUAD : (g + 1) * QUAD] = jnp.concatenate(items, 0).T.astype(bf16)


def turn_codes(code_ref, codes_ref):
    keys, lanes = codes_ref.shape
    for t in range(keys // TILE):
        span = slice(t * TILE, (t + 1) * TILE)
        codes_ref[span, :] = jnp.broadcast_to(code_ref[:, span], (lanes, TILE)).T


def attend_forward(q, keys, values, seen, span):
    lo, hi, code, need = seen
    groups, stacked = len(keys), QUAD // HEAD_DIM * TILE
    width, depth = groups * QUAD, keys[0][0].shape[0]
    heads = width // HEAD_DIM
    start, count = span
    skip = start // TILE
    need = need[skip * (depth // TILE) :]
    col = lambda i, need: (0, i + skip)
    return pl.pallas_call(
        attend_forward_kernel,
        grid_spec=pltpu.PrefetchScalarGridSpec(
            num_scalar_prefetch=1,
            grid=(count // TILE,),
            in_specs=[pl.BlockSpec((TILE, width), lambda i, need: (i + skip, q[1]))]
            + [pl.BlockSpec((depth, QUAD), lambda i, need, n=n: (0, n)) for _, n in keys + values]
            + [
                pl.BlockSpec((1, TILE), col),
                pl.BlockSpec((1, TILE), col),
                pl.BlockSpec((1, depth), lambda i, need: (0, 0)),
            ],
            out_specs=[
                pl.BlockSpec((TILE, width), lambda i, need: (i, 0)),
                pl.BlockSpec((heads, TILE), lambda i, need: (0, i)),
            ],
            scratch_shapes=[
                pltpu.VMEM((depth // TILE, groups, TILE, stacked), f32),
                pltpu.VMEM((width, depth), bf16),
                pltpu.VMEM((groups, stacked, QUAD), bf16),
                pltpu.VMEM((groups, stacked), f32),
                pltpu.VMEM((groups, stacked), f32),
                pltpu.VMEM((heads, HEAD_DIM, TILE), f32),
                pltpu.VMEM((depth, TILE), jnp.int32),
            ],
        ),
        out_shape=[
            jax.ShapeDtypeStruct((count, width), bf16),
            jax.ShapeDtypeStruct((heads, count), f32),
        ],
        compiler_params=pltpu.CompilerParams(vmem_limit_bytes=VMEM),
        cost_estimate=cost(1e8),
        name="attend_forward",
    )(need, q[0], *[item for item, _ in keys + values], lo, hi, code)


def attend_backward_kernel(parts, need, q_ref, *refs):
    groups = q_ref.shape[1] // QUAD
    k_refs, v_refs, refs = refs[:groups], refs[groups : 2 * groups], refs[2 * groups :]
    rows = []
    for _ in range(3):
        rows.append(refs[:parts])
        refs = refs[parts:]
    lo_ref, hi_ref, code_ref, gq_ref, *refs = refs
    gkv_refs, refs = refs[:groups], refs[groups:]
    gk_acc, gv_acc, gq_acc, qs_ref, gs_ref, inner_ref, lse_ref, p_ref, ds_ref, dst_ref, codes_ref = refs
    step = pl.program_id(0)
    width = q_ref.shape[1]
    depth = k_refs[0].shape[0]
    tiles = depth // TILE
    per = QUAD // HEAD_DIM
    heads = width // HEAD_DIM

    @pl.when(step == 0)
    def _():
        gk_acc[...] = jnp.zeros_like(gk_acc)
        gv_acc[...] = jnp.zeros_like(gv_acc)
        turn_codes(code_ref, codes_ref)

    def chosen(items):
        if len(items) == 1:
            return items[0][...]
        return jnp.where(step < pl.num_programs(0) // 2, items[0][...], items[1][...])

    gq_acc[...] = jnp.zeros_like(gq_acc)
    grad, out = chosen(rows[0]), chosen(rows[1])
    lse_ref[...] = chosen(rows[2])
    both = grad.astype(f32) * out.astype(f32)
    pick = lax.broadcasted_iota(jnp.int32, (heads, width), 0) == (
        lax.broadcasted_iota(jnp.int32, (heads, width), 1) // HEAD_DIM
    )
    inner_ref[...] = lax.dot_general(
        pick.astype(f32),
        both,
        (((1,), (1,)), ((), ())),
        precision=lax.Precision.HIGHEST,
        preferred_element_type=f32,
    )
    for g in range(groups):
        lanes = slice(g * QUAD, (g + 1) * QUAD)
        qs_ref[g] = head_stack(q_ref[:, lanes])
        gs_ref[g] = head_stack(grad[:, lanes])
    for t in range(tiles):

        @pl.when(need[step * tiles + t] != 0)
        def _():
            span = slice(t * TILE, (t + 1) * TILE)
            code = codes_ref[span, :]
            allowed = (code >= lo_ref[...]) & (code <= hi_ref[...])
            for g in range(groups):
                lanes = slice(g * QUAD, (g + 1) * QUAD)
                scores = nt(k_refs[g][span, :], qs_ref[g])
                grads = nt(v_refs[g][span, :], gs_ref[g])
                for i in range(per):
                    at = slice(i * TILE, (i + 1) * TILE)
                    h = g * per + i
                    item = jnp.where(allowed, scores[:, at] * SCORE_SCALE, MASKED)
                    probs = jnp.exp2(item - lse_ref[h : h + 1, :])
                    p_ref[:, at] = probs.astype(bf16)
                    grad = (probs * (grads[:, at] - inner_ref[h : h + 1, :])).astype(bf16)
                    ds_ref[:, at] = grad
                    dst_ref[:, at] = grad.T
                gv_acc[span, lanes] += nn(p_ref[...], gs_ref[g])
                gk_acc[span, lanes] += nn(ds_ref[...], qs_ref[g])
                gq_acc[:, lanes] += nn(dst_ref[...], head_stack(k_refs[g][span, :]))

    gq_ref[...] = (gq_acc[...] * HEAD_DIM**-0.5).astype(bf16)

    @pl.when(step == pl.num_programs(0) - 1)
    def _():
        half = depth // 2
        for g, ref in enumerate(gkv_refs):
            lanes = slice(g * QUAD, (g + 1) * QUAD)
            for here in (slice(0, half), slice(half, depth)):
                there = here if g == 0 else slice(half - here.start, depth - here.start)
                ref[there, :QUAD] = (gk_acc[here, lanes] * HEAD_DIM**-0.5).astype(bf16)
                ref[there, QUAD:] = gv_acc[here, lanes].astype(bf16)


def attend_backward(g, q, keys, values, o, lse, seen):
    lo, hi, code, need = seen
    groups, stacked = len(keys), QUAD // HEAD_DIM * TILE
    width, depth = groups * QUAD, keys[0][0].shape[0]
    rows, heads, parts = q[0].shape[0], width // HEAD_DIM, len(g)
    each = rows // TILE // parts
    row = lambda i, need: (i, 0)
    col = lambda i, need: (0, i)
    full = lambda i, need: (0, 0)
    places = [lambda i: jnp.clip(i, 0, each - 1), lambda i: jnp.clip(i - each, 0, each - 1)][:parts]
    tall = [pl.BlockSpec((TILE, width), lambda i, need, at=at: (at(i), 0)) for at in places]
    flat = [pl.BlockSpec((heads, TILE), lambda i, need, at=at: (0, at(i))) for at in places]
    return pl.pallas_call(
        functools.partial(attend_backward_kernel, parts),
        grid_spec=pltpu.PrefetchScalarGridSpec(
            num_scalar_prefetch=1,
            grid=(rows // TILE,),
            in_specs=[pl.BlockSpec((TILE, width), lambda i, need: (i, q[1]))]
            + [pl.BlockSpec((depth, QUAD), lambda i, need, n=n: (0, n)) for _, n in keys + values]
            + tall
            + tall
            + flat
            + [
                pl.BlockSpec((1, TILE), col),
                pl.BlockSpec((1, TILE), col),
                pl.BlockSpec((1, depth), full),
            ],
            out_specs=[pl.BlockSpec((TILE, width), row)]
            + [pl.BlockSpec((depth, 2 * QUAD), full)] * groups,
            scratch_shapes=[
                pltpu.VMEM((depth, width), f32),
                pltpu.VMEM((depth, width), f32),
                pltpu.VMEM((TILE, width), f32),
                pltpu.VMEM((groups, stacked, QUAD), bf16),
                pltpu.VMEM((groups, stacked, QUAD), bf16),
                pltpu.VMEM((heads, TILE), f32),
                pltpu.VMEM((heads, TILE), f32),
                pltpu.VMEM((TILE, stacked), bf16),
                pltpu.VMEM((TILE, stacked), bf16),
                pltpu.VMEM((TILE, stacked), bf16),
                pltpu.VMEM((depth, TILE), jnp.int32),
            ],
        ),
        out_shape=[jax.ShapeDtypeStruct((rows, width), bf16)]
        + [jax.ShapeDtypeStruct((depth, 2 * QUAD), bf16)] * groups,
        compiler_params=pltpu.CompilerParams(vmem_limit_bytes=VMEM),
        cost_estimate=cost(1e8),
        name="attend_backward",
    )(need, q[0], *[item for item, _ in keys + values], *g, *o, *lse, lo, hi, code)


def seen_by(lo, hi, code):
    first, last, codes = (item.reshape(-1, TILE) for item in (lo, hi, code))
    need = (first[:, None, 0] <= codes[None, :, -1]) & (codes[None, :, 0] <= last[:, None, -1])
    return lo[None, :], hi[None, :], code[None, :], need.astype(jnp.int32).reshape(-1)


def gelu_pair(u):
    c = 0.7978845608028654
    square = u * u
    t = jnp.tanh(u * (c + (c * 0.044715) * square))
    half = 0.5 + 0.5 * t
    slope = half + 0.5 * u * (1.0 - t * t) * (c + (3 * c * 0.044715) * square)
    return u * half, slope


def start_pieces(places, refs, scratch, sems, which=slice(None)):
    copies = []
    for n, ((row, col), ref) in enumerate(zip(places, refs)):
        _, r, c = ref.shape
        target = scratch.at[:, pl.ds(row, r), pl.ds(col, c)]
        copies.append(pltpu.make_async_copy(ref.at[which], target, sems.at[n]))
        copies[-1].start()
    return copies


def rows_by_core(scalars, step):
    return jnp.where(step < 2, 1 - scalars[1], scalars[1])


def core_outputs(tile, width):
    specs = [pl.BlockSpec((tile, width), lambda i, scalars: (0, 0))] * 4
    return specs, [jax.ShapeDtypeStruct((tile, width), bf16)] * 4


def core_store(refs, value):
    for n, ref in enumerate(refs):

        @pl.when(pl.program_id(0) == n)
        def _():
            ref[...] = value


def ffn_first(scalars, a, g, shards):
    places, arrays = shards
    rows, width = a[0].shape
    cols = max(col + piece.shape[2] for (_, col), piece in zip(places, arrays))
    tile = rows // 2
    chunk = min(FFN_TILE, cols)

    def body(scalars_ref, a_ref, far_a_ref, g_ref, far_g_ref, *refs):
        pieces, (act_ref, gu_ref, *gn_refs), (w, sems) = refs[: len(places)], refs[len(places) : -2], refs[-2:]
        step = pl.program_id(0)

        @pl.when(step == 0)
        def _():
            for copy in start_pieces(places, pieces, w, sems):
                copy.wait()

        near = step % 2 == 0
        a, g = jnp.where(near, a_ref[...], far_a_ref[...]), jnp.where(near, g_ref[...], far_g_ref[...])
        total = jnp.zeros((tile, width), f32)
        for j in range(cols // chunk):
            span = slice(j * chunk, (j + 1) * chunk)
            act, slope = gelu_pair(nn(a, w[0, :, span]))
            act_ref[:, span] = act.astype(bf16)
            gu = (nn(g, w[1, :, span]) * slope).astype(bf16)
            gu_ref[:, span] = gu
            total = total + nt(gu, w[0, :, span])
        core_store(gn_refs, total.astype(bf16))

    block = pl.BlockSpec((tile, width), lambda i, scalars: (rows_by_core(scalars, i), 0))
    narrow = pl.BlockSpec((tile, cols), lambda i, scalars: (2 * (i % 2) + rows_by_core(scalars, i), 0))
    out_specs, out_shapes = core_outputs(tile, width)
    return pl.pallas_call(
        body,
        grid_spec=pltpu.PrefetchScalarGridSpec(
            num_scalar_prefetch=1,
            grid=(4,),
            in_specs=[block] * 4 + [pl.BlockSpec(memory_space=pltpu.HBM)] * len(arrays),
            out_specs=[narrow, narrow] + out_specs,
            scratch_shapes=[
                pltpu.VMEM((2, width, cols), bf16),
                pltpu.SemaphoreType.DMA((len(arrays),)),
            ],
        ),
        out_shape=[jax.ShapeDtypeStruct((2 * rows, cols), bf16)] * 2 + out_shapes,
        compiler_params=pltpu.CompilerParams(vmem_limit_bytes=VMEM),
        cost_estimate=cost(1e8),
        name="ffn_first",
    )(scalars, *a, *g, *arrays)


def ffn_grads(ring, a, g, act, gu):
    rows, width = a[0].shape
    cols = act.shape[1]
    steps = FFN_STEPS
    tile = width // steps
    shape = (2, width, cols)
    far = far_block(ring, shape)

    def body(a_ref, far_a_ref, g_ref, far_g_ref, act_ref, gu_ref, dw_ref, *far_refs):
        for n, (near, other, right) in enumerate(
            ((a_ref, far_a_ref, gu_ref), (g_ref, far_g_ref, act_ref))
        ):
            left = jnp.concatenate([near[...].T, other[...].T], 1)
            grad = nn(left, right[...]).astype(bf16)
            dw_ref[n] = grad
            store_far(far, far_refs, tile, grad, n)

    full = pl.BlockSpec((2 * rows, cols), lambda i: (0, 0))
    wide = pl.BlockSpec((rows, tile), lambda i: (0, i))
    far_specs, far_shapes = far_outputs(far, shape)
    return pl.pallas_call(
        body,
        grid=(steps,),
        in_specs=[wide] * 4 + [full, full],
        out_specs=[pl.BlockSpec((2, tile, cols), lambda i: (0, i, 0))] + far_specs,
        out_shape=[jax.ShapeDtypeStruct(shape, bf16)] + far_shapes,
        compiler_params=pltpu.CompilerParams(vmem_limit_bytes=VMEM),
        cost_estimate=cost(1e8),
        name="ffn_grads",
    )(*a, *g, act, gu)


def ffn_output(act, shards):
    places, arrays = shards
    rows, cols = act.shape
    width = max(row + piece.shape[1] for (row, _), piece in zip(places, arrays))
    steps = FFN_STEPS
    tile = rows // steps
    near = steps // 2

    def body(act_ref, *refs):
        pieces, (near_ref, far_ref, w, sems) = refs[:-4], refs[-4:]
        step = pl.program_id(0)

        @pl.when(step == 0)
        def _():
            for copy in start_pieces(places, pieces, w, sems, slice(1, 2)):
                copy.wait()

        out = nt(act_ref[...], w[0]).astype(bf16)

        @pl.when(step < near)
        def _():
            near_ref[...] = out

        @pl.when(step >= near)
        def _():
            far_ref[...] = out

    block = (tile, width)
    return pl.pallas_call(
        body,
        grid=(steps,),
        in_specs=[pl.BlockSpec((tile, cols), lambda i: (i, 0))]
        + [pl.BlockSpec(memory_space=pltpu.HBM)] * len(arrays),
        out_specs=[
            pl.BlockSpec(block, lambda i: (jnp.minimum(i, near - 1), 0)),
            pl.BlockSpec(block, lambda i: (jnp.maximum(i - near, 0), 0)),
        ],
        out_shape=[jax.ShapeDtypeStruct((rows // 2, width), bf16)] * 2,
        scratch_shapes=[
            pltpu.VMEM((1, width, cols), bf16),
            pltpu.SemaphoreType.DMA((len(arrays),)),
        ],
        compiler_params=pltpu.CompilerParams(vmem_limit_bytes=VMEM),
        cost_estimate=cost(1e8),
        name="ffn_output",
    )(act, *arrays)


def normalized(values):
    centre = jnp.mean(values, axis=-1, keepdims=True)
    centred = values - centre
    factor = lax.rsqrt(jnp.mean(centred * centred, axis=-1, keepdims=True) + EPSILON)
    return centred * factor, factor


def norm_backward(grad_norm, normal, factor, gain):
    scaled = grad_norm * gain
    inner = (
        scaled
        - jnp.mean(scaled, axis=-1, keepdims=True)
        - normal * jnp.mean(scaled * normal, axis=-1, keepdims=True)
    )
    return factor * inner


def kernel_call(body, ins, outs, scalars=None, scratch=(), name=None, spaces=None):
    spaces = spaces or {}
    specs = [pl.BlockSpec(memory_space=spaces.get(n, pltpu.VMEM)) for n in range(len(ins))]
    out_specs = [pl.BlockSpec(memory_space=spaces.get(("out", n), pltpu.VMEM)) for n in range(len(outs))]
    if scalars is not None:
        specs = [pl.BlockSpec(memory_space=pltpu.SMEM)] + specs
        ins = [scalars] + list(ins)
    return pl.pallas_call(
        body,
        in_specs=specs,
        out_specs=out_specs,
        out_shape=[jax.ShapeDtypeStruct(*out) for out in outs],
        scratch_shapes=list(scratch),
        compiler_params=pltpu.CompilerParams(vmem_limit_bytes=VMEM),
        cost_estimate=cost(1e8),
        name=name,
    )(*ins)


def tiles_of(rows, most=256):
    tile = min(rows, most)
    return [slice(n, n + tile) for n in range(0, rows, tile)]


def norm_rows(scalars, own, got, rest):
    rows, width = own.shape
    tile = rows // 2

    def body(scalars_ref, own_ref, got_ref, rest_ref, normal_ref):
        step = pl.program_id(0)
        far = jnp.where(step - 2 == scalars_ref[1], got_ref[...], rest_ref[...])
        values = jnp.where(step < 2, own_ref[...], far)
        normal_ref[...] = normalized(values.astype(f32))[0]

    block = (tile, width)
    whole = pl.BlockSpec(block, lambda i, scalars: (0, 0))
    return pl.pallas_call(
        body,
        grid_spec=pltpu.PrefetchScalarGridSpec(
            num_scalar_prefetch=1,
            grid=(4,),
            in_specs=[pl.BlockSpec(block, lambda i, scalars: (jnp.minimum(i, 1), 0)), whole, whole],
            out_specs=pl.BlockSpec(block, lambda i, scalars: (i, 0)),
        ),
        out_shape=jax.ShapeDtypeStruct((2 * rows, width), f32),
        compiler_params=pltpu.CompilerParams(vmem_limit_bytes=VMEM),
        cost_estimate=cost(1e8),
        name="norm_rows",
    )(scalars, own, got, rest)


def row_product(parts, b, turned=False, halves=False, swapped=False):
    rows = parts[0].shape[0]
    columns = b.shape[0] if turned else b.shape[1]
    tile = rows // 2

    def body(*refs):
        a_refs, b_ref, outs = refs[: len(parts)], refs[len(parts)], refs[len(parts) + 1 :]
        a = a_refs[0][...] if len(parts) == 1 else jnp.concatenate([ref[...] for ref in a_refs], 1)
        value = (nt if turned else nn)(a, b_ref[...]).astype(bf16)
        if halves:
            core_store(outs, value)
        else:
            for ref in outs:
                ref[...] = value

    row = lambda i: (i, 0)
    block = (tile, columns)
    if halves:
        specs, shapes = [pl.BlockSpec(block, lambda i: (0, 0))] * 2, [block] * 2
    else:
        specs, shapes = [pl.BlockSpec(block, row)], [(rows, columns)]
        if swapped:
            specs.append(pl.BlockSpec(block, lambda i: (1 - i, 0)))
            shapes.append((rows, columns))
    out = pl.pallas_call(
        body,
        grid=(2,),
        in_specs=[pl.BlockSpec((tile, a.shape[1]), row) for a in parts]
        + [pl.BlockSpec(b.shape, lambda i: (0, 0))],
        out_specs=specs,
        out_shape=[jax.ShapeDtypeStruct(shape, bf16) for shape in shapes],
        compiler_params=pltpu.CompilerParams(vmem_limit_bytes=VMEM),
        cost_estimate=cost(1e8),
        name="row_product",
    )(*parts, b)
    return out if len(shapes) > 1 else out[0]


def weight_grads(ring, pairs):
    width = pairs[0][0].shape[1]
    wide = sum(b.shape[1] for _, items in pairs for b in items)
    steps = 4
    tile = width // steps
    shape = (1, width, wide)
    far = far_block(ring, shape)

    def body(*refs):
        refs, (out_ref, *far_refs) = list(refs[:-3]), refs[-3:]
        start = 0
        for _, items in pairs:
            left = refs.pop(0)[...].T
            for item in items:
                stop = start + item.shape[1]
                out_ref[0, :, start:stop] = nn(left, refs.pop(0)[...]).astype(bf16)
                start = stop
        store_far(far, far_refs, tile, out_ref)

    specs, arrays = [], []
    for a, items in pairs:
        specs.append(pl.BlockSpec((a.shape[0], tile), lambda i: (0, i)))
        specs += [pl.BlockSpec(b.shape, lambda i: (0, 0)) for b in items]
        arrays += [a, *items]
    far_specs, far_shapes = far_outputs(far, shape)
    return pl.pallas_call(
        body,
        grid=(steps,),
        in_specs=specs,
        out_specs=[pl.BlockSpec((1, tile, wide), lambda i: (0, i, 0))] + far_specs,
        out_shape=[jax.ShapeDtypeStruct(shape, bf16)] + far_shapes,
        compiler_params=pltpu.CompilerParams(vmem_limit_bytes=VMEM),
        cost_estimate=cost(1e8),
        name="weight_grads",
    )(*arrays)


def add_up(mine, other, kind, name="add_up"):
    def body(mine_ref, other_ref, out_ref):
        out_ref[...] = (mine_ref[...].astype(f32) + other_ref[...].astype(f32)).astype(kind)

    return kernel_call(body, [mine, other], [(mine.shape, kind)], name=name)[0]


def plain_sum(arrays, places, kind):
    rows, width = arrays[0].shape
    count = places.shape[0]
    block = width // count
    tile = 256

    def body(places_ref, *refs):
        *in_refs, out_ref = refs
        items = [ref[...].astype(f32) for ref in in_refs]
        total = items[-2] + items[-1]
        for item in items[:-2]:
            total = item + total
        if block % 128:
            out_ref[...] = total.astype(kind)
            return
        for k in range(count):
            at = pl.ds(pl.multiple_of(places_ref[k] * block, 128), block)
            out_ref[:, at] = total[:, k * block : (k + 1) * block].astype(kind)

    spec = pl.BlockSpec((tile, width), lambda i, places: (i, 0))
    return pl.pallas_call(
        body,
        grid_spec=pltpu.PrefetchScalarGridSpec(
            num_scalar_prefetch=1,
            grid=(rows // tile,),
            in_specs=[spec] * len(arrays),
            out_specs=spec,
        ),
        out_shape=jax.ShapeDtypeStruct((rows, width), kind),
        compiler_params=pltpu.CompilerParams(vmem_limit_bytes=VMEM),
        cost_estimate=cost(1e8),
        name="plain_sum",
    )(places, *arrays)


def keep_sums(kept, taken):
    def body(near_ref, far_ref, near_got, far_got, near_out, far_out):
        near_out[...] = near_ref[...].astype(f32) + near_got[...].astype(f32)
        far_out[...] = (far_ref[...].astype(f32) + far_got[...].astype(f32)).astype(bf16)

    shape = kept[0].shape
    return kernel_call(body, [*kept, *taken], [(shape, f32), (shape, bf16)], name="keep_sums")


def stack_sums(one, two, three, places):
    width = one.shape[1]
    count = places.shape[0]
    block = width // count

    def body(one_ref, two_ref, three_ref, places_ref, out_ref):
        both = [one_ref[...], 0.5 * two_ref[...], 0.5 * three_ref[...], jnp.zeros_like(one_ref)]
        value = jnp.concatenate(both, 0)
        if block % 128:
            out_ref[...] = value
            return
        for k in range(count):
            at = pl.ds(pl.multiple_of(places_ref[k] * block, 128), block)
            out_ref[:, at] = value[:, k * block : (k + 1) * block]

    ins, outs = [one, two, three, places], [((8, width), f32)]
    return kernel_call(body, ins, outs, name="stack_sums", spaces={3: pltpu.SMEM})[0]


def first_project(normal, shards, columns):
    places, pieces = shards
    rows, width = normal.shape
    total = pieces[0].shape[2]
    tile = 256

    def body(normal_ref, *refs):
        pieces, (qkv_ref, low_ref, vectors_ref, w, sems) = refs[: len(places)], refs[len(places) :]

        @pl.when(pl.program_id(0) == 0)
        def _():
            for copy in start_pieces(places, pieces, w, sems):
                copy.wait()
            vectors_ref[...] = w[0, :, columns:].astype(f32).T[:8]

        low = (normal_ref[...] * vectors_ref[0:1, :] + vectors_ref[3:4, :]).astype(bf16)
        low_ref[...] = low
        qkv_ref[...] = nn(low, w[0, :, :columns]).astype(bf16)

    row = lambda i: (i, 0)
    return pl.pallas_call(
        body,
        grid=(rows // tile,),
        in_specs=[pl.BlockSpec((tile, width), row)] + [pl.BlockSpec(memory_space=pltpu.HBM)] * len(pieces),
        out_specs=[
            pl.BlockSpec((tile, columns), row),
            pl.BlockSpec((tile, width), row),
            pl.BlockSpec((8, width), lambda i: (0, 0)),
        ],
        out_shape=[
            jax.ShapeDtypeStruct((rows, columns), bf16),
            jax.ShapeDtypeStruct((rows, width), bf16),
            jax.ShapeDtypeStruct((8, width), f32),
        ],
        scratch_shapes=[
            pltpu.VMEM((1, width, total), bf16),
            pltpu.SemaphoreType.DMA((len(pieces),)),
        ],
        compiler_params=pltpu.CompilerParams(vmem_limit_bytes=VMEM),
        cost_estimate=cost(1e8),
        name="first_project",
    )(normal, *pieces)


def join_pieces(shards, spans):
    places, pieces = shards
    depth = max(row + piece.shape[1] for (row, _), piece in zip(places, pieces))
    widths = [wide for _, wide in spans]

    def plan():
        for (row, col), n in zip(places, range(len(pieces))):
            _, r, c = pieces[n].shape
            for o, (start, wide) in enumerate(spans):
                low, high = max(col, start), min(col + c, start + wide)
                if low < high:
                    yield n, o, row, r, low - col, low - start, high - low

    moves = list(plan())

    def body(*refs):
        ins, outs, sems = refs[: len(pieces)], refs[len(pieces) : -1], refs[-1]
        copies = []
        for m, (n, o, row, r, source, target, wide) in enumerate(moves):
            copies.append(
                pltpu.make_async_copy(
                    ins[n].at[0, :, pl.ds(source, wide)],
                    outs[o].at[pl.ds(row, r), pl.ds(target, wide)],
                    sems.at[m],
                )
            )
            copies[-1].start()
        for copy in copies:
            copy.wait()

    spaces = {n: pltpu.HBM for n in range(len(pieces))}
    outs = [((int(depth), wide), bf16) for wide in widths]
    scratch = [pltpu.SemaphoreType.DMA((len(moves),))]
    return kernel_call(body, pieces, outs, None, scratch, "join_pieces", spaces)


def branch_norm(before, branch, got, vectors, which, weights=None):
    rows, width = before.shape
    half = rows // 2

    def body(before_ref, low_ref, high_ref, low_got, high_got, vectors_ref, *refs):
        if weights is None:
            out_ref, norm_ref = refs
        else:
            w_ref, out_ref, norm_ref, product_ref = refs
        gain, bias = vectors_ref[which : which + 1, :], vectors_ref[3 + which : 4 + which, :]
        for n, (mine, theirs) in enumerate(((low_ref, low_got), (high_ref, high_got))):
            for part in tiles_of(half, 128):
                at = slice(n * half + part.start, n * half + part.stop)
                out = before_ref[at, :].astype(f32) + (
                    mine[part, :].astype(f32) + theirs[part, :].astype(f32)
                )
                out_ref[at, :] = out
                norm_ref[at, :] = (normalized(out)[0] * gain + bias).astype(bf16)
        if weights is not None:
            product_ref[...] = nn(norm_ref[...], w_ref[...]).astype(bf16)

    outs = [((rows, width), f32), ((rows, width), bf16)]
    ins = [before, *branch, *got, vectors]
    if weights is not None:
        ins.append(weights)
        outs.append(((rows, weights.shape[1]), bf16))
    return kernel_call(body, ins, outs, name="branch_norm")


def norm_back(scalars, first, second, split, above, values, vectors, which, weights, pieces):
    rows, width = values.shape
    half = rows // 2
    ins = [*first, *second, above, values, vectors, weights]
    columns = weights.shape[1] // pieces

    def body(scalars_ref, *refs):
        sources, (above_ref, values_ref, vectors_ref, w_ref) = refs[: len(ins) - 4], refs[len(ins) - 4 : len(ins)]
        low_ref, out_ref, sums_ref, *product_refs = refs[len(ins) :]
        gain = vectors_ref[which : which + 1, :]
        core = scalars_ref[1]
        totals = [jnp.zeros((8, width), f32)] * 2

        def tile(grad, at, size):
            normal, factor = normalized(values_ref[at, :].astype(f32))
            out = above_ref[at, :].astype(f32) + norm_backward(grad, normal, factor, gain)
            out_ref[at, :] = out
            low_ref[at, :] = out.astype(bf16)
            eight = lambda item: jnp.sum(item.reshape(size // 8, 8, width), axis=0)
            totals[0] = totals[0] + eight(grad * normal)
            totals[1] = totals[1] + eight(grad)

        for n in range(2):
            for part in tiles_of(half, 128):
                size = part.stop - part.start
                if split:
                    far = core if n == 0 else 1 - core
                    at = pl.ds(pl.multiple_of(far * half + part.start, 128), size)
                    tile(sources[n][part, :].astype(f32), at, size)
                else:
                    at = slice(n * half + part.start, n * half + part.stop)
                    grad = sources[n][part, :].astype(f32) + sources[n + 2][part, :].astype(f32)
                    tile(grad, at, size)
        sums_ref[0:1, :] = jnp.sum(totals[0], axis=0, keepdims=True)
        sums_ref[1:2, :] = jnp.sum(totals[1], axis=0, keepdims=True)
        for n, ref in enumerate(product_refs):
            at = slice(n * columns, (n + 1) * columns)
            ref[...] = nn(low_ref[...], w_ref[:, at]).astype(bf16)

    outs = [((rows, width), bf16), ((rows, width), f32), ((2, width), f32)]
    outs += [((rows, columns), bf16)] * pieces
    return kernel_call(body, ins, outs, scalars, name="norm_back")


def last_norm_back(scalars, first, second, above, values, vectors, places):
    rows, width = values.shape
    count = places.shape[0]
    block = width // count

    def body(scalars_ref, first_ref, second_ref, above_ref, values_ref, vectors_ref, places_ref, out_ref):
        core = scalars_ref[1]
        half = rows // 2
        for ref, far in ((first_ref, core), (second_ref, 1 - core)):
            for part in tiles_of(half, 128):
                size = part.stop - part.start
                at = pl.ds(pl.multiple_of(far * half + part.start, 128), size)
                normal, factor = normalized(values_ref[at, :].astype(f32))
                grad = norm_backward(ref[part, :].astype(f32), normal, factor, vectors_ref[0:1, :])
                out = above_ref[at, :] + grad
                if block % 128:
                    out_ref[at, :] = out
                else:
                    for k in range(count):
                        to = pl.ds(pl.multiple_of(places_ref[k] * block, 128), block)
                        out_ref[at, to] = out[:, k * block : (k + 1) * block]

    ins = [first, second, above, values, vectors, places]
    outs = [((rows, width), f32)]
    return kernel_call(body, ins, outs, scalars, name="last_norm_back", spaces={5: pltpu.SMEM})[0]


def first_partial(scalars, gq, gkv, weights, normal):
    rows, width = normal.shape
    tile = rows // 4

    def body(scalars_ref, gq_ref, gkv_ref, w_ref, normal_ref, *outs):
        grad = nt(jnp.concatenate([gq_ref[...], gkv_ref[...]], 1), w_ref[...])
        *out_refs, sums_ref = outs
        core_store(out_refs, grad.astype(bf16))
        sums = [jnp.sum(grad * normal_ref[...], 0, keepdims=True), jnp.sum(grad, 0, keepdims=True)]
        step = pl.program_id(0)
        for n, item in enumerate(sums):
            sums_ref[n : n + 1, :] = jnp.where(step == 0, item, sums_ref[n : n + 1, :] + item)

    row = lambda i, scalars: (2 * (i % 2) + rows_by_core(scalars, i), 0)
    full = lambda i, scalars: (0, 0)
    out_specs, out_shapes = core_outputs(tile, width)
    return pl.pallas_call(
        body,
        grid_spec=pltpu.PrefetchScalarGridSpec(
            num_scalar_prefetch=1,
            grid=(4,),
            in_specs=[
                pl.BlockSpec((tile, gq.shape[1]), row),
                pl.BlockSpec((tile, gkv.shape[1]), row),
                pl.BlockSpec(weights.shape, full),
                pl.BlockSpec((tile, width), row),
            ],
            out_specs=out_specs + [pl.BlockSpec((2, width), full)],
        ),
        out_shape=out_shapes + [jax.ShapeDtypeStruct((2, width), f32)],
        compiler_params=pltpu.CompilerParams(vmem_limit_bytes=VMEM),
        cost_estimate=cost(1e8),
        name="first_partial",
    )(scalars, gq, gkv, weights, normal)


def first_shards(scalars, self_in, gain, bias):
    count, rows, columns = self_in.shape
    half = columns // 2

    def body(scalars_ref, w_ref, gain_ref, bias_ref, out_ref, table):
        at = pl.ds(pl.multiple_of(scalars_ref[0] * half, 128), half)
        for n in range(count):
            out_ref[0, :, n * half : (n + 1) * half] = w_ref[n, :, at]
        table[...] = jnp.zeros_like(table)
        table[0:3, 0:rows] = gain_ref[...].astype(f32)
        table[3:6, 0:rows] = bias_ref[...].astype(f32)
        out_ref[0, :, count * half :] = table[...].T[0:rows].astype(bf16)

    outs = [((1, rows, count * half + 128), bf16)]
    scratch = [pltpu.VMEM((128, 128), f32)]
    return kernel_call(body, [self_in, gain, bias], outs, scalars, scratch, "first_shards")[0]


def other_shards(scalars, self_out, cross_in, cross_out, ffn_in, ffn_out, chunks):
    _, rows, columns = cross_in.shape
    half = columns // 2
    units = ffn_in.shape[1] // 2 // chunks

    def body(scalars_ref, so_ref, cross_ref, co_ref, in_ref, out_ref, second_ref, *ffn_refs):
        ctx = scalars_ref[0]
        mine = pl.multiple_of(ctx * half, 128)
        theirs = pl.multiple_of((1 - ctx) * half, 128)
        place = 0
        for n in (1, 2):
            second_ref[0, :, place : place + half] = cross_ref[n, :, pl.ds(mine, half)]
            place += half
        for ref in (so_ref, None, co_ref):
            for at in (mine, theirs):
                if ref is None:
                    item = cross_ref[0, :, pl.ds(at, half)]
                else:
                    item = ref[pl.ds(at, half), :].T
                second_ref[0, :, place : place + half] = item
                place += half
        for n in range(chunks):
            at = pl.ds(pl.multiple_of(ctx * (units * chunks) + n * units, 128), units)
            ffn_refs[n][0] = in_ref[:, at]
            ffn_refs[n][1] = out_ref[at, :].T

    outs = [((1, rows, 2 * half + 3 * columns), bf16)] + [((2, rows, units), bf16)] * chunks
    ins = [self_out, cross_in, cross_out, ffn_in, ffn_out]
    return kernel_call(body, ins, outs, scalars, name="other_shards")


def ffn_results(scalars, mine, theirs):
    _, rows, units = mine[0].shape
    chunks = len(mine)

    def body(scalars_ref, *refs):
        in_ref, out_ref = refs[-2:]
        ctx = scalars_ref[0]
        for place, refs_ in ((ctx, refs[:chunks]), (1 - ctx, refs[chunks : 2 * chunks])):
            for n, ref in enumerate(refs_):
                at = pl.ds(pl.multiple_of(place * (units * chunks) + n * units, 128), units)
                in_ref[:, at] = ref[0].astype(f32)
                out_ref[at, :] = ref[1].astype(f32).T

    whole = 2 * chunks * units
    outs = [((rows, whole), f32), ((whole, rows), f32)]
    return kernel_call(body, [*mine, *theirs], outs, scalars, name="ffn_results")


def first_results(scalars, mine, theirs):
    _, rows, columns = mine.shape
    half = columns // 3

    def body(scalars_ref, mine_ref, theirs_ref, out_ref):
        ctx = scalars_ref[0]
        for place, ref in ((ctx, mine_ref), (1 - ctx, theirs_ref)):
            at = pl.ds(pl.multiple_of(place * half, 128), half)
            for n in range(3):
                out_ref[n, :, at] = ref[0, :, n * half : (n + 1) * half].astype(f32)

    return kernel_call(body, [mine, theirs], [((3, rows, 2 * half), f32)], scalars, name="first_results")[0]


def second_results(scalars, mine, theirs, half):
    _, rows, _ = mine.shape

    def body(scalars_ref, mine_ref, theirs_ref, so_ref, cross_ref, co_ref):
        ctx = scalars_ref[0]
        here = pl.multiple_of(ctx * half, 128)
        there = pl.multiple_of((1 - ctx) * half, 128)
        for at, ref in ((here, mine_ref), (there, theirs_ref)):
            for n in range(2):
                cross_ref[n + 1, :, pl.ds(at, half)] = ref[0, :, n * half : (n + 1) * half].astype(f32)
        for n, ref in enumerate((so_ref, None, co_ref)):
            start = 2 * half + 2 * n * half
            for at, a, b in ((here, start, start + half), (there, start + half, start)):
                item = mine_ref[0, :, a : a + half].astype(f32) + theirs_ref[0, :, b : b + half].astype(f32)
                if ref is None:
                    cross_ref[0, :, pl.ds(at, half)] = item
                else:
                    ref[pl.ds(at, half), :] = item.T

    outs = [((2 * half, rows), f32), ((3, rows, 2 * half), f32), ((2 * half, rows), f32)]
    return kernel_call(body, [mine, theirs], outs, scalars, name="second_results")


def move_blocks(arrays, places):
    count = places.shape[0]

    def body(places_ref, *refs):
        half = len(refs) // 2
        for in_ref, out_ref in zip(refs[:half], refs[half:]):
            width = in_ref.shape[1] // count
            for k in range(count):
                start = pl.multiple_of(places_ref[k] * width, width)
                out_ref[:, k * width : (k + 1) * width] = in_ref[:, pl.ds(start, width)]

    return pl.pallas_call(
        body,
        in_specs=[pl.BlockSpec(memory_space=pltpu.SMEM)]
        + [pl.BlockSpec(memory_space=pltpu.VMEM)] * len(arrays),
        out_specs=[pl.BlockSpec(memory_space=pltpu.VMEM)] * len(arrays),
        out_shape=[jax.ShapeDtypeStruct(a.shape, a.dtype) for a in arrays],
        compiler_params=pltpu.CompilerParams(vmem_limit_bytes=VMEM),
        cost_estimate=cost(1e8),
        name="move_blocks",
    )(places, *arrays)


def swap(values, axis):
    return lax.ppermute(values, axis, [(0, 1), (1, 0)])


class Ring:
    def __init__(self, size):
        self.size = size
        self.short = size <= RING_MOST and size % 2 == 0
        half = size // 2
        if self.short:
            self.order = [2 * p if p < half else 2 * (size - 1 - p) + 1 for p in range(size)]
        else:
            self.order = list(range(size))
        position = np.zeros(size, np.int32)
        position[self.order] = np.arange(size)
        there = np.zeros((size, size), np.int32)
        back = np.zeros((size, size), np.int32)
        for device in range(size):
            for k in range(size):
                place = self.order[(position[device] + k) % size] if self.short else k
                there[device, k] = place
                back[device, place] = k
        self.there, self.back = there, back

    def places(self, table):
        return lax.dynamic_index_in_dim(jnp.asarray(table), lax.axis_index("dp"), 0, False)

    def into(self, *arrays):
        return move_blocks(arrays, self.places(self.there)) if self.short else arrays

    def out_of(self, *arrays):
        return move_blocks(arrays, self.places(self.back)) if self.short else arrays

    def send(self, values, step):
        size, order = self.size, self.order
        pairs = [(order[p], order[(p + step) % size]) for p in range(size)]
        return lax.ppermute(values, "dp", pairs)

def far_block(ring, full):
    rows = full[1] // ring.size
    return ring.size // 2 * rows, rows, middle_cut(full[2])


def store_far(far, refs, tile, value, n=slice(None)):
    start, rows, cut = far
    step, at = start // tile, start % tile

    @pl.when(pl.program_id(0) == step)
    def _():
        refs[0][n] = value[..., at : at + rows, :cut]
        refs[1][n] = value[..., at : at + rows, cut:]


def far_outputs(far, full):
    _, rows, cut = far
    shapes = [(full[0], rows, cut), (full[0], rows, full[2] - cut)]
    specs = [pl.BlockSpec(shape, lambda i: (0, 0, 0)) for shape in shapes]
    return specs, [jax.ShapeDtypeStruct(shape, bf16) for shape in shapes]


class Order:
    def __init__(self):
        self.mark = None

    def pin(self, *arrays):
        if self.mark is not None:
            _, arrays = hold((self.mark, arrays))
        return arrays if len(arrays) > 1 else arrays[0]

    def ran(self, result):
        self.mark = result
        return result

    def step(self, run, *arrays):
        if self.mark is not None:
            _, arrays = hold((self.mark, arrays))
        return self.ran(run(*arrays))


def middle_cut(columns):
    return columns // 2 // 128 * 128


class Gather:
    def __init__(self, ring, order, shard):
        self.ring, self.order, self.shard = ring, order, shard
        self.places, self.arrays = [(0, 0)], [shard]
        self.hop = 0
        if not ring.short:
            self.arrays = [lax.all_gather(shard, "dp", axis=1, tiled=True)]

    def advance(self):
        ring, size, rows = self.ring, self.ring.size, self.shard.shape[1]
        if not ring.short or self.hop > size // 2:
            return
        if self.hop == 0:
            self.ahead = self.behind = self.order.pin(self.shard)
        else:
            self.ahead, self.behind = self.order.ran(self.order.pin(self.ahead, self.behind))
            if self.hop < size // 2:
                self.places += [(self.hop * rows, 0), ((size - self.hop) * rows, 0)]
            else:
                cut = middle_cut(self.shard.shape[2])
                self.places += [(size // 2 * rows, 0), (size // 2 * rows, cut)]
            self.arrays += [self.ahead, self.behind]
        self.hop += 1
        if self.hop == size // 2:
            cut = middle_cut(self.shard.shape[2])
            self.ahead, self.behind = self.ahead[..., :cut], self.behind[..., cut:]
        if self.hop <= size // 2:
            self.ahead = ring.send(self.ahead, -1)
            self.behind = ring.send(self.behind, 1)

    def pieces(self):
        return self.places, self.arrays


def ring_add(full, ahead, behind, hop, size):
    count, rows, columns = full.shape
    rows = rows // size
    last = hop == 0
    cut = ahead.shape[2]

    def body(up_ref, down_ref, ahead_ref, behind_ref, *out_refs):
        if last:
            out = up_ref[...].astype(f32) + (ahead_ref[...].astype(f32) + behind_ref[...].astype(f32))
            out_refs[0][...] = out.astype(bf16)
            return
        up_out, down_out = out_refs
        if cut < columns:
            up_out[..., :cut] = (up_ref[..., :cut].astype(f32) + ahead_ref[...].astype(f32)).astype(bf16)
            up_out[..., cut:] = up_ref[..., cut:]
            down_out[..., :cut] = down_ref[..., :cut]
            down_out[..., cut:] = (down_ref[..., cut:].astype(f32) + behind_ref[...].astype(f32)).astype(bf16)
        else:
            up_out[...] = (up_ref[...].astype(f32) + ahead_ref[...].astype(f32)).astype(bf16)
            down_out[...] = (down_ref[...].astype(f32) + behind_ref[...].astype(f32)).astype(bf16)

    block = (1, rows, columns)
    moved = [pl.BlockSpec((1,) + item.shape[1:], lambda i: (i, 0, 0)) for item in (ahead, behind)]
    outs = 1 if last else 2
    return pl.pallas_call(
        body,
        grid=(count,),
        in_specs=[
            pl.BlockSpec(block, lambda i: (i, hop, 0)),
            pl.BlockSpec(block, lambda i: (i, (size - hop) % size, 0)),
            *moved,
        ],
        out_specs=[pl.BlockSpec(block, lambda i: (i, 0, 0))] * outs,
        out_shape=[jax.ShapeDtypeStruct((count, rows, columns), bf16)] * outs,
        compiler_params=pltpu.CompilerParams(vmem_limit_bytes=VMEM),
        cost_estimate=cost(1e8),
        name="ring_add",
    )(full, full, ahead, behind)


class Scatter:
    def __init__(self, ring, order, grads):
        full, self.ahead, self.behind = grads
        self.ring, self.order, self.full, self.hop = ring, order, full, ring.size // 2
        if not ring.short:
            self.result = lax.psum_scatter(full, "dp", scatter_dimension=1, tiled=True)
            self.hop = -1

    def advance(self):
        ring, size = self.ring, self.ring.size
        if self.hop < 0:
            return
        if self.hop == size // 2:
            self.ahead, self.behind = self.order.pin(self.ahead, self.behind)
        else:
            run = functools.partial(ring_add, hop=self.hop, size=size)
            out = self.order.step(run, self.full, self.ahead, self.behind)
            if self.hop == 0:
                self.result, self.hop = out[0], -1
                return
            self.ahead, self.behind = out
        self.hop -= 1
        self.ahead = ring.send(self.ahead, 1)
        self.behind = ring.send(self.behind, -1)


def per_device(
    ring,
    hidden_in,
    encoder_states,
    out_grad,
    target_ids,
    source_ids,
    self_in,
    self_out,
    cross_in,
    cross_out,
    ffn_in,
    ffn_out,
    norm_gain,
    norm_bias,
):
    ctx = lax.axis_index("ctx")
    core = lax.axis_index("tp")
    scalars = jnp.stack([ctx, core]).astype(jnp.int32)
    rows, width = hidden_in.shape
    source_rows = encoder_states.shape[0]
    inner = self_in.shape[2]
    half = inner // 2
    units = ffn_in.shape[1] // 2 // FFN_CHUNKS
    order = Order()

    def part(array, axis, place):
        count = array.shape[axis] // 2
        return lax.dynamic_slice_in_dim(array, place * count, count, axis)

    def ordered(mine, theirs, axis, place=ctx):
        first = place == 0
        return jnp.concatenate(
            [jnp.where(first, mine, theirs), jnp.where(first, theirs, mine)], axis
        )

    def relative(array, axis):
        return jnp.concatenate([part(array, axis, ctx), part(array, axis, 1 - ctx)], axis)

    def core_swap(items):
        return [swap(item, "tp") for item in items]

    def swap_bit(values, bit):
        pairs = [(n, n ^ (1 << bit)) for n in range(ring.size)]
        return lax.ppermute(values, "dp", pairs)

    def make_seen(target_ids, source_ids):
        stride = 2 * max(rows, source_rows)
        lo = relative(target_ids[0], 0) * stride
        code = lo + relative(jnp.arange(2 * rows, dtype=jnp.int32), 0)
        sources = relative(source_ids[0], 0) * stride
        return seen_by(lo, code, code), seen_by(lo[:rows], lo[:rows], sources)

    first = Gather(ring, order, order.ran(first_shards(scalars, self_in, norm_gain, norm_bias)))
    first.advance()
    (hidden_own,) = order.step(ring.into, hidden_in)
    hidden_got = swap(part(hidden_own, 0, core), "ctx")
    first.advance()
    second_shard, ffn_shard = order.step(
        lambda *arrays: other_shards(scalars, *arrays, FFN_CHUNKS),
        self_out,
        cross_in,
        cross_out,
        ffn_in,
        ffn_out,
    )
    second = Gather(ring, order, second_shard)
    ffn = Gather(ring, order, ffn_shard)
    first.advance()
    self_seen, cross_seen = order.step(make_seen, target_ids, source_ids)
    cotangent, states = order.step(ring.into, out_grad, encoder_states)
    hidden_got = order.ran(order.pin(hidden_got))
    hidden_rest = swap(hidden_got, "tp")
    first.advance()
    normal_one = order.step(
        lambda *arrays: norm_rows(scalars, *arrays), hidden_own, hidden_got, hidden_rest
    )
    states_other = swap(order.pin(states), "ctx")
    first.advance()
    second.advance()

    first_places, first_pieces = first.pieces()
    qkv, input_one, vectors = order.step(
        lambda normal, *arrays: first_project(normal, (first_places, arrays), 3 * half),
        normal_one,
        *first_pieces,
    )
    mixed_far, total_far = order.step(
        lambda qkv: attend_forward((qkv, 0), [(qkv, 1)], [(qkv, 2)], self_seen, (rows, rows)), qkv
    )
    mixed_got = swap(mixed_far, "ctx")
    second.advance()
    mixed_near, total_near = order.step(
        lambda qkv: attend_forward((qkv, 0), [(qkv, 1)], [(qkv, 2)], self_seen, (0, rows)), qkv
    )
    second.advance()
    source = order.step(lambda a, b: jnp.concatenate([a, b], 0), states, states_other)
    mixed_got = order.ran(order.pin(mixed_got))
    second.advance()
    (first_w,) = order.step(
        lambda *arrays: join_pieces((first_places, arrays), [(0, 3 * half)]), *first_pieces
    )
    second.advance()
    ffn.advance()
    cotangent_other = swap(order.pin(cotangent), "ctx")
    second_places, pieces = second.pieces()
    spans = [(0, 2 * half), (2 * half, inner)]
    key_w, self_o = order.step(
        lambda *arrays: join_pieces((second_places, arrays), spans), *pieces
    )
    kv, kv_turned = order.step(lambda a, w: row_product([a], w, swapped=True), source, key_w)
    kv_got = swap(kv_turned, "ctx")
    branch = order.step(
        lambda a, b, w: row_product([a, b], w, True, True), mixed_near, mixed_got, self_o
    )
    branch_got = core_swap(branch)

    rest_spans = [(2 * half + inner, inner), (2 * half + 2 * inner, inner)]
    cross_q, cross_o = order.step(
        lambda *arrays: join_pieces((second_places, arrays), rest_spans), *pieces
    )
    first_rows, input_two, cross_queries = order.step(
        lambda before, a, b, c, d, *rest: branch_norm(before, (a, b), (c, d), rest[0], 1, rest[1]),
        hidden_own,
        *branch,
        *branch_got,
        vectors,
        cross_q,
    )
    kv_got = order.ran(order.pin(kv_got))
    ffn.advance()
    cross_keys, cross_values = [(kv, 0), (kv_got, 0)], [(kv, 1), (kv_got, 1)]
    mixed_two, total_two = order.step(
        lambda q: attend_forward((q, 0), cross_keys, cross_values, cross_seen, (0, rows)),
        cross_queries,
    )
    branch = order.step(lambda a, w: row_product([a], w, True, True), mixed_two, cross_o)
    branch_got = core_swap(branch)
    second_rows, input_own = order.step(
        lambda before, a, b, c, d, vectors: branch_norm(before, (a, b), (c, d), vectors, 2),
        first_rows,
        *branch,
        *branch_got,
        vectors,
    )
    input_other = swap(input_own, "ctx")
    ffn.advance()
    input_other = order.ran(order.pin(input_other))
    ffn.advance()
    ffn.advance()
    input_three, out_cot = (input_own, input_other), (cotangent, cotangent_other)

    ffn_places, ffn_pieces = ffn.pieces()
    act, grad_up, *quarters = order.step(
        lambda a, b, c, d, *arrays: ffn_first(scalars, (a, b), (c, d), (ffn_places, arrays)),
        *input_three,
        *out_cot,
        *ffn_pieces,
    )
    taken = core_swap(quarters[:2])
    near, far = order.step(
        lambda a, b, c, d: keep_sums((a, b), (c, d)), *quarters[2:], *taken
    )
    far_got = swap(far, "ctx")
    ffn_scatter = Scatter(
        ring,
        order,
        order.step(
            lambda a, b, c, d, act, gu: ffn_grads(ring, (a, b), (c, d), act, gu),
            *input_three,
            *out_cot,
            act,
            grad_up,
        ),
    )
    ffn_scatter.advance()
    done = order.step(lambda a, b: add_up(a, b, bf16), near, far_got)
    done_got = swap(done, "tp")
    grad_branch_two, grad_second, sums_three, grad_mixed = order.step(
        lambda a, b, *rest: norm_back(scalars, (a,), (b,), True, *rest[:3], 2, rest[3], 1),
        done,
        done_got,
        cotangent,
        second_rows,
        vectors,
        cross_o,
    )

    grad_cq, grad_kv, grad_far_kv = order.step(
        lambda g, q, o: attend_backward(
            [g], (q, 0), cross_keys, cross_values, [o], [total_two], cross_seen
        ),
        grad_mixed,
        cross_queries,
        mixed_two,
    )
    given = swap(grad_far_kv, "ctx")
    ffn_scatter.advance()
    branch = order.step(lambda a, w: row_product([a], w, True, True), grad_cq, cross_q)
    branch_got = core_swap(branch)
    grad_branch, grad_first, sums_two, *grad_mixed = order.step(
        lambda a, b, c, d, *rest: norm_back(
            scalars, (a, b), (c, d), False, *rest[:3], 1, rest[3], 2
        ),
        *branch,
        *branch_got,
        grad_second,
        first_rows,
        vectors,
        self_o,
    )
    mixed_other = swap(grad_mixed[1], "ctx")
    grad_kv = order.step(lambda a, b: add_up(a, b, bf16), grad_kv, given)
    result, result_far = order.step(
        lambda act, *arrays: ffn_output(act, (ffn_places, arrays)), act, *ffn_pieces
    )
    ffn_scatter.advance()
    result_got = swap(result_far, "ctx")
    grad_third = order.step(
        lambda a, b, c, d, e, f, g, h, i: weight_grads(
            ring, [(a, [b]), (c, [d, e]), (f, [g]), (h, [i])]
        ),
        source,
        grad_kv,
        grad_branch,
        mixed_near,
        mixed_got,
        input_two,
        grad_cq,
        grad_branch_two,
        mixed_two,
    )
    second_scatter = Scatter(ring, order, grad_third)
    second_scatter.advance()

    mixed_other = order.ran(order.pin(mixed_other))
    grad_q, grad_self_kv = order.step(
        lambda a, b, qkv: attend_backward(
            [a, b],
            (qkv, 0),
            [(qkv, 1)],
            [(qkv, 2)],
            [mixed_near, mixed_far],
            [total_near, total_far],
            self_seen,
        ),
        grad_mixed[0],
        mixed_other,
        qkv,
    )
    ffn_scatter.advance()
    second_scatter.advance()
    grad_first_w = order.step(
        lambda a, q, kv: weight_grads(ring, [(a, [q, kv])]), input_one, grad_q, grad_self_kv
    )
    first_scatter = Scatter(ring, order, grad_first_w)
    first_scatter.advance()
    *quarters, sums_one = order.step(
        lambda *arrays: first_partial(scalars, *arrays), grad_q, grad_self_kv, first_w, normal_one
    )
    taken = core_swap(quarters[:2])
    near, far = order.step(
        lambda a, b, c, d: keep_sums((a, b), (c, d)), *quarters[2:], *taken
    )
    far_got = swap(far, "ctx")
    ffn_scatter.advance()
    ffn_mine = ffn_scatter.result
    ffn_got = swap(ffn_mine, "ctx")
    sums = order.step(stack_sums, sums_one, sums_two, sums_three, ring.places(ring.there))
    sums_got = swap(sums, "tp")
    source_low, source_far = order.step(
        lambda a, w: row_product([a], w, True, True), grad_kv, key_w
    )
    source_got = swap(source_far, "ctx")
    second_scatter.advance()
    first_scatter.advance()
    result_low = order.step(lambda a, b: add_up(a, b, bf16), result, result_got)
    result_got = swap(result_low, "tp")
    sums = order.step(lambda a, b: add_up(a, b, f32), sums, sums_got)
    sums_got = swap(sums, "ctx")
    done = order.step(lambda a, b: add_up(a, b, bf16), near, far_got)
    done_got = swap(done, "tp")
    source_low = order.step(lambda a, b: add_up(a, b, bf16), source_low, source_got)
    source_got = swap(source_low, "tp")
    second_scatter.advance()
    first_scatter.advance()
    sums = order.step(lambda a, b: add_up(a, b, f32), sums, sums_got)
    far_bit = ring.size.bit_length() - 1
    sums_got = swap_bit(sums, 0)
    back = ring.places(ring.there)
    result = order.step(
        lambda a, b, c: plain_sum([a, b, c], back, bf16), second_rows, result_low, result_got
    )
    grad_input = order.step(
        lambda *arrays: last_norm_back(scalars, *arrays, back),
        done,
        done_got,
        grad_first,
        hidden_own,
        vectors,
    )
    second_scatter.advance()
    second_mine = second_scatter.result
    second_other = swap(second_mine, "ctx")
    first_scatter.advance()
    for bit in range(1, far_bit):
        sums = order.step(lambda a, b: add_up(a, b, f32), sums, sums_got)
        sums_got = swap_bit(sums, bit)
        if bit == 1:
            grad_source = order.step(
                lambda a, b: plain_sum([a, b], back, f32), source_low, source_got
            )
    first_scatter.advance()
    first_mine = first_scatter.result
    first_other = swap(first_mine, "ctx")

    grad_ffn_in, grad_ffn_out = order.step(
        lambda a, b: ffn_results(scalars, [a], [b]), ffn_mine, ffn_got
    )
    grad_self_out, grad_cross_in, grad_cross_out = order.step(
        lambda a, b: second_results(scalars, a, b, half), second_mine, second_other
    )
    grad_self_in = order.step(
        lambda a, b: first_results(scalars, a, b), first_mine, first_other
    )
    sums = order.step(lambda a, b: add_up(a, b, f32), sums, sums_got)
    shard = norm_gain.shape[1]
    sums = lax.dynamic_slice_in_dim(sums, lax.axis_index("dp") * shard, shard, 1)
    return (
        result,
        grad_input,
        grad_source,
        grad_self_in,
        grad_self_out,
        grad_cross_in,
        grad_cross_out,
        grad_ffn_in,
        grad_ffn_out,
        jnp.stack([sums[0], sums[2], sums[4]]),
        jnp.stack([sums[1], sums[3], sums[5]]),
    )


def solution(mesh):
    return jax.shard_map(
        functools.partial(per_device, Ring(mesh.shape["dp"])),
        mesh=mesh,
        in_specs=(
            P(("dp", "ctx"), None),
            P(("dp", "ctx"), None),
            P(("dp", "ctx"), None),
            P("dp", None),
            P("dp", None),
            P(None, "dp", "tp"),
            P("tp", "dp"),
            P(None, "dp", "tp"),
            P("tp", "dp"),
            P("dp", "tp"),
            P("tp", "dp"),
            P(None, "dp"),
            P(None, "dp"),
        ),
        out_specs=(
            P(("dp", "ctx"), None),
            P(("dp", "ctx"), None),
            P(("dp", "ctx"), None),
            P(None, "dp", "tp"),
            P("tp", "dp"),
            P(None, "dp", "tp"),
            P("tp", "dp"),
            P("dp", "tp"),
            P("tp", "dp"),
            P(None, "dp"),
            P(None, "dp"),
        ),
        check_vma=False,
    )
```

```python
import functools

import jax
import jax.numpy as jnp
import numpy as np
from jax import lax
from jax.experimental import pallas as pl
from jax.experimental.pallas import tpu as pltpu
from jax.sharding import PartitionSpec as P

HEAD_DIM = 64
EPSILON = 1e-05
RING_MOST = 8
SCORE_SCALE = HEAD_DIM**-0.5 * 1.4426950408889634
MASKED = -1e30
TILE = 256
QUAD = 256
FFN_TILE = 1024
FFN_STEPS = 4
VMEM = 52 << 20

f32 = jnp.float32
bf16 = jnp.bfloat16
hold = lax.optimization_barrier


def nn(left, right):
    return jnp.dot(left, right, preferred_element_type=f32)


def tn(left, right):
    return lax.dot_general(left, right, (((0,), (0,)), ((), ())), preferred_element_type=f32)


def nt(left, right):
    return lax.dot_general(left, right, (((1,), (1,)), ((), ())), preferred_element_type=f32)


def cost(flops):
    return pl.CostEstimate(flops=int(flops), bytes_accessed=0, transcendentals=0)


def head_stack(values):
    lane = lax.broadcasted_iota(jnp.int32, values.shape, 1) // HEAD_DIM
    return jnp.concatenate(
        [jnp.where(lane == h, values, jnp.zeros_like(values)) for h in range(QUAD // HEAD_DIM)], 0
    )


def attend_forward_kernel(causal, skip, scalars, query_ids, key_ids, q_ref, *refs):
    groups = q_ref.shape[1] // QUAD
    k_refs, v_refs, refs = refs[:groups], refs[groups : 2 * groups], refs[2 * groups :]
    query_row, key_row = refs[:2]
    o_refs, lse_refs = refs[2 : 2 + groups], refs[2 + groups : 2 + 2 * groups]
    s_ref, vt_ref, qs_ref, peak_ref, total_ref, out_ref, codes_ref = refs[-7:]
    step = pl.program_id(0)
    sight = Sight(scalars, (query_ids, query_row), (key_ids, key_row), step + skip, causal)
    lo, hi = sight.bounds()
    tiles = k_refs[0].shape[0] // TILE
    per = QUAD // HEAD_DIM

    @pl.when(step == 0)
    def _():
        for t in range(tiles):
            for g in range(groups):
                span = slice(t * TILE, (t + 1) * TILE)
                vt_ref[g * QUAD : (g + 1) * QUAD, span] = v_refs[g][span, :].T
        sight.turn(codes_ref)

    peak_ref[...] = jnp.full_like(peak_ref, MASKED)
    total_ref[...] = jnp.zeros_like(total_ref)
    out_ref[...] = jnp.zeros_like(out_ref)
    for g in range(groups):
        qs_ref[g] = head_stack(q_ref[:, g * QUAD : (g + 1) * QUAD])
    for t in range(tiles):

        @pl.when(sight.needed(t))
        def _():
            span = slice(t * TILE, (t + 1) * TILE)
            code = codes_ref[span, :]
            allowed = (code >= lo) & (code <= hi)
            for g in range(groups):
                scores = nt(k_refs[g][span, :], qs_ref[g])
                for i in range(per):
                    lanes = slice(i * TILE, (i + 1) * TILE)
                    item = jnp.where(allowed, scores[:, lanes] * SCORE_SCALE, MASKED)
                    s_ref[t, g, :, lanes] = item
                    peak_ref[g : g + 1, lanes] = jnp.maximum(
                        peak_ref[g : g + 1, lanes], jnp.max(item, axis=0, keepdims=True)
                    )

    for t in range(tiles):

        @pl.when(sight.needed(t))
        def _():
            span = slice(t * TILE, (t + 1) * TILE)
            for g in range(groups):
                for i in range(per):
                    lanes = slice(i * TILE, (i + 1) * TILE)
                    h = g * per + i
                    expo = jnp.exp2(s_ref[t, g, :, lanes] - peak_ref[g : g + 1, lanes])
                    total_ref[g : g + 1, lanes] += jnp.sum(expo, axis=0, keepdims=True)
                    out_ref[h] += nn(vt_ref[h * HEAD_DIM : (h + 1) * HEAD_DIM, span], expo.astype(bf16))

    for g in range(groups):
        items = []
        for i in range(per):
            lanes = slice(i * TILE, (i + 1) * TILE)
            h = g * per + i
            total = total_ref[g : g + 1, lanes]
            lse_refs[g][i : i + 1, :] = peak_ref[g : g + 1, lanes] + jnp.log2(total)
            items.append(out_ref[h] * (1.0 / total))
        o_refs[g][...] = jnp.concatenate(items, 0).T.astype(bf16)


def tile_place(tile, count, ctx):
    half = count // TILE // 2
    return (jnp.where(tile < half, ctx, 1 - ctx) * half + tile % half) * TILE


class Sight:
    def __init__(self, scalars, query_ids, key_ids, tile, causal):
        self.ctx, self.causal = scalars[0], causal
        self.query_ids, self.key_ids = query_ids, key_ids
        self.queries, self.keys = query_ids[1].shape[1], key_ids[1].shape[1]
        self.stride = 2 * max(self.queries, self.keys)
        self.at = tile_place(tile, self.queries, self.ctx)

    def codes(self, row, at):
        at = pl.multiple_of(at, TILE)
        code = row[:, pl.ds(at, TILE)] * self.stride
        return code, code + (at + lax.broadcasted_iota(jnp.int32, (1, TILE), 1) if self.causal else 0)

    def bounds(self):
        return self.codes(self.query_ids[1], self.at)

    def turn(self, codes_ref):
        for t in range(self.keys // TILE):
            _, code = self.codes(self.key_ids[1], tile_place(t, self.keys, self.ctx))
            codes_ref[t * TILE : (t + 1) * TILE, :] = jnp.broadcast_to(code, (TILE, TILE)).T

    def needed(self, t):
        place = tile_place(t, self.keys, self.ctx)
        queries, keys = self.query_ids[0], self.key_ids[0]
        seen = (keys[place] <= queries[self.at + TILE - 1]) & (queries[self.at] <= keys[place + TILE - 1])
        return seen & (place <= self.at) if self.causal else seen


def attend_forward(q, keys, values, seen, span):
    scalars, query_ids, key_ids, causal = seen
    groups, stacked = len(keys), QUAD // HEAD_DIM * TILE
    width, depth = groups * QUAD, keys[0][0].shape[0]
    heads = width // HEAD_DIM
    start, count = span
    skip = start // TILE
    return pl.pallas_call(
        functools.partial(attend_forward_kernel, causal, skip),
        grid_spec=pltpu.PrefetchScalarGridSpec(
            num_scalar_prefetch=3,
            grid=(count // TILE,),
            in_specs=[pl.BlockSpec((TILE, width), lambda i, *_: (i + skip, q[1]))]
            + [pl.BlockSpec((depth, QUAD), lambda i, *_, n=n: (0, n)) for _, n in keys + values]
            + [pl.BlockSpec(ids.shape, lambda i, *_: (0, 0)) for ids in (query_ids, key_ids)],
            out_specs=[pl.BlockSpec((TILE, QUAD), lambda i, *_: (i, 0))] * groups
            + [pl.BlockSpec((QUAD // HEAD_DIM, TILE), lambda i, *_: (0, i))] * groups,
            scratch_shapes=[
                pltpu.VMEM((depth // TILE, groups, TILE, stacked), f32),
                pltpu.VMEM((width, depth), bf16),
                pltpu.VMEM((groups, stacked, QUAD), bf16),
                pltpu.VMEM((groups, stacked), f32),
                pltpu.VMEM((groups, stacked), f32),
                pltpu.VMEM((heads, HEAD_DIM, TILE), f32),
                pltpu.VMEM((depth, TILE), jnp.int32),
            ],
        ),
        out_shape=[jax.ShapeDtypeStruct((count, QUAD), bf16)] * groups
        + [jax.ShapeDtypeStruct((QUAD // HEAD_DIM, count), f32)] * groups,
        compiler_params=pltpu.CompilerParams(vmem_limit_bytes=VMEM),
        cost_estimate=cost(1e8),
        name="attend_forward",
    )(scalars, query_ids[0], key_ids[0], q[0], *[item for item, _ in keys + values], query_ids, key_ids)


def attend_backward_kernel(parts, turn, causal, scalars, query_ids, key_ids, q_ref, *refs):
    groups = q_ref.shape[1] // QUAD
    k_refs, v_refs, refs = refs[:groups], refs[groups : 2 * groups], refs[2 * groups :]
    rows = []
    for _ in range(3):
        rows.append(refs[:parts])
        refs = refs[parts:]
    query_row, key_row, gq_ref, *refs = refs
    gkv_refs, refs = refs[:groups], refs[groups:]
    gk_acc, gv_acc, gq_acc, qs_ref, gs_ref, inner_ref, lse_ref, p_ref, ds_ref, dst_ref, codes_ref = refs
    step = pl.program_id(0)
    sight = Sight(scalars, (query_ids, query_row), (key_ids, key_row), step, causal)
    lo, hi = sight.bounds()
    width = q_ref.shape[1]
    depth = k_refs[0].shape[0]
    tiles = depth // TILE
    per = QUAD // HEAD_DIM
    heads = width // HEAD_DIM

    @pl.when(step == 0)
    def _():
        gk_acc[...] = jnp.zeros_like(gk_acc)
        gv_acc[...] = jnp.zeros_like(gv_acc)
        sight.turn(codes_ref)

    def chosen(items):
        if len(items) == 1:
            return items[0][...]
        return jnp.where(step < pl.num_programs(0) // 2, items[0][...], items[1][...])

    gq_acc[...] = jnp.zeros_like(gq_acc)
    grad, out = chosen(rows[0]), chosen(rows[1])
    lse_ref[...] = chosen(rows[2])
    both = grad.astype(f32) * out.astype(f32)
    pick = lax.broadcasted_iota(jnp.int32, (heads, width), 0) == (
        lax.broadcasted_iota(jnp.int32, (heads, width), 1) // HEAD_DIM
    )
    inner_ref[...] = lax.dot_general(
        pick.astype(f32),
        both,
        (((1,), (1,)), ((), ())),
        precision=lax.Precision.HIGHEST,
        preferred_element_type=f32,
    )
    for g in range(groups):
        lanes = slice(g * QUAD, (g + 1) * QUAD)
        qs_ref[g] = head_stack(q_ref[:, lanes])
        gs_ref[g] = head_stack(grad[:, lanes])
    for t in range(tiles):

        @pl.when(sight.needed(t))
        def _():
            span = slice(t * TILE, (t + 1) * TILE)
            code = codes_ref[span, :]
            allowed = (code >= lo) & (code <= hi)
            for g in range(groups):
                lanes = slice(g * QUAD, (g + 1) * QUAD)
                scores = nt(k_refs[g][span, :], qs_ref[g])
                grads = nt(v_refs[g][span, :], gs_ref[g])
                for i in range(per):
                    at = slice(i * TILE, (i + 1) * TILE)
                    h = g * per + i
                    item = jnp.where(allowed, scores[:, at] * SCORE_SCALE, MASKED)
                    probs = jnp.exp2(item - lse_ref[h : h + 1, :])
                    p_ref[:, at] = probs.astype(bf16)
                    grad = (probs * (grads[:, at] - inner_ref[h : h + 1, :])).astype(bf16)
                    ds_ref[:, at] = grad
                    dst_ref[:, at] = grad.T
                gv_acc[span, lanes] += nn(p_ref[...], gs_ref[g])
                gk_acc[span, lanes] += nn(ds_ref[...], qs_ref[g])
                gq_acc[:, lanes] += nn(dst_ref[...], head_stack(k_refs[g][span, :]))

    gq_ref[...] = (gq_acc[...] * HEAD_DIM**-0.5).astype(bf16)

    @pl.when(step == pl.num_programs(0) - 1)
    def _():
        half = depth // 2
        for g, ref in enumerate(gkv_refs):
            lanes = slice(g * QUAD, (g + 1) * QUAD)
            for here in (slice(0, half), slice(half, depth)):
                there = slice(half - here.start, depth - here.start) if turn else here
                ref[there, :QUAD] = (gk_acc[here, lanes] * HEAD_DIM**-0.5).astype(bf16)
                ref[there, QUAD:] = gv_acc[here, lanes].astype(bf16)


def attend_backward(g, q, keys, values, o, lse, seen, turn=False):
    scalars, query_ids, key_ids, causal = seen
    groups, stacked = len(keys), QUAD // HEAD_DIM * TILE
    width, depth = groups * QUAD, keys[0][0].shape[0]
    rows, heads, parts = q[0].shape[0], width // HEAD_DIM, len(g)
    each = rows // TILE // parts
    row = lambda i, *_: (i, 0)
    full = lambda i, *_: (0, 0)
    places = [lambda i: jnp.clip(i, 0, each - 1), lambda i: jnp.clip(i - each, 0, each - 1)][:parts]
    tall = [pl.BlockSpec((TILE, width), lambda i, *_, at=at: (at(i), 0)) for at in places]
    flat = [pl.BlockSpec((heads, TILE), lambda i, *_, at=at: (0, at(i))) for at in places]
    return pl.pallas_call(
        functools.partial(attend_backward_kernel, parts, turn, causal),
        grid_spec=pltpu.PrefetchScalarGridSpec(
            num_scalar_prefetch=3,
            grid=(rows // TILE,),
            in_specs=[pl.BlockSpec((TILE, width), lambda i, *_: (i, q[1]))]
            + [pl.BlockSpec((depth, QUAD), lambda i, *_, n=n: (0, n)) for _, n in keys + values]
            + tall
            + tall
            + flat
            + [pl.BlockSpec(ids.shape, full) for ids in (query_ids, key_ids)],
            out_specs=[pl.BlockSpec((TILE, width), row)]
            + [pl.BlockSpec((depth, 2 * QUAD), full)] * groups,
            scratch_shapes=[
                pltpu.VMEM((depth, width), f32),
                pltpu.VMEM((depth, width), f32),
                pltpu.VMEM((TILE, width), f32),
                pltpu.VMEM((groups, stacked, QUAD), bf16),
                pltpu.VMEM((groups, stacked, QUAD), bf16),
                pltpu.VMEM((heads, TILE), f32),
                pltpu.VMEM((heads, TILE), f32),
                pltpu.VMEM((TILE, stacked), bf16),
                pltpu.VMEM((TILE, stacked), bf16),
                pltpu.VMEM((TILE, stacked), bf16),
                pltpu.VMEM((depth, TILE), jnp.int32),
            ],
        ),
        out_shape=[jax.ShapeDtypeStruct((rows, width), bf16)]
        + [jax.ShapeDtypeStruct((depth, 2 * QUAD), bf16)] * groups,
        compiler_params=pltpu.CompilerParams(vmem_limit_bytes=VMEM),
        cost_estimate=cost(1e8),
        name="attend_backward",
    )(scalars, query_ids[0], key_ids[0], q[0], *[item for item, _ in keys + values], *g, *o, *lse, query_ids, key_ids)


def gelu_pair(u):
    c = 0.7978845608028654
    square = u * u
    t = jnp.tanh(u * (c + (c * 0.044715) * square))
    half = 0.5 + 0.5 * t
    slope = half + 0.5 * u * (1.0 - t * t) * (c + (3 * c * 0.044715) * square)
    return u * half, slope


def start_pieces(places, refs, scratch, sems, which=slice(None)):
    copies = []
    for n, ((row, col), ref) in enumerate(zip(places, refs)):
        _, r, c = ref.shape
        target = scratch.at[:, pl.ds(row, r), pl.ds(col, c)]
        copies.append(pltpu.make_async_copy(ref.at[which], target, sems.at[n]))
        copies[-1].start()
    return copies


def rows_by_core(scalars, step):
    return jnp.where(step < 2, 1 - scalars[1], scalars[1])


def core_outputs(tile, width):
    specs = [pl.BlockSpec((tile, width), lambda i, scalars: (0, 0))] * 4
    return specs, [jax.ShapeDtypeStruct((tile, width), bf16)] * 4


def core_store(refs, value):
    for n, ref in enumerate(refs):

        @pl.when(pl.program_id(0) == n)
        def _():
            ref[...] = value


def ffn_first(scalars, a, g, shards):
    places, arrays = shards
    rows, width = a[0].shape
    cols = max(col + piece.shape[2] for (_, col), piece in zip(places, arrays))
    tile = rows // 2
    chunk = min(FFN_TILE, cols)
    count = len(arrays)

    def body(scalars_ref, a_ref, far_a_ref, g_ref, far_g_ref, *refs):
        pieces, (act_ref, gu_ref, *gn_refs), (w, sems) = refs[:count], refs[count:-2], refs[-2:]
        step = pl.program_id(0)

        @pl.when(step == 0)
        def _():
            copies = [
                start_pieces(places, pieces, w.at[n : n + 1], sems.at[n], slice(n, n + 1))
                for n in range(2)
            ]
            for copy in copies[0] + copies[1]:
                copy.wait()

        near = step % 2 == 0
        a, g = jnp.where(near, a_ref[...], far_a_ref[...]), jnp.where(near, g_ref[...], far_g_ref[...])
        total = jnp.zeros((tile, width), f32)
        for j in range(cols // chunk):
            span = slice(j * chunk, (j + 1) * chunk)
            act, slope = gelu_pair(nn(a, w[0, :, span]))
            act_ref[:, span] = act.astype(bf16)
            gu = (nn(g, w[1, :, span]) * slope).astype(bf16)
            gu_ref[:, span] = gu
            total = total + nt(gu, w[0, :, span])
        core_store(gn_refs, total.astype(bf16))

    block = pl.BlockSpec((tile, width), lambda i, scalars: (rows_by_core(scalars, i), 0))
    narrow = pl.BlockSpec((tile, cols), lambda i, scalars: (2 * (i % 2) + rows_by_core(scalars, i), 0))
    out_specs, out_shapes = core_outputs(tile, width)
    return pl.pallas_call(
        body,
        grid_spec=pltpu.PrefetchScalarGridSpec(
            num_scalar_prefetch=1,
            grid=(4,),
            in_specs=[block] * 4 + [pl.BlockSpec(memory_space=pltpu.HBM)] * count,
            out_specs=[narrow, narrow] + out_specs,
            scratch_shapes=[
                pltpu.VMEM((2, width, cols), bf16),
                pltpu.SemaphoreType.DMA((2, count)),
            ],
        ),
        out_shape=[jax.ShapeDtypeStruct((2 * rows, cols), bf16)] * 2 + out_shapes,
        compiler_params=pltpu.CompilerParams(vmem_limit_bytes=VMEM),
        cost_estimate=cost(1e8),
        name="ffn_first",
    )(scalars, *a, *g, *arrays)


def ffn_grads(ring, a, g, act, gu):
    rows, width = a[0].shape
    cols = act.shape[1]
    steps = FFN_STEPS
    tile = width // steps
    shape = (2, width, cols)
    far = far_block(ring, shape)

    def body(a_ref, far_a_ref, g_ref, far_g_ref, act_ref, gu_ref, dw_ref, *far_refs):
        for n, (near, other, right) in enumerate(
            ((a_ref, far_a_ref, gu_ref), (g_ref, far_g_ref, act_ref))
        ):
            left = jnp.concatenate([near[...].T, other[...].T], 1)
            grad = nn(left, right[...]).astype(bf16)
            dw_ref[n] = grad
            store_far(far, far_refs, tile, grad, n)

    full = pl.BlockSpec((2 * rows, cols), lambda i: (0, 0))
    wide = pl.BlockSpec((rows, tile), lambda i: (0, i))
    far_specs, far_shapes = far_outputs(far, shape)
    return pl.pallas_call(
        body,
        grid=(steps,),
        in_specs=[wide] * 4 + [full, full],
        out_specs=[pl.BlockSpec((2, tile, cols), lambda i: (0, i, 0))] + far_specs,
        out_shape=[jax.ShapeDtypeStruct(shape, bf16)] + far_shapes,
        compiler_params=pltpu.CompilerParams(vmem_limit_bytes=VMEM),
        cost_estimate=cost(1e8),
        name="ffn_grads",
    )(*a, *g, act, gu)


def ffn_output(scalars, act, shards):
    places, arrays = shards
    rows, cols = act.shape
    width = max(row + piece.shape[1] for (row, _), piece in zip(places, arrays))
    tile = rows // 4

    def body(scalars_ref, act_ref, *refs):
        pieces, out_refs, (w, sems) = refs[: len(places)], refs[len(places) : -2], refs[-2:]

        @pl.when(pl.program_id(0) == 0)
        def _():
            for copy in start_pieces(places, pieces, w, sems, slice(1, 2)):
                copy.wait()

        core_store(out_refs, nt(act_ref[...], w[0]).astype(bf16))

    out_specs, out_shapes = core_outputs(tile, width)
    return pl.pallas_call(
        body,
        grid_spec=pltpu.PrefetchScalarGridSpec(
            num_scalar_prefetch=1,
            grid=(4,),
            in_specs=[
                pl.BlockSpec((tile, cols), lambda i, scalars: (2 * (i % 2) + rows_by_core(scalars, i), 0))
            ]
            + [pl.BlockSpec(memory_space=pltpu.HBM)] * len(arrays),
            out_specs=out_specs,
            scratch_shapes=[
                pltpu.VMEM((1, width, cols), bf16),
                pltpu.SemaphoreType.DMA((len(arrays),)),
            ],
        ),
        out_shape=out_shapes,
        compiler_params=pltpu.CompilerParams(vmem_limit_bytes=VMEM),
        cost_estimate=cost(1e8),
        name="ffn_output",
    )(scalars, act, *arrays)


def normalized(values):
    centre = jnp.mean(values, axis=-1, keepdims=True)
    centred = values - centre
    factor = lax.rsqrt(jnp.mean(centred * centred, axis=-1, keepdims=True) + EPSILON)
    return centred * factor, factor


def norm_backward(grad_norm, normal, factor, gain):
    scaled = grad_norm * gain
    inner = (
        scaled
        - jnp.mean(scaled, axis=-1, keepdims=True)
        - normal * jnp.mean(scaled * normal, axis=-1, keepdims=True)
    )
    return factor * inner


def kernel_call(body, ins, outs, scalars=None, scratch=(), name=None, spaces=None):
    spaces = spaces or {}
    specs = [pl.BlockSpec(memory_space=spaces.get(n, pltpu.VMEM)) for n in range(len(ins))]
    out_specs = [pl.BlockSpec(memory_space=spaces.get(("out", n), pltpu.VMEM)) for n in range(len(outs))]
    if scalars is not None:
        specs = [pl.BlockSpec(memory_space=pltpu.SMEM)] + specs
        ins = [scalars] + list(ins)
    return pl.pallas_call(
        body,
        in_specs=specs,
        out_specs=out_specs,
        out_shape=[jax.ShapeDtypeStruct(*out) for out in outs],
        scratch_shapes=list(scratch),
        compiler_params=pltpu.CompilerParams(vmem_limit_bytes=VMEM),
        cost_estimate=cost(1e8),
        name=name,
    )(*ins)


def tiles_of(rows, most=256):
    tile = min(rows, most)
    return [slice(n, n + tile) for n in range(0, rows, tile)]


def norm_rows(scalars, own, got, rest):
    rows, width = own.shape
    tile = rows // 2

    def body(scalars_ref, own_ref, got_ref, rest_ref, normal_ref):
        step = pl.program_id(0)
        far = jnp.where(step - 2 == scalars_ref[1], got_ref[...], rest_ref[...])
        values = jnp.where(step < 2, own_ref[...], far)
        normal_ref[...] = normalized(values.astype(f32))[0]

    block = (tile, width)
    whole = pl.BlockSpec(block, lambda i, scalars: (0, 0))
    return pl.pallas_call(
        body,
        grid_spec=pltpu.PrefetchScalarGridSpec(
            num_scalar_prefetch=1,
            grid=(4,),
            in_specs=[pl.BlockSpec(block, lambda i, scalars: (jnp.minimum(i, 1), 0)), whole, whole],
            out_specs=pl.BlockSpec(block, lambda i, scalars: (i, 0)),
        ),
        out_shape=jax.ShapeDtypeStruct((2 * rows, width), f32),
        compiler_params=pltpu.CompilerParams(vmem_limit_bytes=VMEM),
        cost_estimate=cost(1e8),
        name="norm_rows",
    )(scalars, own, got, rest)


def row_product(parts, b, turned=False, halves=False, swapped=False):
    rows = parts[0].shape[0]
    columns = b.shape[0] if turned else b.shape[1]
    tile = rows // 2

    def body(*refs):
        a_refs, b_ref, outs = refs[: len(parts)], refs[len(parts)], refs[len(parts) + 1 :]
        a = a_refs[0][...] if len(parts) == 1 else jnp.concatenate([ref[...] for ref in a_refs], 1)
        value = (nt if turned else nn)(a, b_ref[...]).astype(bf16)
        if halves:
            core_store(outs, value)
        else:
            for ref in outs:
                ref[...] = value

    row = lambda i: (i, 0)
    block = (tile, columns)
    if halves:
        specs, shapes = [pl.BlockSpec(block, lambda i: (0, 0))] * 2, [block] * 2
    else:
        specs, shapes = [pl.BlockSpec(block, row)], [(rows, columns)]
        if swapped:
            specs.append(pl.BlockSpec(block, lambda i: (1 - i, 0)))
            shapes.append((rows, columns))
    out = pl.pallas_call(
        body,
        grid=(2,),
        in_specs=[pl.BlockSpec((tile, a.shape[1]), row) for a in parts]
        + [pl.BlockSpec(b.shape, lambda i: (0, 0))],
        out_specs=specs,
        out_shape=[jax.ShapeDtypeStruct(shape, bf16) for shape in shapes],
        compiler_params=pltpu.CompilerParams(vmem_limit_bytes=VMEM),
        cost_estimate=cost(1e8),
        name="row_product",
    )(*parts, b)
    return out if len(shapes) > 1 else out[0]


def weight_grads(ring, pairs, extra=()):
    width = pairs[0][0].shape[1]
    wide = sum(b.shape[1] for _, items in pairs for b in items) + sum(item.shape[1] for item in extra)
    steps = 4
    tile = width // steps
    shape = (1, width, wide)
    far = far_block(ring, shape)

    def body(*refs):
        refs, (out_ref, *far_refs) = list(refs[:-3]), refs[-3:]
        start = 0
        for _, items in pairs:
            left = refs.pop(0)[...].T
            for item in items:
                stop = start + item.shape[1]
                out_ref[0, :, start:stop] = nn(left, refs.pop(0)[...]).astype(bf16)
                start = stop
        for ref in refs:
            out_ref[0, :, start:] = ref[...]
        store_far(far, far_refs, tile, out_ref)

    specs, arrays = [], []
    for a, items in pairs:
        specs.append(pl.BlockSpec((a.shape[0], tile), lambda i: (0, i)))
        specs += [pl.BlockSpec(b.shape, lambda i: (0, 0)) for b in items]
        arrays += [a, *items]
    specs += [pl.BlockSpec((tile, item.shape[1]), lambda i: (i, 0)) for item in extra]
    arrays += extra
    far_specs, far_shapes = far_outputs(far, shape)
    return pl.pallas_call(
        body,
        grid=(steps,),
        in_specs=specs,
        out_specs=[pl.BlockSpec((1, tile, wide), lambda i: (0, i, 0))] + far_specs,
        out_shape=[jax.ShapeDtypeStruct(shape, bf16)] + far_shapes,
        compiler_params=pltpu.CompilerParams(vmem_limit_bytes=VMEM),
        cost_estimate=cost(1e8),
        name="weight_grads",
    )(*arrays)


def add_up(mine, other, kind, name="add_up"):
    def body(mine_ref, other_ref, out_ref):
        out_ref[...] = (mine_ref[...].astype(f32) + other_ref[...].astype(f32)).astype(kind)

    return kernel_call(body, [mine, other], [(mine.shape, kind)], name=name)[0]


def plain_sum(arrays, places, kind):
    rows, width = arrays[0].shape
    count = places.shape[0]
    block = width // count
    tile = 256

    def body(places_ref, *refs):
        *in_refs, out_ref = refs
        items = [ref[...].astype(f32) for ref in in_refs]
        total = items[-2] + items[-1]
        for item in items[:-2]:
            total = item + total
        if block % 128:
            out_ref[...] = total.astype(kind)
            return
        for k in range(count):
            at = pl.ds(pl.multiple_of(places_ref[k] * block, 128), block)
            out_ref[:, at] = total[:, k * block : (k + 1) * block].astype(kind)

    spec = pl.BlockSpec((tile, width), lambda i, places: (i, 0))
    return pl.pallas_call(
        body,
        grid_spec=pltpu.PrefetchScalarGridSpec(
            num_scalar_prefetch=1,
            grid=(rows // tile,),
            in_specs=[spec] * len(arrays),
            out_specs=spec,
        ),
        out_shape=jax.ShapeDtypeStruct((rows, width), kind),
        compiler_params=pltpu.CompilerParams(vmem_limit_bytes=VMEM),
        cost_estimate=cost(1e8),
        name="plain_sum",
    )(places, *arrays)


def core_sum(scalars, base, mine, got, places, kind):
    rows, width = base.shape
    count = places.shape[0]
    block = width // count
    tile = rows // 2

    def body(scalars_ref, places_ref, base_ref, mine_ref, got_ref, out_ref):
        own = pl.program_id(0) == scalars_ref[1]
        total = base_ref[...] + jnp.where(own, mine_ref[...], got_ref[...]).astype(f32)
        if block % 128:
            out_ref[...] = total.astype(kind)
            return
        for k in range(count):
            at = pl.ds(pl.multiple_of(places_ref[k] * block, 128), block)
            out_ref[:, at] = total[:, k * block : (k + 1) * block].astype(kind)

    spec = pl.BlockSpec((tile, width), lambda i, *_: (i, 0))
    whole = pl.BlockSpec((tile, width), lambda i, *_: (0, 0))
    return pl.pallas_call(
        body,
        grid_spec=pltpu.PrefetchScalarGridSpec(
            num_scalar_prefetch=2,
            grid=(2,),
            in_specs=[spec, whole, whole],
            out_specs=spec,
        ),
        out_shape=jax.ShapeDtypeStruct((rows, width), kind),
        compiler_params=pltpu.CompilerParams(vmem_limit_bytes=VMEM),
        cost_estimate=cost(1e8),
        name="core_sum",
    )(scalars, places, base, mine, got)


def keep_sums(kept, taken):
    def body(near_ref, far_ref, near_got, far_got, near_out, far_out):
        near_out[...] = near_ref[...].astype(f32) + near_got[...].astype(f32)
        far_out[...] = (far_ref[...].astype(f32) + far_got[...].astype(f32)).astype(bf16)

    shape = kept[0].shape
    return kernel_call(body, [*kept, *taken], [(shape, f32), (shape, bf16)], name="keep_sums")


def sum_columns(one, other, two, three):
    width = one.shape[1]

    def body(one_ref, other_ref, two_ref, three_ref, out_ref, table):
        table[...] = jnp.zeros_like(table)
        table[0:2, :] = one_ref[...] + other_ref[...]
        table[2:4, :] = two_ref[...]
        table[4:6, :] = three_ref[...]
        out_ref[...] = table[...].T.astype(bf16)

    scratch = [pltpu.VMEM((128, width), f32)]
    ins = [one, other, two, three]
    return kernel_call(body, ins, [((width, 128), bf16)], None, scratch, "sum_columns")[0]


def first_project(normal, shards, columns):
    places, pieces = shards
    rows, width = normal.shape
    total = pieces[0].shape[2]
    tile = 256

    def body(normal_ref, *refs):
        pieces, (qkv_ref, low_ref, vectors_ref, w, sems) = refs[: len(places)], refs[len(places) :]

        @pl.when(pl.program_id(0) == 0)
        def _():
            for copy in start_pieces(places, pieces, w, sems):
                copy.wait()
            vectors_ref[...] = w[0, :, columns:].astype(f32).T[:8]

        low = (normal_ref[...] * vectors_ref[0:1, :] + vectors_ref[3:4, :]).astype(bf16)
        low_ref[...] = low
        qkv_ref[...] = nn(low, w[0, :, :columns]).astype(bf16)

    row = lambda i: (i, 0)
    return pl.pallas_call(
        body,
        grid=(rows // tile,),
        in_specs=[pl.BlockSpec((tile, width), row)] + [pl.BlockSpec(memory_space=pltpu.HBM)] * len(pieces),
        out_specs=[
            pl.BlockSpec((tile, columns), row),
            pl.BlockSpec((tile, width), row),
            pl.BlockSpec((8, width), lambda i: (0, 0)),
        ],
        out_shape=[
            jax.ShapeDtypeStruct((rows, columns), bf16),
            jax.ShapeDtypeStruct((rows, width), bf16),
            jax.ShapeDtypeStruct((8, width), f32),
        ],
        scratch_shapes=[
            pltpu.VMEM((1, width, total), bf16),
            pltpu.SemaphoreType.DMA((len(pieces),)),
        ],
        compiler_params=pltpu.CompilerParams(vmem_limit_bytes=VMEM),
        cost_estimate=cost(1e8),
        name="first_project",
    )(normal, *pieces)


def join_pieces(shards, spans):
    places, pieces = shards
    depth = max(row + piece.shape[1] for (row, _), piece in zip(places, pieces))
    widths = [wide for _, wide in spans]

    def plan():
        for (row, col), n in zip(places, range(len(pieces))):
            _, r, c = pieces[n].shape
            for o, (start, wide) in enumerate(spans):
                low, high = max(col, start), min(col + c, start + wide)
                if low < high:
                    yield n, o, row, r, low - col, low - start, high - low

    moves = list(plan())

    def body(*refs):
        ins, outs, sems = refs[: len(pieces)], refs[len(pieces) : -1], refs[-1]
        copies = []
        for m, (n, o, row, r, source, target, wide) in enumerate(moves):
            copies.append(
                pltpu.make_async_copy(
                    ins[n].at[0, :, pl.ds(source, wide)],
                    outs[o].at[pl.ds(row, r), pl.ds(target, wide)],
                    sems.at[m],
                )
            )
            copies[-1].start()
        for copy in copies:
            copy.wait()

    spaces = {n: pltpu.HBM for n in range(len(pieces))}
    outs = [((int(depth), wide), bf16) for wide in widths]
    scratch = [pltpu.SemaphoreType.DMA((len(moves),))]
    return kernel_call(body, pieces, outs, None, scratch, "join_pieces", spaces)


def branch_norm(before, branch, got, vectors, which, weights=None):
    rows, width = before.shape
    half = rows // 2
    more = [] if weights is None else [weights]

    def body(before_ref, low_ref, high_ref, low_got, high_got, vectors_ref, *refs):
        out_ref, norm_ref = refs[len(more) : len(more) + 2]
        gain, bias = vectors_ref[which : which + 1, :], vectors_ref[3 + which : 4 + which, :]
        first = pl.program_id(0) == 0
        for part in tiles_of(half, 128):
            mine = jnp.where(first, low_ref[part, :], high_ref[part, :]).astype(f32)
            theirs = jnp.where(first, low_got[part, :], high_got[part, :]).astype(f32)
            out = before_ref[part, :].astype(f32) + (mine + theirs)
            out_ref[part, :] = out
            norm_ref[part, :] = (normalized(out)[0] * gain + bias).astype(bf16)
        if more:
            refs[-1][...] = nn(norm_ref[...], refs[0][...]).astype(bf16)

    row = lambda i: (i, 0)
    full = lambda i: (0, 0)
    block = pl.BlockSpec((half, width), row)
    whole = pl.BlockSpec((half, width), full)
    out_specs = [block, block] + [pl.BlockSpec((half, w.shape[1]), row) for w in more]
    shapes = [((rows, width), f32), ((rows, width), bf16)] + [((rows, w.shape[1]), bf16) for w in more]
    return pl.pallas_call(
        body,
        grid=(2,),
        in_specs=[block]
        + [whole] * 4
        + [pl.BlockSpec(vectors.shape, full)]
        + [pl.BlockSpec(w.shape, full) for w in more],
        out_specs=out_specs,
        out_shape=[jax.ShapeDtypeStruct(*shape) for shape in shapes],
        compiler_params=pltpu.CompilerParams(vmem_limit_bytes=VMEM),
        cost_estimate=cost(1e8),
        name="branch_norm",
    )(before, *branch, *got, vectors, *more)


def norm_back(scalars, first, second, split, above, values, vectors, which, weights, pieces):
    rows, width = values.shape
    half = rows // 2
    sources = [*first, *second]
    columns = weights.shape[1] // pieces

    def body(scalars_ref, *refs):
        source_refs, refs = refs[: len(sources)], refs[len(sources) :]
        above_ref, values_ref, vectors_ref, w_ref, low_ref, out_ref, sums_ref, *product_refs = refs
        gain = vectors_ref[which : which + 1, :]
        start = pl.program_id(0) == 0
        totals = [jnp.zeros((8, width), f32)] * 2
        for part in tiles_of(half, 128):
            size = part.stop - part.start
            grad = jnp.where(start, source_refs[0][part, :], source_refs[1][part, :]).astype(f32)
            if not split:
                other = jnp.where(start, source_refs[2][part, :], source_refs[3][part, :])
                grad = grad + other.astype(f32)
            normal, factor = normalized(values_ref[part, :].astype(f32))
            out = above_ref[part, :].astype(f32) + norm_backward(grad, normal, factor, gain)
            out_ref[part, :] = out
            low_ref[part, :] = out.astype(bf16)
            eight = lambda item: jnp.sum(item.reshape(size // 8, 8, width), axis=0)
            totals[0] = totals[0] + eight(grad * normal)
            totals[1] = totals[1] + eight(grad)
        for n in range(2):
            total = jnp.sum(totals[n], axis=0, keepdims=True)
            sums_ref[n : n + 1, :] = jnp.where(start, total, sums_ref[n : n + 1, :] + total)
        for n, ref in enumerate(product_refs):
            at = slice(n * columns, (n + 1) * columns)
            ref[...] = nn(low_ref[...], w_ref[:, at]).astype(bf16)

    place = lambda i, scalars: (jnp.where(i == 0, scalars[1], 1 - scalars[1]) if split else i, 0)
    full = lambda i, scalars: (0, 0)
    block = pl.BlockSpec((half, width), place)
    return pl.pallas_call(
        body,
        grid_spec=pltpu.PrefetchScalarGridSpec(
            num_scalar_prefetch=1,
            grid=(2,),
            in_specs=[pl.BlockSpec((half, width), full)] * len(sources)
            + [block, block, pl.BlockSpec(vectors.shape, full), pl.BlockSpec(weights.shape, full)],
            out_specs=[block, block, pl.BlockSpec((2, width), full)]
            + [pl.BlockSpec((half, columns), place)] * pieces,
        ),
        out_shape=[
            jax.ShapeDtypeStruct((rows, width), bf16),
            jax.ShapeDtypeStruct((rows, width), f32),
            jax.ShapeDtypeStruct((2, width), f32),
        ]
        + [jax.ShapeDtypeStruct((rows, columns), bf16)] * pieces,
        compiler_params=pltpu.CompilerParams(vmem_limit_bytes=VMEM),
        cost_estimate=cost(1e8),
        name="norm_back",
    )(scalars, *sources, above, values, vectors, weights)


def last_norm_back(scalars, first, second, above, values, vectors, places):
    rows, width = values.shape
    count = places.shape[0]
    block = width // count

    def body(scalars_ref, first_ref, second_ref, above_ref, values_ref, vectors_ref, places_ref, out_ref):
        core = scalars_ref[1]
        half = rows // 2
        for ref, far in ((first_ref, core), (second_ref, 1 - core)):
            for part in tiles_of(half, 128):
                size = part.stop - part.start
                at = pl.ds(pl.multiple_of(far * half + part.start, 128), size)
                normal, factor = normalized(values_ref[at, :].astype(f32))
                grad = norm_backward(ref[part, :].astype(f32), normal, factor, vectors_ref[0:1, :])
                out = above_ref[at, :] + grad
                if block % 128:
                    out_ref[at, :] = out
                else:
                    for k in range(count):
                        to = pl.ds(pl.multiple_of(places_ref[k] * block, 128), block)
                        out_ref[at, to] = out[:, k * block : (k + 1) * block]

    ins = [first, second, above, values, vectors, places]
    outs = [((rows, width), f32)]
    return kernel_call(body, ins, outs, scalars, name="last_norm_back", spaces={5: pltpu.SMEM})[0]


def first_partial(scalars, gq, gkv, weights, normal):
    rows, width = normal.shape
    tile = rows // 4

    def body(scalars_ref, gq_ref, gkv_ref, w_ref, normal_ref, *outs):
        grad = nt(jnp.concatenate([gq_ref[...], gkv_ref[...]], 1), w_ref[...])
        *out_refs, sums_ref = outs
        core_store(out_refs, grad.astype(bf16))
        sums = [jnp.sum(grad * normal_ref[...], 0, keepdims=True), jnp.sum(grad, 0, keepdims=True)]
        step = pl.program_id(0)
        for n, item in enumerate(sums):
            sums_ref[n : n + 1, :] = jnp.where(step == 0, item, sums_ref[n : n + 1, :] + item)

    row = lambda i, scalars: (2 * (i % 2) + rows_by_core(scalars, i), 0)
    full = lambda i, scalars: (0, 0)
    out_specs, out_shapes = core_outputs(tile, width)
    return pl.pallas_call(
        body,
        grid_spec=pltpu.PrefetchScalarGridSpec(
            num_scalar_prefetch=1,
            grid=(4,),
            in_specs=[
                pl.BlockSpec((tile, gq.shape[1]), row),
                pl.BlockSpec((tile, gkv.shape[1]), row),
                pl.BlockSpec(weights.shape, full),
                pl.BlockSpec((tile, width), row),
            ],
            out_specs=out_specs + [pl.BlockSpec((2, width), full)],
        ),
        out_shape=out_shapes + [jax.ShapeDtypeStruct((2, width), f32)],
        compiler_params=pltpu.CompilerParams(vmem_limit_bytes=VMEM),
        cost_estimate=cost(1e8),
        name="first_partial",
    )(scalars, gq, gkv, weights, normal)


def first_shards(scalars, self_in, gain, bias):
    count, rows, columns = self_in.shape
    half = columns // 2

    def body(scalars_ref, w_ref, gain_ref, bias_ref, out_ref, table):
        at = pl.ds(pl.multiple_of(scalars_ref[0] * half, 128), half)
        for n in range(count):
            out_ref[0, :, n * half : (n + 1) * half] = w_ref[n, :, at]
        table[...] = jnp.zeros_like(table)
        table[0:3, 0:rows] = gain_ref[...].astype(f32)
        table[3:6, 0:rows] = bias_ref[...].astype(f32)
        out_ref[0, :, count * half :] = table[...].T[0:rows].astype(bf16)

    outs = [((1, rows, count * half + 128), bf16)]
    scratch = [pltpu.VMEM((128, 128), f32)]
    return kernel_call(body, [self_in, gain, bias], outs, scalars, scratch, "first_shards")[0]


def other_shards(scalars, self_out, cross_in, cross_out, ffn_in, ffn_out):
    _, rows, columns = cross_in.shape
    half = columns // 2
    units = ffn_in.shape[1] // 2

    def body(scalars_ref, so_ref, cross_ref, co_ref, in_ref, out_ref, a_ref, b_ref, ffn_ref):
        ctx = scalars_ref[0]
        mine = pl.ds(pl.multiple_of(ctx * half, 128), half)
        theirs = pl.ds(pl.multiple_of((1 - ctx) * half, 128), half)
        for n in (1, 2):
            a_ref[0, :, (n - 1) * half : n * half] = cross_ref[n, :, mine]
        for n, at in enumerate((mine, theirs)):
            a_ref[0, :, (2 + n) * half : (3 + n) * half] = so_ref[at, :].T
            b_ref[0, :, n * half : (n + 1) * half] = cross_ref[0, :, at]
            b_ref[0, :, (2 + n) * half : (3 + n) * half] = co_ref[at, :].T
        at = pl.ds(pl.multiple_of(ctx * units, 128), units)
        ffn_ref[0] = in_ref[:, at]
        ffn_ref[1] = out_ref[at, :].T

    outs = [((1, rows, 2 * columns), bf16)] * 2 + [((2, rows, units), bf16)]
    ins = [self_out, cross_in, cross_out, ffn_in, ffn_out]
    return kernel_call(body, ins, outs, scalars, name="other_shards")


def ffn_results(scalars, mine, theirs):
    _, rows, units = mine[0].shape
    chunks = len(mine)

    def body(scalars_ref, *refs):
        in_ref, out_ref = refs[-2:]
        ctx = scalars_ref[0]
        for place, refs_ in ((ctx, refs[:chunks]), (1 - ctx, refs[chunks : 2 * chunks])):
            for n, ref in enumerate(refs_):
                at = pl.ds(pl.multiple_of(place * (units * chunks) + n * units, 128), units)
                in_ref[:, at] = ref[0].astype(f32)
                out_ref[at, :] = ref[1].astype(f32).T

    whole = 2 * chunks * units
    outs = [((rows, whole), f32), ((whole, rows), f32)]
    return kernel_call(body, [*mine, *theirs], outs, scalars, name="ffn_results")


def first_results(scalars, mine, theirs, half):
    _, rows, columns = mine.shape
    count = (columns - 128) // half

    def body(scalars_ref, mine_ref, theirs_ref, out_ref, gain_ref, bias_ref):
        ctx = scalars_ref[0]
        for place, ref in ((ctx, mine_ref), (1 - ctx, theirs_ref)):
            at = pl.ds(pl.multiple_of(place * half, 128), half)
            for n in range(count):
                out_ref[n, :, at] = ref[0, :, n * half : (n + 1) * half].astype(f32)
        sums = mine_ref[0, :, count * half :].astype(f32) + theirs_ref[0, :, count * half :].astype(f32)
        turned = sums.T
        for n in range(count):
            gain_ref[n : n + 1, :] = turned[2 * n : 2 * n + 1, :]
            bias_ref[n : n + 1, :] = turned[2 * n + 1 : 2 * n + 2, :]

    outs = [((count, rows, 2 * half), f32), ((count, rows), f32), ((count, rows), f32)]
    return kernel_call(body, [mine, theirs], outs, scalars, name="first_results")


def second_results(scalars, mine, theirs, half):
    _, rows, _ = mine.shape

    def body(scalars_ref, mine_ref, theirs_ref, so_ref, cross_ref, co_ref):
        ctx = scalars_ref[0]
        here = pl.multiple_of(ctx * half, 128)
        there = pl.multiple_of((1 - ctx) * half, 128)
        for at, ref in ((here, mine_ref), (there, theirs_ref)):
            for n in range(2):
                cross_ref[n + 1, :, pl.ds(at, half)] = ref[0, :, n * half : (n + 1) * half].astype(f32)
        for n, ref in enumerate((so_ref, None, co_ref)):
            start = 2 * half + 2 * n * half
            for at, a, b in ((here, start, start + half), (there, start + half, start)):
                item = mine_ref[0, :, a : a + half].astype(f32) + theirs_ref[0, :, b : b + half].astype(f32)
                if ref is None:
                    cross_ref[0, :, pl.ds(at, half)] = item
                else:
                    ref[pl.ds(at, half), :] = item.T

    outs = [((2 * half, rows), f32), ((3, rows, 2 * half), f32), ((2 * half, rows), f32)]
    return kernel_call(body, [mine, theirs], outs, scalars, name="second_results")


def move_blocks(arrays, places):
    count = places.shape[0]

    def body(places_ref, *refs):
        half = len(refs) // 2
        for in_ref, out_ref in zip(refs[:half], refs[half:]):
            width = in_ref.shape[1] // count
            for k in range(count):
                start = pl.multiple_of(places_ref[k] * width, width)
                out_ref[:, k * width : (k + 1) * width] = in_ref[:, pl.ds(start, width)]

    return pl.pallas_call(
        body,
        in_specs=[pl.BlockSpec(memory_space=pltpu.SMEM)]
        + [pl.BlockSpec(memory_space=pltpu.VMEM)] * len(arrays),
        out_specs=[pl.BlockSpec(memory_space=pltpu.VMEM)] * len(arrays),
        out_shape=[jax.ShapeDtypeStruct(a.shape, a.dtype) for a in arrays],
        compiler_params=pltpu.CompilerParams(vmem_limit_bytes=VMEM),
        cost_estimate=cost(1e8),
        name="move_blocks",
    )(places, *arrays)


def swap(values, axis):
    return lax.ppermute(values, axis, [(0, 1), (1, 0)])


class Ring:
    def __init__(self, size):
        self.size = size
        self.short = size <= RING_MOST and size % 2 == 0
        half = size // 2
        if self.short:
            self.order = [2 * p if p < half else 2 * (size - 1 - p) + 1 for p in range(size)]
        else:
            self.order = list(range(size))
        position = np.zeros(size, np.int32)
        position[self.order] = np.arange(size)
        there = np.zeros((size, size), np.int32)
        back = np.zeros((size, size), np.int32)
        for device in range(size):
            for k in range(size):
                place = self.order[(position[device] + k) % size] if self.short else k
                there[device, k] = place
                back[device, place] = k
        self.there, self.back = there, back

    def places(self, table):
        return lax.dynamic_index_in_dim(jnp.asarray(table), lax.axis_index("dp"), 0, False)

    def into(self, *arrays):
        return move_blocks(arrays, self.places(self.there)) if self.short else arrays

    def out_of(self, *arrays):
        return move_blocks(arrays, self.places(self.back)) if self.short else arrays

    def send(self, values, step):
        size, order = self.size, self.order
        pairs = [(order[p], order[(p + step) % size]) for p in range(size)]
        return lax.ppermute(values, "dp", pairs)

def far_block(ring, full):
    rows = full[1] // ring.size
    return ring.size // 2 * rows, rows, middle_cut(full[2])


def store_far(far, refs, tile, value, n=slice(None)):
    start, rows, cut = far
    step, at = start // tile, start % tile

    @pl.when(pl.program_id(0) == step)
    def _():
        refs[0][n] = value[..., at : at + rows, :cut]
        refs[1][n] = value[..., at : at + rows, cut:]


def far_outputs(far, full):
    _, rows, cut = far
    shapes = [(full[0], rows, cut), (full[0], rows, full[2] - cut)]
    specs = [pl.BlockSpec(shape, lambda i: (0, 0, 0)) for shape in shapes]
    return specs, [jax.ShapeDtypeStruct(shape, bf16) for shape in shapes]


class Order:
    def __init__(self):
        self.mark = None

    def pin(self, *arrays):
        if self.mark is not None:
            _, arrays = hold((self.mark, arrays))
        return arrays if len(arrays) > 1 else arrays[0]

    def ran(self, result):
        self.mark = result
        return result

    def step(self, run, *arrays):
        if self.mark is not None:
            _, arrays = hold((self.mark, arrays))
        return self.ran(run(*arrays))


def middle_cut(columns):
    return columns // 2 // 128 * 128


class Gather:
    def __init__(self, ring, order, shard):
        self.ring, self.order, self.shard = ring, order, shard
        self.places, self.arrays = [(0, 0)], [shard]
        self.hop = 0
        if not ring.short:
            self.arrays = [lax.all_gather(shard, "dp", axis=1, tiled=True)]

    def advance(self):
        ring, size, rows = self.ring, self.ring.size, self.shard.shape[1]
        if not ring.short or self.hop > size // 2:
            return
        if self.hop == 0:
            self.ahead = self.behind = self.order.pin(self.shard)
        else:
            self.ahead, self.behind = self.order.ran(self.order.pin(self.ahead, self.behind))
            if self.hop < size // 2:
                self.places += [(self.hop * rows, 0), ((size - self.hop) * rows, 0)]
            else:
                cut = middle_cut(self.shard.shape[2])
                self.places += [(size // 2 * rows, 0), (size // 2 * rows, cut)]
            self.arrays += [self.ahead, self.behind]
        self.hop += 1
        if self.hop == size // 2:
            cut = middle_cut(self.shard.shape[2])
            self.ahead, self.behind = self.ahead[..., :cut], self.behind[..., cut:]
        if self.hop <= size // 2:
            self.ahead = ring.send(self.ahead, -1)
            self.behind = ring.send(self.behind, 1)

    def pieces(self):
        return self.places, self.arrays


def ring_add(full, ahead, behind, hop, size):
    count, rows, columns = full.shape
    rows = rows // size
    last = hop == 0
    cut = ahead.shape[2]

    def body(up_ref, down_ref, ahead_ref, behind_ref, *out_refs):
        if last:
            out = up_ref[...].astype(f32) + (ahead_ref[...].astype(f32) + behind_ref[...].astype(f32))
            out_refs[0][...] = out.astype(bf16)
            return
        up_out, down_out = out_refs
        if cut < columns:
            up_out[..., :cut] = (up_ref[..., :cut].astype(f32) + ahead_ref[...].astype(f32)).astype(bf16)
            up_out[..., cut:] = up_ref[..., cut:]
            down_out[..., :cut] = down_ref[..., :cut]
            down_out[..., cut:] = (down_ref[..., cut:].astype(f32) + behind_ref[...].astype(f32)).astype(bf16)
        else:
            up_out[...] = (up_ref[...].astype(f32) + ahead_ref[...].astype(f32)).astype(bf16)
            down_out[...] = (down_ref[...].astype(f32) + behind_ref[...].astype(f32)).astype(bf16)

    block = (1, rows, columns)
    moved = [pl.BlockSpec((1,) + item.shape[1:], lambda i: (i, 0, 0)) for item in (ahead, behind)]
    outs = 1 if last else 2
    return pl.pallas_call(
        body,
        grid=(count,),
        in_specs=[
            pl.BlockSpec(block, lambda i: (i, hop, 0)),
            pl.BlockSpec(block, lambda i: (i, (size - hop) % size, 0)),
            *moved,
        ],
        out_specs=[pl.BlockSpec(block, lambda i: (i, 0, 0))] * outs,
        out_shape=[jax.ShapeDtypeStruct((count, rows, columns), bf16)] * outs,
        compiler_params=pltpu.CompilerParams(vmem_limit_bytes=VMEM),
        cost_estimate=cost(1e8),
        name="ring_add",
    )(full, full, ahead, behind)


class Scatter:
    def __init__(self, ring, order, grads):
        full, self.ahead, self.behind = grads
        self.ring, self.order, self.full, self.hop = ring, order, full, ring.size // 2
        if not ring.short:
            self.result = lax.psum_scatter(full, "dp", scatter_dimension=1, tiled=True)
            self.hop = -1

    def advance(self):
        ring, size = self.ring, self.ring.size
        if self.hop < 0:
            return
        if self.hop == size // 2:
            self.ahead, self.behind = self.order.pin(self.ahead, self.behind)
        else:
            run = functools.partial(ring_add, hop=self.hop, size=size)
            out = self.order.step(run, self.full, self.ahead, self.behind)
            if self.hop == 0:
                self.result, self.hop = out[0], -1
                return
            self.ahead, self.behind = out
        self.hop -= 1
        self.ahead = ring.send(self.ahead, 1)
        self.behind = ring.send(self.behind, -1)


def chain_add(items, size, ahead, behind, new):
    rows = ahead.shape[1]
    through = [item for item in items if item["hop"] == 0]
    going = [item for item in items if item["hop"] > 0]
    wide = sum(item["full"].shape[2] for item in going)
    far = new or []
    out_wide = [wide + (far[n].shape[2] if far else 0) for n in range(2)]

    def body(*refs):
        blocks = [refs[2 * n : 2 * n + 2] for n in range(len(items))]
        refs = refs[2 * len(items) :]
        (ahead_ref, behind_ref), refs = refs[:2], refs[2:]
        far_refs, outs = refs[: len(far)], refs[len(far) :]
        at = [0, 0]
        place = 0
        for item, (up_ref, down_ref) in zip(items, blocks):
            columns = item["full"].shape[2]
            widths = (item["cut"], columns - item["cut"]) if item["fresh"] else (columns, columns)
            a = ahead_ref[:, :, at[0] : at[0] + widths[0]].astype(f32)
            b = behind_ref[:, :, at[1] : at[1] + widths[1]].astype(f32)
            at = [at[0] + widths[0], at[1] + widths[1]]
            up, down = up_ref[...].astype(f32), down_ref[...].astype(f32)
            if item["hop"] == 0:
                result = outs[-len(through) :][through.index(item)]
                if item["fresh"]:
                    cut = item["cut"]
                    result[:, :, :cut] = (up[..., :cut] + a).astype(bf16)
                    result[:, :, cut:] = (up[..., cut:] + b).astype(bf16)
                else:
                    result[...] = (up + (a + b)).astype(bf16)
                continue
            spot = slice(place, place + columns)
            place += columns
            if item["fresh"]:
                cut = item["cut"]
                up = jnp.concatenate([up[..., :cut] + a, up[..., cut:]], 2)
                down = jnp.concatenate([down[..., :cut], down[..., cut:] + b], 2)
            else:
                up, down = up + a, down + b
            outs[0][:, :, spot] = up.astype(bf16)
            outs[1][:, :, spot] = down.astype(bf16)
        for n, ref in enumerate(far_refs):
            outs[n][:, :, place:] = ref[...]

    specs, arrays = [], []
    for item in items:
        block = (1, rows, item["full"].shape[2])
        hop = item["hop"]
        specs += [
            pl.BlockSpec(block, lambda i, hop=hop: (0, hop, 0)),
            pl.BlockSpec(block, lambda i, hop=hop: (0, (size - hop) % size, 0)),
        ]
        arrays += [item["full"]] * 2
    moved = [ahead, behind, *far]
    specs += [pl.BlockSpec(item.shape, lambda i: (0, 0, 0)) for item in moved]
    shapes = [(1, rows, columns) for columns in out_wide] if going or far else []
    shapes += [(1, rows, item["full"].shape[2]) for item in through]
    return pl.pallas_call(
        body,
        grid=(1,),
        in_specs=specs,
        out_specs=[pl.BlockSpec(shape, lambda i: (0, 0, 0)) for shape in shapes],
        out_shape=[jax.ShapeDtypeStruct(shape, bf16) for shape in shapes],
        compiler_params=pltpu.CompilerParams(vmem_limit_bytes=VMEM),
        cost_estimate=cost(1e8),
        name="chain_add",
    )(*arrays, *moved)


class Chain:
    def __init__(self, ring, order):
        self.ring, self.order, self.items, self.results = ring, order, [], []
        self.ahead = None

    def arrived(self):
        if self.ahead is not None:
            self.ahead, self.behind = self.order.ran(self.order.pin(self.ahead, self.behind))

    def advance(self, grads=None):
        ring, half = self.ring, self.ring.size // 2
        if not ring.short:
            if grads is not None:
                self.results.append(lax.psum_scatter(grads[0], "dp", scatter_dimension=1, tiled=True))
            return
        if self.ahead is None:
            out = self.order.pin(*grads[1:])
        else:
            far = [] if grads is None else list(grads[1:])
            items = [dict(item) for item in self.items]
            count = len(far)

            def run(ahead, behind, *arrays):
                for item, full in zip(items, arrays[count:]):
                    item["full"] = full
                return chain_add(items, ring.size, ahead, behind, list(arrays[:count]))

            fulls = [item["full"] for item in self.items]
            out = self.order.step(run, self.ahead, self.behind, *far, *fulls)
            through = sum(item["hop"] == 0 for item in self.items)
            self.results += out[len(out) - through :]
            self.items = [
                {**item, "hop": item["hop"] - 1, "fresh": False} for item in self.items if item["hop"]
            ]
        if grads is not None:
            cut = grads[1].shape[2]
            self.items.append({"full": grads[0], "hop": half - 1, "fresh": True, "cut": cut})
        if self.items:
            self.ahead, self.behind = ring.send(out[0], 1), ring.send(out[1], -1)


def per_device(
    ring,
    hidden_in,
    encoder_states,
    out_grad,
    target_ids,
    source_ids,
    self_in,
    self_out,
    cross_in,
    cross_out,
    ffn_in,
    ffn_out,
    norm_gain,
    norm_bias,
):
    ctx = lax.axis_index("ctx")
    core = lax.axis_index("tp")
    scalars = jnp.stack([ctx, core]).astype(jnp.int32)
    rows, width = hidden_in.shape
    source_rows = encoder_states.shape[0]
    inner = self_in.shape[2]
    half = inner // 2
    order = Order()

    def part(array, axis, place):
        count = array.shape[axis] // 2
        return lax.dynamic_slice_in_dim(array, place * count, count, axis)

    def ordered(mine, theirs, axis, place=ctx):
        first = place == 0
        return jnp.concatenate(
            [jnp.where(first, mine, theirs), jnp.where(first, theirs, mine)], axis
        )

    def core_swap(items):
        return [swap(item, "tp") for item in items]

    self_seen = (scalars, target_ids, target_ids, True)
    cross_seen = (scalars, target_ids, source_ids, False)

    first = Gather(ring, order, order.ran(first_shards(scalars, self_in, norm_gain, norm_bias)))
    first.advance()
    (hidden_own,) = order.step(ring.into, hidden_in)
    first.advance()
    hidden_got = swap(part(order.pin(hidden_own), 0, core), "ctx")
    shards = order.step(
        lambda *arrays: other_shards(scalars, *arrays),
        self_out,
        cross_in,
        cross_out,
        ffn_in,
        ffn_out,
    )
    second, third, ffn = [Gather(ring, order, shard) for shard in shards]
    first.advance()
    second.advance()
    cotangent, states = order.step(ring.into, out_grad, encoder_states)
    first.advance()
    hidden_got = order.ran(order.pin(hidden_got))
    hidden_rest = swap(hidden_got, "tp")
    normal_one = order.step(
        lambda *arrays: norm_rows(scalars, *arrays), hidden_own, hidden_got, hidden_rest
    )
    states_other = swap(order.pin(states), "ctx")
    second.advance()
    first.advance()
    third.advance()

    first_places, first_pieces = first.pieces()
    qkv, input_one, vectors = order.step(
        lambda normal, *arrays: first_project(normal, (first_places, arrays), 3 * half),
        normal_one,
        *first_pieces,
    )
    second.advance()
    third.advance()
    mixed_far, total_far = order.step(
        lambda qkv: attend_forward((qkv, 0), [(qkv, 1)], [(qkv, 2)], self_seen, (rows, rows)), qkv
    )
    mixed_got = swap(mixed_far, "ctx")
    second.advance()
    third.advance()
    mixed_near, total_near = order.step(
        lambda qkv: attend_forward((qkv, 0), [(qkv, 1)], [(qkv, 2)], self_seen, (0, rows)), qkv
    )
    second.advance()
    third.advance()
    source = order.step(lambda a, b: jnp.concatenate([a, b], 0), states, states_other)
    (first_w,) = order.step(
        lambda *arrays: join_pieces((first_places, arrays), [(0, 3 * half)]), *first_pieces
    )
    mixed_got = order.ran(order.pin(mixed_got))
    second_places, pieces = second.pieces()
    spans = [(0, 2 * half), (2 * half, inner)]
    key_w, self_o = order.step(
        lambda *arrays: join_pieces((second_places, arrays), spans), *pieces
    )
    third.advance()
    ffn.advance()
    kv, kv_turned = order.step(lambda a, w: row_product([a], w, swapped=True), source, key_w)
    kv_got = swap(kv_turned, "ctx")
    branch = order.step(
        lambda a, b, w: row_product([a, b], w, True, True), mixed_near, mixed_got, self_o
    )
    branch_got = core_swap(branch)

    _, pieces = third.pieces()
    spans = [(0, inner), (inner, inner)]
    cross_q, cross_o = order.step(
        lambda *arrays: join_pieces((second_places, arrays), spans), *pieces
    )
    first_rows, input_two, cross_queries = order.step(
        lambda before, a, b, c, d, *rest: branch_norm(before, (a, b), (c, d), rest[0], 1, rest[1]),
        hidden_own,
        *branch,
        *branch_got,
        vectors,
        cross_q,
    )
    kv_got = order.ran(order.pin(kv_got))
    ffn.advance()
    cotangent_other = swap(order.pin(cotangent), "ctx")
    cross_keys, cross_values = [(kv, 0), (kv_got, 0)], [(kv, 1), (kv_got, 1)]
    *mixed_two, total_two, far_total_two = order.step(
        lambda q: attend_forward((q, 0), cross_keys, cross_values, cross_seen, (0, rows)),
        cross_queries,
    )
    branch = order.step(
        lambda a, b, w: row_product([a, b], w, True, True), *mixed_two, cross_o
    )
    branch_got = core_swap(branch)
    second_rows, input_own = order.step(
        lambda before, a, b, c, d, vectors: branch_norm(before, (a, b), (c, d), vectors, 2),
        first_rows,
        *branch,
        *branch_got,
        vectors,
    )
    input_other = swap(input_own, "ctx")
    cotangent_other = order.ran(order.pin(cotangent_other))
    ffn.advance()
    input_other = order.ran(order.pin(input_other))
    ffn.advance()
    ffn.advance()
    input_three, out_cot = (input_own, input_other), (cotangent, cotangent_other)

    ffn_places, ffn_pieces = ffn.pieces()
    act, grad_up, *quarters = order.step(
        lambda a, b, c, d, *arrays: ffn_first(scalars, (a, b), (c, d), (ffn_places, arrays)),
        *input_three,
        *out_cot,
        *ffn_pieces,
    )
    taken = core_swap(quarters[:2])
    near, far = order.step(
        lambda a, b, c, d: keep_sums((a, b), (c, d)), *quarters[2:], *taken
    )
    far_got = swap(far, "ctx")
    ffn_scatter = Scatter(
        ring,
        order,
        order.step(
            lambda a, b, c, d, act, gu: ffn_grads(ring, (a, b), (c, d), act, gu),
            *input_three,
            *out_cot,
            act,
            grad_up,
        ),
    )
    ffn_scatter.advance()
    done = order.step(lambda a, b: add_up(a, b, bf16), near, far_got)
    done_got = swap(done, "tp")
    grad_branch_two, grad_second, sums_three, *grad_mixed = order.step(
        lambda a, b, *rest: norm_back(scalars, (a,), (b,), True, *rest[:3], 2, rest[3], 2),
        done,
        done_got,
        cotangent,
        second_rows,
        vectors,
        cross_o,
    )

    def cross_back(g, q, o, group, total):
        keys, values = cross_keys[group : group + 1], cross_values[group : group + 1]
        return attend_backward([g], (q, group), keys, values, [o], [total], cross_seen, group == 1)

    grad_far_q, grad_far_kv = order.step(
        lambda *arrays: cross_back(*arrays, 1, far_total_two), grad_mixed[1], cross_queries, mixed_two[1]
    )
    given = swap(grad_far_kv, "ctx")
    ffn_scatter.advance()
    grad_near_q, grad_kv = order.step(
        lambda *arrays: cross_back(*arrays, 0, total_two), grad_mixed[0], cross_queries, mixed_two[0]
    )
    branch = order.step(
        lambda a, b, w: row_product([a, b], w, True, True), grad_near_q, grad_far_q, cross_q
    )
    branch_got = core_swap(branch)
    grad_kv = order.step(lambda a, b: add_up(a, b, bf16), grad_kv, given)
    grad_branch, grad_first, sums_two, *grad_mixed = order.step(
        lambda a, b, c, d, *rest: norm_back(
            scalars, (a, b), (c, d), False, *rest[:3], 1, rest[3], 2
        ),
        *branch,
        *branch_got,
        grad_second,
        first_rows,
        vectors,
        self_o,
    )
    mixed_other = swap(grad_mixed[1], "ctx")
    ffn_scatter.advance()
    grad_third = order.step(
        lambda a, b, c, d, e, f, g, h, i, j, k: weight_grads(
            ring, [(a, [b]), (c, [d, e]), (f, [g, h]), (i, [j, k])]
        ),
        source,
        grad_kv,
        grad_branch,
        mixed_near,
        mixed_got,
        input_two,
        grad_near_q,
        grad_far_q,
        grad_branch_two,
        *mixed_two,
    )
    chain = Chain(ring, order)
    chain.advance(grad_third)
    source_low, source_far = order.step(
        lambda a, w: row_product([a], w, True, True), grad_kv, key_w
    )
    source_got = swap(source_far, "ctx")

    mixed_other = order.ran(order.pin(mixed_other))
    grad_q, grad_self_kv = order.step(
        lambda a, b, qkv: attend_backward(
            [a, b],
            (qkv, 0),
            [(qkv, 1)],
            [(qkv, 2)],
            [mixed_near, mixed_far],
            [total_near, total_far],
            self_seen,
        ),
        grad_mixed[0],
        mixed_other,
        qkv,
    )
    chain.arrived()
    source_got = order.ran(order.pin(source_got))
    ffn_scatter.advance()
    *quarters, sums_one = order.step(
        lambda *arrays: first_partial(scalars, *arrays), grad_q, grad_self_kv, first_w, normal_one
    )
    taken = core_swap(quarters[:2])
    columns = order.step(sum_columns, sums_one, swap(sums_one, "tp"), sums_two, sums_three)
    grad_first_w = order.step(
        lambda a, q, kv, columns: weight_grads(ring, [(a, [q, kv])], [columns]),
        input_one,
        grad_q,
        grad_self_kv,
        columns,
    )
    chain.advance(grad_first_w)
    near, far = order.step(
        lambda a, b, c, d: keep_sums((a, b), (c, d)), *quarters[2:], *taken
    )
    far_got = swap(far, "ctx")
    ffn_scatter.advance()
    ffn_mine = ffn_scatter.result
    ffn_got = swap(ffn_mine, "ctx")
    quarters = order.step(
        lambda act, *arrays: ffn_output(scalars, act, (ffn_places, arrays)), act, *ffn_pieces
    )
    far_got = order.ran(order.pin(far_got))
    taken = core_swap(quarters[:2])
    chain.advance()
    result_near, result_far = order.step(
        lambda a, b, c, d: keep_sums((a, b), (c, d)), *quarters[2:], *taken
    )
    result_got = swap(result_far, "ctx")
    done = order.step(lambda a, b: add_up(a, b, bf16), near, far_got)
    done_got = swap(done, "tp")
    source_low = order.step(lambda a, b: add_up(a, b, bf16), source_low, source_got)
    source_got = swap(source_low, "tp")
    back = ring.places(ring.there)
    grad_input = order.step(
        lambda *arrays: last_norm_back(scalars, *arrays, back),
        done,
        done_got,
        grad_first,
        hidden_own,
        vectors,
    )
    grad_source = order.step(lambda a, b: plain_sum([a, b], back, f32), source_low, source_got)
    chain.advance()
    result = order.step(lambda a, b: add_up(a, b, bf16), result_near, result_got)
    result_got = swap(result, "tp")
    result = order.step(
        lambda *arrays: core_sum(scalars, *arrays, back, bf16), second_rows, result, result_got
    )
    chain.advance()
    second_mine = chain.results[0]
    second_other = swap(second_mine, "ctx")
    grad_ffn_in, grad_ffn_out = order.step(
        lambda a, b: ffn_results(scalars, [a], [b]), ffn_mine, ffn_got
    )
    chain.advance()
    first_mine = chain.results[1]
    first_other = swap(first_mine, "ctx")

    grad_self_out, grad_cross_in, grad_cross_out = order.step(
        lambda a, b: second_results(scalars, a, b, half), second_mine, second_other
    )
    grad_self_in, grad_gain, grad_bias = order.step(
        lambda a, b: first_results(scalars, a, b, half), first_mine, first_other
    )
    return (
        result,
        grad_input,
        grad_source,
        grad_self_in,
        grad_self_out,
        grad_cross_in,
        grad_cross_out,
        grad_ffn_in,
        grad_ffn_out,
        grad_gain,
        grad_bias,
    )


def solution(mesh):
    return jax.shard_map(
        functools.partial(per_device, Ring(mesh.shape["dp"])),
        mesh=mesh,
        in_specs=(
            P(("dp", "ctx"), None),
            P(("dp", "ctx"), None),
            P(("dp", "ctx"), None),
            P("dp", None),
            P("dp", None),
            P(None, "dp", "tp"),
            P("tp", "dp"),
            P(None, "dp", "tp"),
            P("tp", "dp"),
            P("dp", "tp"),
            P("tp", "dp"),
            P(None, "dp"),
            P(None, "dp"),
        ),
        out_specs=(
            P(("dp", "ctx"), None),
            P(("dp", "ctx"), None),
            P(("dp", "ctx"), None),
            P(None, "dp", "tp"),
            P("tp", "dp"),
            P(None, "dp", "tp"),
            P("tp", "dp"),
            P("dp", "tp"),
            P("tp", "dp"),
            P(None, "dp"),
            P(None, "dp"),
        ),
        check_vma=False,
    )
```

```python
import functools

import jax
import jax.numpy as jnp
import numpy as np
from jax import lax
from jax.experimental import pallas as pl
from jax.experimental.pallas import tpu as pltpu
from jax.sharding import PartitionSpec as P

HEAD_DIM = 64
EPSILON = 1e-05
RING_MOST = 8
SCORE_SCALE = HEAD_DIM**-0.5 * 1.4426950408889634
MASKED = -1e30
TILE = 256
QUAD = 256
FFN_TILE = 1024
FFN_STEPS = 4
VMEM = 52 << 20

f32 = jnp.float32
bf16 = jnp.bfloat16
hold = lax.optimization_barrier


def nn(left, right):
    return jnp.dot(left, right, preferred_element_type=f32)


def tn(left, right):
    return lax.dot_general(left, right, (((0,), (0,)), ((), ())), preferred_element_type=f32)


def nt(left, right):
    return lax.dot_general(left, right, (((1,), (1,)), ((), ())), preferred_element_type=f32)


def cost(flops):
    return pl.CostEstimate(flops=int(flops), bytes_accessed=0, transcendentals=0)


def head_stack(values):
    lane = lax.broadcasted_iota(jnp.int32, values.shape, 1) // HEAD_DIM
    return jnp.concatenate(
        [jnp.where(lane == h, values, jnp.zeros_like(values)) for h in range(QUAD // HEAD_DIM)], 0
    )


def attend_forward_kernel(causal, skip, scalars, query_ids, key_ids, q_ref, *refs):
    groups = q_ref.shape[1] // QUAD
    k_refs, v_refs, refs = refs[:groups], refs[groups : 2 * groups], refs[2 * groups :]
    query_row, key_row = refs[:2]
    o_refs, lse_refs = refs[2 : 2 + groups], refs[2 + groups : 2 + 2 * groups]
    s_ref, vt_ref, qs_ref, peak_ref, total_ref, out_ref, codes_ref = refs[-7:]
    step = pl.program_id(0)
    sight = Sight(scalars, (query_ids, query_row), (key_ids, key_row), step + skip, causal)
    lo, hi = sight.bounds()
    tiles = k_refs[0].shape[0] // TILE
    per = QUAD // HEAD_DIM

    @pl.when(step == 0)
    def _():
        for t in range(tiles):
            for g in range(groups):
                span = slice(t * TILE, (t + 1) * TILE)
                vt_ref[g * QUAD : (g + 1) * QUAD, span] = v_refs[g][span, :].T
        sight.turn(codes_ref)

    peak_ref[...] = jnp.full_like(peak_ref, MASKED)
    total_ref[...] = jnp.zeros_like(total_ref)
    out_ref[...] = jnp.zeros_like(out_ref)
    for g in range(groups):
        qs_ref[g] = head_stack(q_ref[:, g * QUAD : (g + 1) * QUAD])
    for t in range(tiles):

        @pl.when(sight.needed(t))
        def _():
            span = slice(t * TILE, (t + 1) * TILE)
            code = codes_ref[span, :]
            allowed = (code >= lo) & (code <= hi)
            for g in range(groups):
                scores = nt(k_refs[g][span, :], qs_ref[g])
                for i in range(per):
                    lanes = slice(i * TILE, (i + 1) * TILE)
                    item = jnp.where(allowed, scores[:, lanes] * SCORE_SCALE, MASKED)
                    s_ref[t, g, :, lanes] = item
                    peak_ref[g : g + 1, lanes] = jnp.maximum(
                        peak_ref[g : g + 1, lanes], jnp.max(item, axis=0, keepdims=True)
                    )

    for t in range(tiles):

        @pl.when(sight.needed(t))
        def _():
            span = slice(t * TILE, (t + 1) * TILE)
            for g in range(groups):
                for i in range(per):
                    lanes = slice(i * TILE, (i + 1) * TILE)
                    h = g * per + i
                    expo = jnp.exp2(s_ref[t, g, :, lanes] - peak_ref[g : g + 1, lanes])
                    total_ref[g : g + 1, lanes] += jnp.sum(expo, axis=0, keepdims=True)
                    out_ref[h] += nn(vt_ref[h * HEAD_DIM : (h + 1) * HEAD_DIM, span], expo.astype(bf16))

    for g in range(groups):
        items = []
        for i in range(per):
            lanes = slice(i * TILE, (i + 1) * TILE)
            h = g * per + i
            total = total_ref[g : g + 1, lanes]
            lse_refs[g][i : i + 1, :] = peak_ref[g : g + 1, lanes] + jnp.log2(total)
            items.append(out_ref[h] * (1.0 / total))
        o_refs[g][...] = jnp.concatenate(items, 0).T.astype(bf16)


def tile_place(tile, count, ctx):
    half = count // TILE // 2
    return (jnp.where(tile < half, ctx, 1 - ctx) * half + tile % half) * TILE


class Sight:
    def __init__(self, scalars, query_ids, key_ids, tile, causal):
        self.ctx, self.causal = scalars[0], causal
        self.query_ids, self.key_ids = query_ids, key_ids
        self.queries, self.keys = query_ids[1].shape[1], key_ids[1].shape[1]
        self.stride = 2 * max(self.queries, self.keys)
        self.at = tile_place(tile, self.queries, self.ctx)

    def codes(self, row, at):
        at = pl.multiple_of(at, TILE)
        code = row[:, pl.ds(at, TILE)] * self.stride
        return code, code + (at + lax.broadcasted_iota(jnp.int32, (1, TILE), 1) if self.causal else 0)

    def bounds(self):
        return self.codes(self.query_ids[1], self.at)

    def turn(self, codes_ref):
        for t in range(self.keys // TILE):
            _, code = self.codes(self.key_ids[1], tile_place(t, self.keys, self.ctx))
            codes_ref[t * TILE : (t + 1) * TILE, :] = jnp.broadcast_to(code, (TILE, TILE)).T

    def needed(self, t):
        place = tile_place(t, self.keys, self.ctx)
        queries, keys = self.query_ids[0], self.key_ids[0]
        seen = (keys[place] <= queries[self.at + TILE - 1]) & (queries[self.at] <= keys[place + TILE - 1])
        return seen & (place <= self.at) if self.causal else seen


def attend_forward(q, keys, values, seen, span):
    scalars, query_ids, key_ids, causal = seen
    groups, stacked = len(keys), QUAD // HEAD_DIM * TILE
    width, depth = groups * QUAD, keys[0][0].shape[0]
    heads = width // HEAD_DIM
    start, count = span
    skip = start // TILE
    return pl.pallas_call(
        functools.partial(attend_forward_kernel, causal, skip),
        grid_spec=pltpu.PrefetchScalarGridSpec(
            num_scalar_prefetch=3,
            grid=(count // TILE,),
            in_specs=[pl.BlockSpec((TILE, width), lambda i, *_: (i + skip, q[1]))]
            + [pl.BlockSpec((depth, QUAD), lambda i, *_, n=n: (0, n)) for _, n in keys + values]
            + [pl.BlockSpec(ids.shape, lambda i, *_: (0, 0)) for ids in (query_ids, key_ids)],
            out_specs=[pl.BlockSpec((TILE, QUAD), lambda i, *_: (i, 0))] * groups
            + [pl.BlockSpec((QUAD // HEAD_DIM, TILE), lambda i, *_: (0, i))] * groups,
            scratch_shapes=[
                pltpu.VMEM((depth // TILE, groups, TILE, stacked), f32),
                pltpu.VMEM((width, depth), bf16),
                pltpu.VMEM((groups, stacked, QUAD), bf16),
                pltpu.VMEM((groups, stacked), f32),
                pltpu.VMEM((groups, stacked), f32),
                pltpu.VMEM((heads, HEAD_DIM, TILE), f32),
                pltpu.VMEM((depth, TILE), jnp.int32),
            ],
        ),
        out_shape=[jax.ShapeDtypeStruct((count, QUAD), bf16)] * groups
        + [jax.ShapeDtypeStruct((QUAD // HEAD_DIM, count), f32)] * groups,
        compiler_params=pltpu.CompilerParams(vmem_limit_bytes=VMEM),
        cost_estimate=cost(1e8),
        name="attend_forward",
    )(scalars, query_ids[0], key_ids[0], q[0], *[item for item, _ in keys + values], query_ids, key_ids)


def attend_backward_kernel(parts, turn, causal, scalars, query_ids, key_ids, q_ref, *refs):
    groups = q_ref.shape[1] // QUAD
    k_refs, v_refs, refs = refs[:groups], refs[groups : 2 * groups], refs[2 * groups :]
    rows = []
    for _ in range(3):
        rows.append(refs[:parts])
        refs = refs[parts:]
    query_row, key_row, gq_ref, *refs = refs
    gkv_refs, refs = refs[:groups], refs[groups:]
    gk_acc, gv_acc, gq_acc, qs_ref, gs_ref, inner_ref, lse_ref, p_ref, ds_ref, dst_ref, codes_ref = refs
    step = pl.program_id(0)
    sight = Sight(scalars, (query_ids, query_row), (key_ids, key_row), step, causal)
    lo, hi = sight.bounds()
    width = q_ref.shape[1]
    depth = k_refs[0].shape[0]
    tiles = depth // TILE
    per = QUAD // HEAD_DIM
    heads = width // HEAD_DIM

    @pl.when(step == 0)
    def _():
        gk_acc[...] = jnp.zeros_like(gk_acc)
        gv_acc[...] = jnp.zeros_like(gv_acc)
        sight.turn(codes_ref)

    def chosen(items):
        if len(items) == 1:
            return items[0][...]
        return jnp.where(step < pl.num_programs(0) // 2, items[0][...], items[1][...])

    gq_acc[...] = jnp.zeros_like(gq_acc)
    grad, out = chosen(rows[0]), chosen(rows[1])
    lse_ref[...] = chosen(rows[2])
    both = grad.astype(f32) * out.astype(f32)
    pick = lax.broadcasted_iota(jnp.int32, (heads, width), 0) == (
        lax.broadcasted_iota(jnp.int32, (heads, width), 1) // HEAD_DIM
    )
    inner_ref[...] = lax.dot_general(
        pick.astype(f32),
        both,
        (((1,), (1,)), ((), ())),
        precision=lax.Precision.HIGHEST,
        preferred_element_type=f32,
    )
    for g in range(groups):
        lanes = slice(g * QUAD, (g + 1) * QUAD)
        qs_ref[g] = head_stack(q_ref[:, lanes])
        gs_ref[g] = head_stack(grad[:, lanes])
    for t in range(tiles):

        @pl.when(sight.needed(t))
        def _():
            span = slice(t * TILE, (t + 1) * TILE)
            code = codes_ref[span, :]
            allowed = (code >= lo) & (code <= hi)
            for g in range(groups):
                lanes = slice(g * QUAD, (g + 1) * QUAD)
                scores = nt(k_refs[g][span, :], qs_ref[g])
                grads = nt(v_refs[g][span, :], gs_ref[g])
                for i in range(per):
                    at = slice(i * TILE, (i + 1) * TILE)
                    h = g * per + i
                    item = jnp.where(allowed, scores[:, at] * SCORE_SCALE, MASKED)
                    probs = jnp.exp2(item - lse_ref[h : h + 1, :])
                    p_ref[:, at] = probs.astype(bf16)
                    grad = (probs * (grads[:, at] - inner_ref[h : h + 1, :])).astype(bf16)
                    ds_ref[:, at] = grad
                    dst_ref[:, at] = grad.T
                gv_acc[span, lanes] += nn(p_ref[...], gs_ref[g])
                gk_acc[span, lanes] += nn(ds_ref[...], qs_ref[g])
                gq_acc[:, lanes] += nn(dst_ref[...], head_stack(k_refs[g][span, :]))

    gq_ref[...] = (gq_acc[...] * HEAD_DIM**-0.5).astype(bf16)

    @pl.when(step == pl.num_programs(0) - 1)
    def _():
        half = depth // 2
        for g, ref in enumerate(gkv_refs):
            lanes = slice(g * QUAD, (g + 1) * QUAD)
            for here in (slice(0, half), slice(half, depth)):
                there = slice(half - here.start, depth - here.start) if turn else here
                ref[there, :QUAD] = (gk_acc[here, lanes] * HEAD_DIM**-0.5).astype(bf16)
                ref[there, QUAD:] = gv_acc[here, lanes].astype(bf16)


def attend_backward(g, q, keys, values, o, lse, seen, turn=False):
    scalars, query_ids, key_ids, causal = seen
    groups, stacked = len(keys), QUAD // HEAD_DIM * TILE
    width, depth = groups * QUAD, keys[0][0].shape[0]
    rows, heads, parts = q[0].shape[0], width // HEAD_DIM, len(g)
    each = rows // TILE // parts
    row = lambda i, *_: (i, 0)
    full = lambda i, *_: (0, 0)
    places = [lambda i: jnp.clip(i, 0, each - 1), lambda i: jnp.clip(i - each, 0, each - 1)][:parts]
    tall = [pl.BlockSpec((TILE, width), lambda i, *_, at=at: (at(i), 0)) for at in places]
    flat = [pl.BlockSpec((heads, TILE), lambda i, *_, at=at: (0, at(i))) for at in places]
    return pl.pallas_call(
        functools.partial(attend_backward_kernel, parts, turn, causal),
        grid_spec=pltpu.PrefetchScalarGridSpec(
            num_scalar_prefetch=3,
            grid=(rows // TILE,),
            in_specs=[pl.BlockSpec((TILE, width), lambda i, *_: (i, q[1]))]
            + [pl.BlockSpec((depth, QUAD), lambda i, *_, n=n: (0, n)) for _, n in keys + values]
            + tall
            + tall
            + flat
            + [pl.BlockSpec(ids.shape, full) for ids in (query_ids, key_ids)],
            out_specs=[pl.BlockSpec((TILE, width), row)]
            + [pl.BlockSpec((depth, 2 * QUAD), full)] * groups,
            scratch_shapes=[
                pltpu.VMEM((depth, width), f32),
                pltpu.VMEM((depth, width), f32),
                pltpu.VMEM((TILE, width), f32),
                pltpu.VMEM((groups, stacked, QUAD), bf16),
                pltpu.VMEM((groups, stacked, QUAD), bf16),
                pltpu.VMEM((heads, TILE), f32),
                pltpu.VMEM((heads, TILE), f32),
                pltpu.VMEM((TILE, stacked), bf16),
                pltpu.VMEM((TILE, stacked), bf16),
                pltpu.VMEM((TILE, stacked), bf16),
                pltpu.VMEM((depth, TILE), jnp.int32),
            ],
        ),
        out_shape=[jax.ShapeDtypeStruct((rows, width), bf16)]
        + [jax.ShapeDtypeStruct((depth, 2 * QUAD), bf16)] * groups,
        compiler_params=pltpu.CompilerParams(vmem_limit_bytes=VMEM),
        cost_estimate=cost(1e8),
        name="attend_backward",
    )(scalars, query_ids[0], key_ids[0], q[0], *[item for item, _ in keys + values], *g, *o, *lse, query_ids, key_ids)


def gelu_pair(u):
    c = 0.7978845608028654
    square = u * u
    t = jnp.tanh(u * (c + (c * 0.044715) * square))
    half = 0.5 + 0.5 * t
    slope = half + 0.5 * u * (1.0 - t * t) * (c + (3 * c * 0.044715) * square)
    return u * half, slope


def start_pieces(places, refs, scratch, sems, which=slice(None)):
    copies = []
    for n, ((row, col), ref) in enumerate(zip(places, refs)):
        _, r, c = ref.shape
        target = scratch.at[:, pl.ds(row, r), pl.ds(col, c)]
        copies.append(pltpu.make_async_copy(ref.at[which], target, sems.at[n]))
        copies[-1].start()
    return copies


def rows_by_core(scalars, step):
    return jnp.where(step < 2, 1 - scalars[1], scalars[1])


def core_outputs(tile, width):
    specs = [pl.BlockSpec((tile, width), lambda i, scalars: (0, 0))] * 4
    return specs, [jax.ShapeDtypeStruct((tile, width), bf16)] * 4


def core_store(refs, value):
    for n, ref in enumerate(refs):

        @pl.when(pl.program_id(0) == n)
        def _():
            ref[...] = value


def ffn_first(scalars, a, g, shards):
    places, arrays = shards
    rows, width = a[0].shape
    cols = max(col + piece.shape[2] for (_, col), piece in zip(places, arrays))
    tile = rows // 2
    chunk = min(FFN_TILE, cols)
    count = len(arrays)

    def body(scalars_ref, a_ref, far_a_ref, g_ref, far_g_ref, *refs):
        pieces, (act_ref, gu_ref, *gn_refs), (w, sems) = refs[:count], refs[count:-2], refs[-2:]
        step = pl.program_id(0)

        @pl.when(step == 0)
        def _():
            copies = [
                start_pieces(places, pieces, w.at[n : n + 1], sems.at[n], slice(n, n + 1))
                for n in range(2)
            ]
            for copy in copies[0] + copies[1]:
                copy.wait()

        near = step % 2 == 0
        a, g = jnp.where(near, a_ref[...], far_a_ref[...]), jnp.where(near, g_ref[...], far_g_ref[...])
        total = jnp.zeros((tile, width), f32)
        for j in range(cols // chunk):
            span = slice(j * chunk, (j + 1) * chunk)
            act, slope = gelu_pair(nn(a, w[0, :, span]))
            act_ref[:, span] = act.astype(bf16)
            gu = (nn(g, w[1, :, span]) * slope).astype(bf16)
            gu_ref[:, span] = gu
            total = total + nt(gu, w[0, :, span])
        core_store(gn_refs, total.astype(bf16))

    block = pl.BlockSpec((tile, width), lambda i, scalars: (rows_by_core(scalars, i), 0))
    narrow = pl.BlockSpec((tile, cols), lambda i, scalars: (2 * (i % 2) + rows_by_core(scalars, i), 0))
    out_specs, out_shapes = core_outputs(tile, width)
    return pl.pallas_call(
        body,
        grid_spec=pltpu.PrefetchScalarGridSpec(
            num_scalar_prefetch=1,
            grid=(4,),
            in_specs=[block] * 4 + [pl.BlockSpec(memory_space=pltpu.HBM)] * count,
            out_specs=[narrow, narrow] + out_specs,
            scratch_shapes=[
                pltpu.VMEM((2, width, cols), bf16),
                pltpu.SemaphoreType.DMA((2, count)),
            ],
        ),
        out_shape=[jax.ShapeDtypeStruct((2 * rows, cols), bf16)] * 2 + out_shapes,
        compiler_params=pltpu.CompilerParams(vmem_limit_bytes=VMEM),
        cost_estimate=cost(1e8),
        name="ffn_first",
    )(scalars, *a, *g, *arrays)


def ffn_grads(ring, a, g, act, gu):
    rows, width = a[0].shape
    cols = act.shape[1]
    steps = FFN_STEPS
    tile = width // steps
    shape = (2, width, cols)
    far = far_block(ring, shape)

    def body(a_ref, far_a_ref, g_ref, far_g_ref, act_ref, gu_ref, dw_ref, *far_refs):
        for n, (near, other, right) in enumerate(
            ((a_ref, far_a_ref, gu_ref), (g_ref, far_g_ref, act_ref))
        ):
            left = jnp.concatenate([near[...].T, other[...].T], 1)
            grad = nn(left, right[...]).astype(bf16)
            dw_ref[n] = grad
            store_far(far, far_refs, tile, grad, n)

    full = pl.BlockSpec((2 * rows, cols), lambda i: (0, 0))
    wide = pl.BlockSpec((rows, tile), lambda i: (0, i))
    far_specs, far_shapes = far_outputs(far, shape)
    return pl.pallas_call(
        body,
        grid=(steps,),
        in_specs=[wide] * 4 + [full, full],
        out_specs=[pl.BlockSpec((2, tile, cols), lambda i: (0, i, 0))] + far_specs,
        out_shape=[jax.ShapeDtypeStruct(shape, bf16)] + far_shapes,
        compiler_params=pltpu.CompilerParams(vmem_limit_bytes=VMEM),
        cost_estimate=cost(1e8),
        name="ffn_grads",
    )(*a, *g, act, gu)


def ffn_output(scalars, act, shards):
    places, arrays = shards
    rows, cols = act.shape
    width = max(row + piece.shape[1] for (row, _), piece in zip(places, arrays))
    tile = rows // 4

    def body(scalars_ref, act_ref, *refs):
        pieces, out_refs, (w, sems) = refs[: len(places)], refs[len(places) : -2], refs[-2:]

        @pl.when(pl.program_id(0) == 0)
        def _():
            for copy in start_pieces(places, pieces, w, sems, slice(1, 2)):
                copy.wait()

        core_store(out_refs, nt(act_ref[...], w[0]).astype(bf16))

    out_specs, out_shapes = core_outputs(tile, width)
    return pl.pallas_call(
        body,
        grid_spec=pltpu.PrefetchScalarGridSpec(
            num_scalar_prefetch=1,
            grid=(4,),
            in_specs=[
                pl.BlockSpec((tile, cols), lambda i, scalars: (2 * (i % 2) + rows_by_core(scalars, i), 0))
            ]
            + [pl.BlockSpec(memory_space=pltpu.HBM)] * len(arrays),
            out_specs=out_specs,
            scratch_shapes=[
                pltpu.VMEM((1, width, cols), bf16),
                pltpu.SemaphoreType.DMA((len(arrays),)),
            ],
        ),
        out_shape=out_shapes,
        compiler_params=pltpu.CompilerParams(vmem_limit_bytes=VMEM),
        cost_estimate=cost(1e8),
        name="ffn_output",
    )(scalars, act, *arrays)


def normalized(values):
    centre = jnp.mean(values, axis=-1, keepdims=True)
    centred = values - centre
    factor = lax.rsqrt(jnp.mean(centred * centred, axis=-1, keepdims=True) + EPSILON)
    return centred * factor, factor


def norm_backward(grad_norm, normal, factor, gain):
    scaled = grad_norm * gain
    inner = (
        scaled
        - jnp.mean(scaled, axis=-1, keepdims=True)
        - normal * jnp.mean(scaled * normal, axis=-1, keepdims=True)
    )
    return factor * inner


def kernel_call(body, ins, outs, scalars=None, scratch=(), name=None, spaces=None):
    spaces = spaces or {}
    specs = [pl.BlockSpec(memory_space=spaces.get(n, pltpu.VMEM)) for n in range(len(ins))]
    out_specs = [pl.BlockSpec(memory_space=spaces.get(("out", n), pltpu.VMEM)) for n in range(len(outs))]
    if scalars is not None:
        specs = [pl.BlockSpec(memory_space=pltpu.SMEM)] + specs
        ins = [scalars] + list(ins)
    return pl.pallas_call(
        body,
        in_specs=specs,
        out_specs=out_specs,
        out_shape=[jax.ShapeDtypeStruct(*out) for out in outs],
        scratch_shapes=list(scratch),
        compiler_params=pltpu.CompilerParams(vmem_limit_bytes=VMEM),
        cost_estimate=cost(1e8),
        name=name,
    )(*ins)


def tiles_of(rows, most=256):
    tile = min(rows, most)
    return [slice(n, n + tile) for n in range(0, rows, tile)]


def norm_rows(scalars, own, got, rest):
    rows, width = own.shape
    tile = rows // 2

    def body(scalars_ref, own_ref, got_ref, rest_ref, normal_ref):
        step = pl.program_id(0)
        far = jnp.where(step - 2 == scalars_ref[1], got_ref[...], rest_ref[...])
        values = jnp.where(step < 2, own_ref[...], far)
        normal_ref[...] = normalized(values.astype(f32))[0]

    block = (tile, width)
    whole = pl.BlockSpec(block, lambda i, scalars: (0, 0))
    return pl.pallas_call(
        body,
        grid_spec=pltpu.PrefetchScalarGridSpec(
            num_scalar_prefetch=1,
            grid=(4,),
            in_specs=[pl.BlockSpec(block, lambda i, scalars: (jnp.minimum(i, 1), 0)), whole, whole],
            out_specs=pl.BlockSpec(block, lambda i, scalars: (i, 0)),
        ),
        out_shape=jax.ShapeDtypeStruct((2 * rows, width), f32),
        compiler_params=pltpu.CompilerParams(vmem_limit_bytes=VMEM),
        cost_estimate=cost(1e8),
        name="norm_rows",
    )(scalars, own, got, rest)


def row_product(parts, b, turned=False, halves=False, swapped=False):
    rows = parts[0].shape[0]
    columns = b.shape[0] if turned else b.shape[1]
    tile = rows // 2

    def body(*refs):
        a_refs, b_ref, outs = refs[: len(parts)], refs[len(parts)], refs[len(parts) + 1 :]
        a = a_refs[0][...] if len(parts) == 1 else jnp.concatenate([ref[...] for ref in a_refs], 1)
        value = (nt if turned else nn)(a, b_ref[...]).astype(bf16)
        if halves:
            core_store(outs, value)
        else:
            for ref in outs:
                ref[...] = value

    row = lambda i: (i, 0)
    block = (tile, columns)
    if halves:
        specs, shapes = [pl.BlockSpec(block, lambda i: (0, 0))] * 2, [block] * 2
    else:
        specs, shapes = [pl.BlockSpec(block, row)], [(rows, columns)]
        if swapped:
            specs.append(pl.BlockSpec(block, lambda i: (1 - i, 0)))
            shapes.append((rows, columns))
    out = pl.pallas_call(
        body,
        grid=(2,),
        in_specs=[pl.BlockSpec((tile, a.shape[1]), row) for a in parts]
        + [pl.BlockSpec(b.shape, lambda i: (0, 0))],
        out_specs=specs,
        out_shape=[jax.ShapeDtypeStruct(shape, bf16) for shape in shapes],
        compiler_params=pltpu.CompilerParams(vmem_limit_bytes=VMEM),
        cost_estimate=cost(1e8),
        name="row_product",
    )(*parts, b)
    return out if len(shapes) > 1 else out[0]


def weight_grads(ring, pairs, extra=()):
    width = pairs[0][0].shape[1]
    wide = sum(b.shape[1] for _, items in pairs for b in items) + sum(item.shape[1] for item in extra)
    steps = 4
    tile = width // steps
    shape = (1, width, wide)
    far = far_block(ring, shape)

    def body(*refs):
        refs, (out_ref, *far_refs) = list(refs[:-3]), refs[-3:]
        start = 0
        for _, items in pairs:
            left = refs.pop(0)[...].T
            for item in items:
                stop = start + item.shape[1]
                out_ref[0, :, start:stop] = nn(left, refs.pop(0)[...]).astype(bf16)
                start = stop
        for ref in refs:
            out_ref[0, :, start:] = ref[...]
        store_far(far, far_refs, tile, out_ref)

    specs, arrays = [], []
    for a, items in pairs:
        specs.append(pl.BlockSpec((a.shape[0], tile), lambda i: (0, i)))
        specs += [pl.BlockSpec(b.shape, lambda i: (0, 0)) for b in items]
        arrays += [a, *items]
    specs += [pl.BlockSpec((tile, item.shape[1]), lambda i: (i, 0)) for item in extra]
    arrays += extra
    far_specs, far_shapes = far_outputs(far, shape)
    return pl.pallas_call(
        body,
        grid=(steps,),
        in_specs=specs,
        out_specs=[pl.BlockSpec((1, tile, wide), lambda i: (0, i, 0))] + far_specs,
        out_shape=[jax.ShapeDtypeStruct(shape, bf16)] + far_shapes,
        compiler_params=pltpu.CompilerParams(vmem_limit_bytes=VMEM),
        cost_estimate=cost(1e8),
        name="weight_grads",
    )(*arrays)


def add_up(mine, other, kind, name="add_up"):
    def body(mine_ref, other_ref, out_ref):
        out_ref[...] = (mine_ref[...].astype(f32) + other_ref[...].astype(f32)).astype(kind)

    return kernel_call(body, [mine, other], [(mine.shape, kind)], name=name)[0]


def plain_sum(arrays, places, kind):
    rows, width = arrays[0].shape
    count = places.shape[0]
    block = width // count
    tile = 256

    def body(places_ref, *refs):
        *in_refs, out_ref = refs
        items = [ref[...].astype(f32) for ref in in_refs]
        total = items[-2] + items[-1]
        for item in items[:-2]:
            total = item + total
        if block % 128:
            out_ref[...] = total.astype(kind)
            return
        for k in range(count):
            at = pl.ds(pl.multiple_of(places_ref[k] * block, 128), block)
            out_ref[:, at] = total[:, k * block : (k + 1) * block].astype(kind)

    spec = pl.BlockSpec((tile, width), lambda i, places: (i, 0))
    return pl.pallas_call(
        body,
        grid_spec=pltpu.PrefetchScalarGridSpec(
            num_scalar_prefetch=1,
            grid=(rows // tile,),
            in_specs=[spec] * len(arrays),
            out_specs=spec,
        ),
        out_shape=jax.ShapeDtypeStruct((rows, width), kind),
        compiler_params=pltpu.CompilerParams(vmem_limit_bytes=VMEM),
        cost_estimate=cost(1e8),
        name="plain_sum",
    )(places, *arrays)


def core_sum(scalars, base, mine, got, places, kind):
    rows, width = base.shape
    count = places.shape[0]
    block = width // count
    tile = rows // 2

    def body(scalars_ref, places_ref, base_ref, mine_ref, got_ref, out_ref):
        own = pl.program_id(0) == scalars_ref[1]
        total = base_ref[...] + jnp.where(own, mine_ref[...], got_ref[...]).astype(f32)
        if block % 128:
            out_ref[...] = total.astype(kind)
            return
        for k in range(count):
            at = pl.ds(pl.multiple_of(places_ref[k] * block, 128), block)
            out_ref[:, at] = total[:, k * block : (k + 1) * block].astype(kind)

    spec = pl.BlockSpec((tile, width), lambda i, *_: (i, 0))
    whole = pl.BlockSpec((tile, width), lambda i, *_: (0, 0))
    return pl.pallas_call(
        body,
        grid_spec=pltpu.PrefetchScalarGridSpec(
            num_scalar_prefetch=2,
            grid=(2,),
            in_specs=[spec, whole, whole],
            out_specs=spec,
        ),
        out_shape=jax.ShapeDtypeStruct((rows, width), kind),
        compiler_params=pltpu.CompilerParams(vmem_limit_bytes=VMEM),
        cost_estimate=cost(1e8),
        name="core_sum",
    )(scalars, places, base, mine, got)


def keep_sums(kept, taken):
    def body(near_ref, far_ref, near_got, far_got, near_out, far_out):
        near_out[...] = near_ref[...].astype(f32) + near_got[...].astype(f32)
        far_out[...] = (far_ref[...].astype(f32) + far_got[...].astype(f32)).astype(bf16)

    shape = kept[0].shape
    return kernel_call(body, [*kept, *taken], [(shape, f32), (shape, bf16)], name="keep_sums")


def sum_columns(one, other, two, three):
    width = one.shape[1]

    def body(one_ref, other_ref, two_ref, three_ref, out_ref, table):
        table[...] = jnp.zeros_like(table)
        table[0:2, :] = one_ref[...] + other_ref[...]
        table[2:4, :] = two_ref[...]
        table[4:6, :] = three_ref[...]
        out_ref[...] = table[...].T.astype(bf16)

    scratch = [pltpu.VMEM((128, width), f32)]
    ins = [one, other, two, three]
    return kernel_call(body, ins, [((width, 128), bf16)], None, scratch, "sum_columns")[0]


def first_project(normal, shards, columns):
    places, pieces = shards
    rows, width = normal.shape
    total = pieces[0].shape[2]
    tile = 256

    def body(normal_ref, *refs):
        pieces, (qkv_ref, low_ref, vectors_ref, w, sems) = refs[: len(places)], refs[len(places) :]

        @pl.when(pl.program_id(0) == 0)
        def _():
            for copy in start_pieces(places, pieces, w, sems):
                copy.wait()
            vectors_ref[...] = w[0, :, columns:].astype(f32).T[:8]

        low = (normal_ref[...] * vectors_ref[0:1, :] + vectors_ref[3:4, :]).astype(bf16)
        low_ref[...] = low
        qkv_ref[...] = nn(low, w[0, :, :columns]).astype(bf16)

    row = lambda i: (i, 0)
    return pl.pallas_call(
        body,
        grid=(rows // tile,),
        in_specs=[pl.BlockSpec((tile, width), row)] + [pl.BlockSpec(memory_space=pltpu.HBM)] * len(pieces),
        out_specs=[
            pl.BlockSpec((tile, columns), row),
            pl.BlockSpec((tile, width), row),
            pl.BlockSpec((8, width), lambda i: (0, 0)),
        ],
        out_shape=[
            jax.ShapeDtypeStruct((rows, columns), bf16),
            jax.ShapeDtypeStruct((rows, width), bf16),
            jax.ShapeDtypeStruct((8, width), f32),
        ],
        scratch_shapes=[
            pltpu.VMEM((1, width, total), bf16),
            pltpu.SemaphoreType.DMA((len(pieces),)),
        ],
        compiler_params=pltpu.CompilerParams(vmem_limit_bytes=VMEM),
        cost_estimate=cost(1e8),
        name="first_project",
    )(normal, *pieces)


def join_pieces(shards, spans):
    places, pieces = shards
    depth = max(row + piece.shape[1] for (row, _), piece in zip(places, pieces))
    widths = [wide for _, wide in spans]

    def plan():
        for (row, col), n in zip(places, range(len(pieces))):
            _, r, c = pieces[n].shape
            for o, (start, wide) in enumerate(spans):
                low, high = max(col, start), min(col + c, start + wide)
                if low < high:
                    yield n, o, row, r, low - col, low - start, high - low

    moves = list(plan())

    def body(*refs):
        ins, outs, sems = refs[: len(pieces)], refs[len(pieces) : -1], refs[-1]
        copies = []
        for m, (n, o, row, r, source, target, wide) in enumerate(moves):
            copies.append(
                pltpu.make_async_copy(
                    ins[n].at[0, :, pl.ds(source, wide)],
                    outs[o].at[pl.ds(row, r), pl.ds(target, wide)],
                    sems.at[m],
                )
            )
            copies[-1].start()
        for copy in copies:
            copy.wait()

    spaces = {n: pltpu.HBM for n in range(len(pieces))}
    outs = [((int(depth), wide), bf16) for wide in widths]
    scratch = [pltpu.SemaphoreType.DMA((len(moves),))]
    return kernel_call(body, pieces, outs, None, scratch, "join_pieces", spaces)


def branch_norm(before, branch, got, vectors, which, weights=None):
    rows, width = before.shape
    half = rows // 2
    more = [] if weights is None else [weights]

    def body(before_ref, low_ref, high_ref, low_got, high_got, vectors_ref, *refs):
        out_ref, norm_ref = refs[len(more) : len(more) + 2]
        gain, bias = vectors_ref[which : which + 1, :], vectors_ref[3 + which : 4 + which, :]
        first = pl.program_id(0) == 0
        for part in tiles_of(half, 128):
            mine = jnp.where(first, low_ref[part, :], high_ref[part, :]).astype(f32)
            theirs = jnp.where(first, low_got[part, :], high_got[part, :]).astype(f32)
            out = before_ref[part, :].astype(f32) + (mine + theirs)
            out_ref[part, :] = out
            norm_ref[part, :] = (normalized(out)[0] * gain + bias).astype(bf16)
        if more:
            refs[-1][...] = nn(norm_ref[...], refs[0][...]).astype(bf16)

    row = lambda i: (i, 0)
    full = lambda i: (0, 0)
    block = pl.BlockSpec((half, width), row)
    whole = pl.BlockSpec((half, width), full)
    out_specs = [block, block] + [pl.BlockSpec((half, w.shape[1]), row) for w in more]
    shapes = [((rows, width), f32), ((rows, width), bf16)] + [((rows, w.shape[1]), bf16) for w in more]
    return pl.pallas_call(
        body,
        grid=(2,),
        in_specs=[block]
        + [whole] * 4
        + [pl.BlockSpec(vectors.shape, full)]
        + [pl.BlockSpec(w.shape, full) for w in more],
        out_specs=out_specs,
        out_shape=[jax.ShapeDtypeStruct(*shape) for shape in shapes],
        compiler_params=pltpu.CompilerParams(vmem_limit_bytes=VMEM),
        cost_estimate=cost(1e8),
        name="branch_norm",
    )(before, *branch, *got, vectors, *more)


def norm_back(scalars, first, second, split, above, values, vectors, which, weights, pieces):
    rows, width = values.shape
    half = rows // 2
    sources = [*first, *second]
    columns = weights.shape[1] // pieces

    def body(scalars_ref, *refs):
        source_refs, refs = refs[: len(sources)], refs[len(sources) :]
        above_ref, values_ref, vectors_ref, w_ref, low_ref, out_ref, sums_ref, *product_refs = refs
        gain = vectors_ref[which : which + 1, :]
        start = pl.program_id(0) == 0
        totals = [jnp.zeros((8, width), f32)] * 2
        for part in tiles_of(half, 128):
            size = part.stop - part.start
            grad = jnp.where(start, source_refs[0][part, :], source_refs[1][part, :]).astype(f32)
            if not split:
                other = jnp.where(start, source_refs[2][part, :], source_refs[3][part, :])
                grad = grad + other.astype(f32)
            normal, factor = normalized(values_ref[part, :].astype(f32))
            out = above_ref[part, :].astype(f32) + norm_backward(grad, normal, factor, gain)
            out_ref[part, :] = out
            low_ref[part, :] = out.astype(bf16)
            eight = lambda item: jnp.sum(item.reshape(size // 8, 8, width), axis=0)
            totals[0] = totals[0] + eight(grad * normal)
            totals[1] = totals[1] + eight(grad)
        for n in range(2):
            total = jnp.sum(totals[n], axis=0, keepdims=True)
            sums_ref[n : n + 1, :] = jnp.where(start, total, sums_ref[n : n + 1, :] + total)
        for n, ref in enumerate(product_refs):
            at = slice(n * columns, (n + 1) * columns)
            ref[...] = nn(low_ref[...], w_ref[:, at]).astype(bf16)

    place = lambda i, scalars: (jnp.where(i == 0, scalars[1], 1 - scalars[1]) if split else i, 0)
    full = lambda i, scalars: (0, 0)
    block = pl.BlockSpec((half, width), place)
    return pl.pallas_call(
        body,
        grid_spec=pltpu.PrefetchScalarGridSpec(
            num_scalar_prefetch=1,
            grid=(2,),
            in_specs=[pl.BlockSpec((half, width), full)] * len(sources)
            + [block, block, pl.BlockSpec(vectors.shape, full), pl.BlockSpec(weights.shape, full)],
            out_specs=[block, block, pl.BlockSpec((2, width), full)]
            + [pl.BlockSpec((half, columns), place)] * pieces,
        ),
        out_shape=[
            jax.ShapeDtypeStruct((rows, width), bf16),
            jax.ShapeDtypeStruct((rows, width), f32),
            jax.ShapeDtypeStruct((2, width), f32),
        ]
        + [jax.ShapeDtypeStruct((rows, columns), bf16)] * pieces,
        compiler_params=pltpu.CompilerParams(vmem_limit_bytes=VMEM),
        cost_estimate=cost(1e8),
        name="norm_back",
    )(scalars, *sources, above, values, vectors, weights)


def last_norm_back(scalars, first, second, above, values, vectors, places):
    rows, width = values.shape
    count = places.shape[0]
    block = width // count

    def body(scalars_ref, first_ref, second_ref, above_ref, values_ref, vectors_ref, places_ref, out_ref):
        core = scalars_ref[1]
        half = rows // 2
        for ref, far in ((first_ref, core), (second_ref, 1 - core)):
            for part in tiles_of(half, 128):
                size = part.stop - part.start
                at = pl.ds(pl.multiple_of(far * half + part.start, 128), size)
                normal, factor = normalized(values_ref[at, :].astype(f32))
                grad = norm_backward(ref[part, :].astype(f32), normal, factor, vectors_ref[0:1, :])
                out = above_ref[at, :] + grad
                if block % 128:
                    out_ref[at, :] = out
                else:
                    for k in range(count):
                        to = pl.ds(pl.multiple_of(places_ref[k] * block, 128), block)
                        out_ref[at, to] = out[:, k * block : (k + 1) * block]

    ins = [first, second, above, values, vectors, places]
    outs = [((rows, width), f32)]
    return kernel_call(body, ins, outs, scalars, name="last_norm_back", spaces={5: pltpu.SMEM})[0]


def first_partial(scalars, gq, gkv, weights, normal):
    rows, width = normal.shape
    tile = rows // 4

    def body(scalars_ref, gq_ref, gkv_ref, w_ref, normal_ref, *outs):
        grad = nt(jnp.concatenate([gq_ref[...], gkv_ref[...]], 1), w_ref[...])
        *out_refs, sums_ref = outs
        core_store(out_refs, grad.astype(bf16))
        sums = [jnp.sum(grad * normal_ref[...], 0, keepdims=True), jnp.sum(grad, 0, keepdims=True)]
        step = pl.program_id(0)
        for n, item in enumerate(sums):
            sums_ref[n : n + 1, :] = jnp.where(step == 0, item, sums_ref[n : n + 1, :] + item)

    row = lambda i, scalars: (2 * (i % 2) + rows_by_core(scalars, i), 0)
    full = lambda i, scalars: (0, 0)
    out_specs, out_shapes = core_outputs(tile, width)
    return pl.pallas_call(
        body,
        grid_spec=pltpu.PrefetchScalarGridSpec(
            num_scalar_prefetch=1,
            grid=(4,),
            in_specs=[
                pl.BlockSpec((tile, gq.shape[1]), row),
                pl.BlockSpec((tile, gkv.shape[1]), row),
                pl.BlockSpec(weights.shape, full),
                pl.BlockSpec((tile, width), row),
            ],
            out_specs=out_specs + [pl.BlockSpec((2, width), full)],
        ),
        out_shape=out_shapes + [jax.ShapeDtypeStruct((2, width), f32)],
        compiler_params=pltpu.CompilerParams(vmem_limit_bytes=VMEM),
        cost_estimate=cost(1e8),
        name="first_partial",
    )(scalars, gq, gkv, weights, normal)


def first_shards(scalars, self_in, gain, bias):
    count, rows, columns = self_in.shape
    half = columns // 2

    def body(scalars_ref, w_ref, gain_ref, bias_ref, out_ref, table):
        at = pl.ds(pl.multiple_of(scalars_ref[0] * half, 128), half)
        for n in range(count):
            out_ref[0, :, n * half : (n + 1) * half] = w_ref[n, :, at]
        table[...] = jnp.zeros_like(table)
        table[0:3, 0:rows] = gain_ref[...].astype(f32)
        table[3:6, 0:rows] = bias_ref[...].astype(f32)
        out_ref[0, :, count * half :] = table[...].T[0:rows].astype(bf16)

    outs = [((1, rows, count * half + 128), bf16)]
    scratch = [pltpu.VMEM((128, 128), f32)]
    return kernel_call(body, [self_in, gain, bias], outs, scalars, scratch, "first_shards")[0]


def other_shards(scalars, self_out, cross_in, cross_out, ffn_in, ffn_out):
    _, rows, columns = cross_in.shape
    half = columns // 2
    units = ffn_in.shape[1] // 2

    def body(scalars_ref, so_ref, cross_ref, co_ref, in_ref, out_ref, a_ref, b_ref, ffn_ref):
        ctx = scalars_ref[0]
        mine = pl.ds(pl.multiple_of(ctx * half, 128), half)
        theirs = pl.ds(pl.multiple_of((1 - ctx) * half, 128), half)
        for n in (1, 2):
            a_ref[0, :, (n - 1) * half : n * half] = cross_ref[n, :, mine]
        for n, at in enumerate((mine, theirs)):
            a_ref[0, :, (2 + n) * half : (3 + n) * half] = so_ref[at, :].T
            b_ref[0, :, n * half : (n + 1) * half] = cross_ref[0, :, at]
            b_ref[0, :, (2 + n) * half : (3 + n) * half] = co_ref[at, :].T
        at = pl.ds(pl.multiple_of(ctx * units, 128), units)
        ffn_ref[0] = in_ref[:, at]
        ffn_ref[1] = out_ref[at, :].T

    outs = [((1, rows, 2 * columns), bf16)] * 2 + [((2, rows, units), bf16)]
    ins = [self_out, cross_in, cross_out, ffn_in, ffn_out]
    return kernel_call(body, ins, outs, scalars, name="other_shards")


def ffn_results(scalars, mine, theirs):
    _, rows, units = mine[0].shape
    chunks = len(mine)

    def body(scalars_ref, *refs):
        in_ref, out_ref = refs[-2:]
        ctx = scalars_ref[0]
        for place, refs_ in ((ctx, refs[:chunks]), (1 - ctx, refs[chunks : 2 * chunks])):
            for n, ref in enumerate(refs_):
                at = pl.ds(pl.multiple_of(place * (units * chunks) + n * units, 128), units)
                in_ref[:, at] = ref[0].astype(f32)
                out_ref[at, :] = ref[1].astype(f32).T

    whole = 2 * chunks * units
    outs = [((rows, whole), f32), ((whole, rows), f32)]
    return kernel_call(body, [*mine, *theirs], outs, scalars, name="ffn_results")


def first_results(scalars, mine, theirs, half):
    _, rows, columns = mine.shape
    count = (columns - 128) // half

    def body(scalars_ref, mine_ref, theirs_ref, out_ref, gain_ref, bias_ref):
        ctx = scalars_ref[0]
        for place, ref in ((ctx, mine_ref), (1 - ctx, theirs_ref)):
            at = pl.ds(pl.multiple_of(place * half, 128), half)
            for n in range(count):
                out_ref[n, :, at] = ref[0, :, n * half : (n + 1) * half].astype(f32)
        sums = mine_ref[0, :, count * half :].astype(f32) + theirs_ref[0, :, count * half :].astype(f32)
        turned = sums.T
        for n in range(count):
            gain_ref[n : n + 1, :] = turned[2 * n : 2 * n + 1, :]
            bias_ref[n : n + 1, :] = turned[2 * n + 1 : 2 * n + 2, :]

    outs = [((count, rows, 2 * half), f32), ((count, rows), f32), ((count, rows), f32)]
    return kernel_call(body, [mine, theirs], outs, scalars, name="first_results")


def second_results(scalars, mine, theirs, half):
    _, rows, _ = mine.shape

    def body(scalars_ref, mine_ref, theirs_ref, so_ref, cross_ref, co_ref):
        ctx = scalars_ref[0]
        here = pl.multiple_of(ctx * half, 128)
        there = pl.multiple_of((1 - ctx) * half, 128)
        for at, ref in ((here, mine_ref), (there, theirs_ref)):
            for n in range(2):
                cross_ref[n + 1, :, pl.ds(at, half)] = ref[0, :, n * half : (n + 1) * half].astype(f32)
        for n, ref in enumerate((so_ref, None, co_ref)):
            start = 2 * half + 2 * n * half
            for at, a, b in ((here, start, start + half), (there, start + half, start)):
                item = mine_ref[0, :, a : a + half].astype(f32) + theirs_ref[0, :, b : b + half].astype(f32)
                if ref is None:
                    cross_ref[0, :, pl.ds(at, half)] = item
                else:
                    ref[pl.ds(at, half), :] = item.T

    outs = [((2 * half, rows), f32), ((3, rows, 2 * half), f32), ((2 * half, rows), f32)]
    return kernel_call(body, [mine, theirs], outs, scalars, name="second_results")


def move_blocks(arrays, places):
    count = places.shape[0]

    def body(places_ref, *refs):
        half = len(refs) // 2
        for in_ref, out_ref in zip(refs[:half], refs[half:]):
            width = in_ref.shape[1] // count
            for k in range(count):
                start = pl.multiple_of(places_ref[k] * width, width)
                out_ref[:, k * width : (k + 1) * width] = in_ref[:, pl.ds(start, width)]

    return pl.pallas_call(
        body,
        in_specs=[pl.BlockSpec(memory_space=pltpu.SMEM)]
        + [pl.BlockSpec(memory_space=pltpu.VMEM)] * len(arrays),
        out_specs=[pl.BlockSpec(memory_space=pltpu.VMEM)] * len(arrays),
        out_shape=[jax.ShapeDtypeStruct(a.shape, a.dtype) for a in arrays],
        compiler_params=pltpu.CompilerParams(vmem_limit_bytes=VMEM),
        cost_estimate=cost(1e8),
        name="move_blocks",
    )(places, *arrays)


def swap(values, axis):
    return lax.ppermute(values, axis, [(0, 1), (1, 0)])


class Ring:
    def __init__(self, size):
        self.size = size
        self.short = size <= RING_MOST and size % 2 == 0
        half = size // 2
        if self.short:
            self.order = [2 * p if p < half else 2 * (size - 1 - p) + 1 for p in range(size)]
        else:
            self.order = list(range(size))
        position = np.zeros(size, np.int32)
        position[self.order] = np.arange(size)
        there = np.zeros((size, size), np.int32)
        back = np.zeros((size, size), np.int32)
        for device in range(size):
            for k in range(size):
                place = self.order[(position[device] + k) % size] if self.short else k
                there[device, k] = place
                back[device, place] = k
        self.there, self.back = there, back

    def places(self, table):
        return lax.dynamic_index_in_dim(jnp.asarray(table), lax.axis_index("dp"), 0, False)

    def into(self, *arrays):
        return move_blocks(arrays, self.places(self.there)) if self.short else arrays

    def out_of(self, *arrays):
        return move_blocks(arrays, self.places(self.back)) if self.short else arrays

    def send(self, values, step):
        size, order = self.size, self.order
        pairs = [(order[p], order[(p + step) % size]) for p in range(size)]
        return lax.ppermute(values, "dp", pairs)

def far_block(ring, full):
    rows = full[1] // ring.size
    return ring.size // 2 * rows, rows, middle_cut(full[2])


def store_far(far, refs, tile, value, n=slice(None)):
    start, rows, cut = far
    step, at = start // tile, start % tile

    @pl.when(pl.program_id(0) == step)
    def _():
        refs[0][n] = value[..., at : at + rows, :cut]
        refs[1][n] = value[..., at : at + rows, cut:]


def far_outputs(far, full):
    _, rows, cut = far
    shapes = [(full[0], rows, cut), (full[0], rows, full[2] - cut)]
    specs = [pl.BlockSpec(shape, lambda i: (0, 0, 0)) for shape in shapes]
    return specs, [jax.ShapeDtypeStruct(shape, bf16) for shape in shapes]


class Order:
    def __init__(self):
        self.mark = None

    def pin(self, *arrays):
        if self.mark is not None:
            _, arrays = hold((self.mark, arrays))
        return arrays if len(arrays) > 1 else arrays[0]

    def ran(self, result):
        self.mark = result
        return result

    def step(self, run, *arrays):
        if self.mark is not None:
            _, arrays = hold((self.mark, arrays))
        return self.ran(run(*arrays))


def middle_cut(columns):
    return columns // 2 // 128 * 128


class Gather:
    def __init__(self, ring, order, shard):
        self.ring, self.order, self.shard = ring, order, shard
        self.places, self.arrays = [(0, 0)], [shard]
        self.hop = 0
        if not ring.short:
            self.arrays = [lax.all_gather(shard, "dp", axis=1, tiled=True)]

    def advance(self):
        ring, size, rows = self.ring, self.ring.size, self.shard.shape[1]
        if not ring.short or self.hop > size // 2:
            return
        if self.hop == 0:
            self.ahead = self.behind = self.order.pin(self.shard)
        else:
            self.ahead, self.behind = self.order.ran(self.order.pin(self.ahead, self.behind))
            if self.hop < size // 2:
                self.places += [(self.hop * rows, 0), ((size - self.hop) * rows, 0)]
            else:
                cut = middle_cut(self.shard.shape[2])
                self.places += [(size // 2 * rows, 0), (size // 2 * rows, cut)]
            self.arrays += [self.ahead, self.behind]
        self.hop += 1
        if self.hop == size // 2:
            cut = middle_cut(self.shard.shape[2])
            self.ahead, self.behind = self.ahead[..., :cut], self.behind[..., cut:]
        if self.hop <= size // 2:
            self.ahead = ring.send(self.ahead, -1)
            self.behind = ring.send(self.behind, 1)

    def pieces(self):
        return self.places, self.arrays


def ring_add(full, ahead, behind, hop, size):
    count, rows, columns = full.shape
    rows = rows // size
    last = hop == 0
    cut = ahead.shape[2]

    def body(up_ref, down_ref, ahead_ref, behind_ref, *out_refs):
        if last:
            out = up_ref[...].astype(f32) + (ahead_ref[...].astype(f32) + behind_ref[...].astype(f32))
            out_refs[0][...] = out.astype(bf16)
            return
        up_out, down_out = out_refs
        if cut < columns:
            up_out[..., :cut] = (up_ref[..., :cut].astype(f32) + ahead_ref[...].astype(f32)).astype(bf16)
            up_out[..., cut:] = up_ref[..., cut:]
            down_out[..., :cut] = down_ref[..., :cut]
            down_out[..., cut:] = (down_ref[..., cut:].astype(f32) + behind_ref[...].astype(f32)).astype(bf16)
        else:
            up_out[...] = (up_ref[...].astype(f32) + ahead_ref[...].astype(f32)).astype(bf16)
            down_out[...] = (down_ref[...].astype(f32) + behind_ref[...].astype(f32)).astype(bf16)

    block = (1, rows, columns)
    moved = [pl.BlockSpec((1,) + item.shape[1:], lambda i: (i, 0, 0)) for item in (ahead, behind)]
    outs = 1 if last else 2
    return pl.pallas_call(
        body,
        grid=(count,),
        in_specs=[
            pl.BlockSpec(block, lambda i: (i, hop, 0)),
            pl.BlockSpec(block, lambda i: (i, (size - hop) % size, 0)),
            *moved,
        ],
        out_specs=[pl.BlockSpec(block, lambda i: (i, 0, 0))] * outs,
        out_shape=[jax.ShapeDtypeStruct((count, rows, columns), bf16)] * outs,
        compiler_params=pltpu.CompilerParams(vmem_limit_bytes=VMEM),
        cost_estimate=cost(1e8),
        name="ring_add",
    )(full, full, ahead, behind)


class Scatter:
    def __init__(self, ring, order, grads):
        full, self.ahead, self.behind = grads
        self.ring, self.order, self.full, self.hop = ring, order, full, ring.size // 2
        if not ring.short:
            self.result = lax.psum_scatter(full, "dp", scatter_dimension=1, tiled=True)
            self.hop = -1

    def advance(self, between=None):
        ring, size = self.ring, self.ring.size
        if self.hop < 0:
            return
        if self.hop == size // 2:
            self.ahead, self.behind = self.order.pin(self.ahead, self.behind)
        else:
            run = functools.partial(ring_add, hop=self.hop, size=size)
            out = self.order.step(run, self.full, self.ahead, self.behind)
            if self.hop == 0:
                self.result, self.hop = out[0], -1
                return
            self.ahead, self.behind = out
            if between is not None:
                between()
                self.ahead, self.behind = self.order.pin(self.ahead, self.behind)
        self.hop -= 1
        self.ahead = ring.send(self.ahead, 1)
        self.behind = ring.send(self.behind, -1)


def chain_add(items, size, ahead, behind, new):
    rows = ahead.shape[1]
    through = [item for item in items if item["hop"] == 0]
    going = [item for item in items if item["hop"] > 0]
    wide = sum(item["full"].shape[2] for item in going)
    far = new or []
    out_wide = [wide + (far[n].shape[2] if far else 0) for n in range(2)]

    def body(*refs):
        blocks = [refs[2 * n : 2 * n + 2] for n in range(len(items))]
        refs = refs[2 * len(items) :]
        (ahead_ref, behind_ref), refs = refs[:2], refs[2:]
        far_refs, outs = refs[: len(far)], refs[len(far) :]
        at = [0, 0]
        place = 0
        for item, (up_ref, down_ref) in zip(items, blocks):
            columns = item["full"].shape[2]
            widths = (item["cut"], columns - item["cut"]) if item["fresh"] else (columns, columns)
            a = ahead_ref[:, :, at[0] : at[0] + widths[0]].astype(f32)
            b = behind_ref[:, :, at[1] : at[1] + widths[1]].astype(f32)
            at = [at[0] + widths[0], at[1] + widths[1]]
            up, down = up_ref[...].astype(f32), down_ref[...].astype(f32)
            if item["hop"] == 0:
                result = outs[-len(through) :][through.index(item)]
                if item["fresh"]:
                    cut = item["cut"]
                    result[:, :, :cut] = (up[..., :cut] + a).astype(bf16)
                    result[:, :, cut:] = (up[..., cut:] + b).astype(bf16)
                else:
                    result[...] = (up + (a + b)).astype(bf16)
                continue
            spot = slice(place, place + columns)
            place += columns
            if item["fresh"]:
                cut = item["cut"]
                up = jnp.concatenate([up[..., :cut] + a, up[..., cut:]], 2)
                down = jnp.concatenate([down[..., :cut], down[..., cut:] + b], 2)
            else:
                up, down = up + a, down + b
            outs[0][:, :, spot] = up.astype(bf16)
            outs[1][:, :, spot] = down.astype(bf16)
        for n, ref in enumerate(far_refs):
            outs[n][:, :, place:] = ref[...]

    specs, arrays = [], []
    for item in items:
        block = (1, rows, item["full"].shape[2])
        hop = item["hop"]
        specs += [
            pl.BlockSpec(block, lambda i, hop=hop: (0, hop, 0)),
            pl.BlockSpec(block, lambda i, hop=hop: (0, (size - hop) % size, 0)),
        ]
        arrays += [item["full"]] * 2
    moved = [ahead, behind, *far]
    specs += [pl.BlockSpec(item.shape, lambda i: (0, 0, 0)) for item in moved]
    shapes = [(1, rows, columns) for columns in out_wide] if going or far else []
    shapes += [(1, rows, item["full"].shape[2]) for item in through]
    return pl.pallas_call(
        body,
        grid=(1,),
        in_specs=specs,
        out_specs=[pl.BlockSpec(shape, lambda i: (0, 0, 0)) for shape in shapes],
        out_shape=[jax.ShapeDtypeStruct(shape, bf16) for shape in shapes],
        compiler_params=pltpu.CompilerParams(vmem_limit_bytes=VMEM),
        cost_estimate=cost(1e8),
        name="chain_add",
    )(*arrays, *moved)


class Chain:
    def __init__(self, ring, order):
        self.ring, self.order, self.items, self.results = ring, order, [], []
        self.ahead = None

    def arrived(self):
        if self.ahead is not None:
            self.ahead, self.behind = self.order.ran(self.order.pin(self.ahead, self.behind))

    def advance(self, grads=None):
        ring, half = self.ring, self.ring.size // 2
        if not ring.short:
            if grads is not None:
                self.results.append(lax.psum_scatter(grads[0], "dp", scatter_dimension=1, tiled=True))
            return
        if self.ahead is None:
            out = self.order.pin(*grads[1:])
        else:
            far = [] if grads is None else list(grads[1:])
            items = [dict(item) for item in self.items]
            count = len(far)

            def run(ahead, behind, *arrays):
                for item, full in zip(items, arrays[count:]):
                    item["full"] = full
                return chain_add(items, ring.size, ahead, behind, list(arrays[:count]))

            fulls = [item["full"] for item in self.items]
            out = self.order.step(run, self.ahead, self.behind, *far, *fulls)
            through = sum(item["hop"] == 0 for item in self.items)
            self.results += out[len(out) - through :]
            self.items = [
                {**item, "hop": item["hop"] - 1, "fresh": False} for item in self.items if item["hop"]
            ]
        if grads is not None:
            cut = grads[1].shape[2]
            self.items.append({"full": grads[0], "hop": half - 1, "fresh": True, "cut": cut})
        if self.items:
            self.ahead, self.behind = ring.send(out[0], 1), ring.send(out[1], -1)


def per_device(
    ring,
    hidden_in,
    encoder_states,
    out_grad,
    target_ids,
    source_ids,
    self_in,
    self_out,
    cross_in,
    cross_out,
    ffn_in,
    ffn_out,
    norm_gain,
    norm_bias,
):
    ctx = lax.axis_index("ctx")
    core = lax.axis_index("tp")
    scalars = jnp.stack([ctx, core]).astype(jnp.int32)
    rows, width = hidden_in.shape
    source_rows = encoder_states.shape[0]
    inner = self_in.shape[2]
    half = inner // 2
    order = Order()

    def part(array, axis, place):
        count = array.shape[axis] // 2
        return lax.dynamic_slice_in_dim(array, place * count, count, axis)

    def ordered(mine, theirs, axis, place=ctx):
        first = place == 0
        return jnp.concatenate(
            [jnp.where(first, mine, theirs), jnp.where(first, theirs, mine)], axis
        )

    def core_swap(items):
        return [swap(item, "tp") for item in items]

    self_seen = (scalars, target_ids, target_ids, True)
    cross_seen = (scalars, target_ids, source_ids, False)

    first = Gather(ring, order, order.ran(first_shards(scalars, self_in, norm_gain, norm_bias)))
    first.advance()
    (hidden_own,) = order.step(ring.into, hidden_in)
    first.advance()
    hidden_got = swap(part(order.pin(hidden_own), 0, core), "ctx")
    shards = order.step(
        lambda *arrays: other_shards(scalars, *arrays),
        self_out,
        cross_in,
        cross_out,
        ffn_in,
        ffn_out,
    )
    second, third, ffn = [Gather(ring, order, shard) for shard in shards]
    first.advance()
    second.advance()
    cotangent, states = order.step(ring.into, out_grad, encoder_states)
    first.advance()
    hidden_got = order.ran(order.pin(hidden_got))
    hidden_rest = swap(hidden_got, "tp")
    normal_one = order.step(
        lambda *arrays: norm_rows(scalars, *arrays), hidden_own, hidden_got, hidden_rest
    )
    states_other = swap(order.pin(states), "ctx")
    second.advance()
    first.advance()
    third.advance()

    first_places, first_pieces = first.pieces()
    qkv, input_one, vectors = order.step(
        lambda normal, *arrays: first_project(normal, (first_places, arrays), 3 * half),
        normal_one,
        *first_pieces,
    )
    second.advance()
    third.advance()
    mixed_far, total_far = order.step(
        lambda qkv: attend_forward((qkv, 0), [(qkv, 1)], [(qkv, 2)], self_seen, (rows, rows)), qkv
    )
    mixed_got = swap(mixed_far, "ctx")
    second.advance()
    third.advance()
    mixed_near, total_near = order.step(
        lambda qkv: attend_forward((qkv, 0), [(qkv, 1)], [(qkv, 2)], self_seen, (0, rows)), qkv
    )
    second.advance()
    third.advance()
    source = order.step(lambda a, b: jnp.concatenate([a, b], 0), states, states_other)
    (first_w,) = order.step(
        lambda *arrays: join_pieces((first_places, arrays), [(0, 3 * half)]), *first_pieces
    )
    mixed_got = order.ran(order.pin(mixed_got))
    second_places, pieces = second.pieces()
    spans = [(0, 2 * half), (2 * half, inner)]
    key_w, self_o = order.step(
        lambda *arrays: join_pieces((second_places, arrays), spans), *pieces
    )
    third.advance()
    ffn.advance()
    kv, kv_turned = order.step(lambda a, w: row_product([a], w, swapped=True), source, key_w)
    kv_got = swap(kv_turned, "ctx")
    branch = order.step(
        lambda a, b, w: row_product([a, b], w, True, True), mixed_near, mixed_got, self_o
    )
    branch_got = core_swap(branch)

    _, pieces = third.pieces()
    spans = [(0, inner), (inner, inner)]
    cross_q, cross_o = order.step(
        lambda *arrays: join_pieces((second_places, arrays), spans), *pieces
    )
    first_rows, input_two, cross_queries = order.step(
        lambda before, a, b, c, d, *rest: branch_norm(before, (a, b), (c, d), rest[0], 1, rest[1]),
        hidden_own,
        *branch,
        *branch_got,
        vectors,
        cross_q,
    )
    kv_got = order.ran(order.pin(kv_got))
    ffn.advance()
    cotangent_other = swap(order.pin(cotangent), "ctx")
    cross_keys, cross_values = [(kv, 0), (kv_got, 0)], [(kv, 1), (kv_got, 1)]
    *mixed_two, total_two, far_total_two = order.step(
        lambda q: attend_forward((q, 0), cross_keys, cross_values, cross_seen, (0, rows)),
        cross_queries,
    )
    branch = order.step(
        lambda a, b, w: row_product([a, b], w, True, True), *mixed_two, cross_o
    )
    branch_got = core_swap(branch)
    second_rows, input_own = order.step(
        lambda before, a, b, c, d, vectors: branch_norm(before, (a, b), (c, d), vectors, 2),
        first_rows,
        *branch,
        *branch_got,
        vectors,
    )
    input_other = swap(input_own, "ctx")
    cotangent_other = order.ran(order.pin(cotangent_other))
    ffn.advance()
    input_other = order.ran(order.pin(input_other))
    ffn.advance()
    ffn.advance()
    input_three, out_cot = (input_own, input_other), (cotangent, cotangent_other)

    ffn_places, ffn_pieces = ffn.pieces()
    act, grad_up, *quarters = order.step(
        lambda a, b, c, d, *arrays: ffn_first(scalars, (a, b), (c, d), (ffn_places, arrays)),
        *input_three,
        *out_cot,
        *ffn_pieces,
    )
    taken = core_swap(quarters[:2])
    near, far = order.step(
        lambda a, b, c, d: keep_sums((a, b), (c, d)), *quarters[2:], *taken
    )
    far_got = swap(far, "ctx")
    ffn_scatter = Scatter(
        ring,
        order,
        order.step(
            lambda a, b, c, d, act, gu: ffn_grads(ring, (a, b), (c, d), act, gu),
            *input_three,
            *out_cot,
            act,
            grad_up,
        ),
    )
    ffn_scatter.advance()
    done = order.step(lambda a, b: add_up(a, b, bf16), near, far_got)
    done_got = swap(done, "tp")
    grad_branch_two, grad_second, sums_three, *grad_mixed = order.step(
        lambda a, b, *rest: norm_back(scalars, (a,), (b,), True, *rest[:3], 2, rest[3], 2),
        done,
        done_got,
        cotangent,
        second_rows,
        vectors,
        cross_o,
    )

    def cross_back(g, q, o, group, total):
        keys, values = cross_keys[group : group + 1], cross_values[group : group + 1]
        return attend_backward([g], (q, group), keys, values, [o], [total], cross_seen, group == 1)

    grad_far_q, grad_far_kv = order.step(
        lambda *arrays: cross_back(*arrays, 1, far_total_two), grad_mixed[1], cross_queries, mixed_two[1]
    )
    given = swap(grad_far_kv, "ctx")
    ffn_scatter.advance()
    grad_near_q, grad_kv = order.step(
        lambda *arrays: cross_back(*arrays, 0, total_two), grad_mixed[0], cross_queries, mixed_two[0]
    )
    branch = order.step(
        lambda a, b, w: row_product([a, b], w, True, True), grad_near_q, grad_far_q, cross_q
    )
    branch_got = core_swap(branch)
    grad_kv = order.step(lambda a, b: add_up(a, b, bf16), grad_kv, given)
    grad_branch, grad_first, sums_two, *grad_mixed = order.step(
        lambda a, b, c, d, *rest: norm_back(
            scalars, (a, b), (c, d), False, *rest[:3], 1, rest[3], 2
        ),
        *branch,
        *branch_got,
        grad_second,
        first_rows,
        vectors,
        self_o,
    )
    mixed_other = swap(grad_mixed[1], "ctx")
    ffn_scatter.advance()
    grad_third = order.step(
        lambda a, b, c, d, e, f, g, h, i, j, k: weight_grads(
            ring, [(a, [b]), (c, [d, e]), (f, [g, h]), (i, [j, k])]
        ),
        source,
        grad_kv,
        grad_branch,
        mixed_near,
        mixed_got,
        input_two,
        grad_near_q,
        grad_far_q,
        grad_branch_two,
        *mixed_two,
    )
    chain = Chain(ring, order)
    chain.advance(grad_third)
    source_low, source_far = order.step(
        lambda a, w: row_product([a], w, True, True), grad_kv, key_w
    )
    source_got = swap(source_far, "ctx")

    mixed_other = order.ran(order.pin(mixed_other))
    grad_q, grad_self_kv = order.step(
        lambda a, b, qkv: attend_backward(
            [a, b],
            (qkv, 0),
            [(qkv, 1)],
            [(qkv, 2)],
            [mixed_near, mixed_far],
            [total_near, total_far],
            self_seen,
        ),
        grad_mixed[0],
        mixed_other,
        qkv,
    )
    ffn_scatter.advance(chain.arrived)
    source_got = order.ran(order.pin(source_got))
    *quarters, sums_one = order.step(
        lambda *arrays: first_partial(scalars, *arrays), grad_q, grad_self_kv, first_w, normal_one
    )
    taken = core_swap(quarters[:2])
    columns = order.step(sum_columns, sums_one, swap(sums_one, "tp"), sums_two, sums_three)
    grad_first_w = order.step(
        lambda a, q, kv, columns: weight_grads(ring, [(a, [q, kv])], [columns]),
        input_one,
        grad_q,
        grad_self_kv,
        columns,
    )
    chain.advance(grad_first_w)
    near, far = order.step(
        lambda a, b, c, d: keep_sums((a, b), (c, d)), *quarters[2:], *taken
    )
    far_got = swap(far, "ctx")
    ffn_scatter.advance()
    ffn_mine = ffn_scatter.result
    ffn_got = swap(ffn_mine, "ctx")
    quarters = order.step(
        lambda act, *arrays: ffn_output(scalars, act, (ffn_places, arrays)), act, *ffn_pieces
    )
    far_got = order.ran(order.pin(far_got))
    taken = core_swap(quarters[:2])
    chain.advance()
    result_near, result_far = order.step(
        lambda a, b, c, d: keep_sums((a, b), (c, d)), *quarters[2:], *taken
    )
    result_got = swap(result_far, "ctx")
    done = order.step(lambda a, b: add_up(a, b, bf16), near, far_got)
    done_got = swap(done, "tp")
    source_low = order.step(lambda a, b: add_up(a, b, bf16), source_low, source_got)
    source_got = swap(source_low, "tp")
    back = ring.places(ring.there)
    grad_input = order.step(
        lambda *arrays: last_norm_back(scalars, *arrays, back),
        done,
        done_got,
        grad_first,
        hidden_own,
        vectors,
    )
    grad_source = order.step(lambda a, b: plain_sum([a, b], back, f32), source_low, source_got)
    chain.advance()
    result = order.step(lambda a, b: add_up(a, b, bf16), result_near, result_got)
    result_got = swap(result, "tp")
    result = order.step(
        lambda *arrays: core_sum(scalars, *arrays, back, bf16), second_rows, result, result_got
    )
    chain.advance()
    second_mine = chain.results[0]
    second_other = swap(second_mine, "ctx")
    chain.advance()
    first_mine = chain.results[1]
    first_other = swap(first_mine, "ctx")
    grad_ffn_in, grad_ffn_out = order.step(
        lambda a, b: ffn_results(scalars, [a], [b]), ffn_mine, ffn_got
    )

    grad_self_out, grad_cross_in, grad_cross_out = order.step(
        lambda a, b: second_results(scalars, a, b, half), second_mine, second_other
    )
    grad_self_in, grad_gain, grad_bias = order.step(
        lambda a, b: first_results(scalars, a, b, half), first_mine, first_other
    )
    return (
        result,
        grad_input,
        grad_source,
        grad_self_in,
        grad_self_out,
        grad_cross_in,
        grad_cross_out,
        grad_ffn_in,
        grad_ffn_out,
        grad_gain,
        grad_bias,
    )


def solution(mesh):
    return jax.shard_map(
        functools.partial(per_device, Ring(mesh.shape["dp"])),
        mesh=mesh,
        in_specs=(
            P(("dp", "ctx"), None),
            P(("dp", "ctx"), None),
            P(("dp", "ctx"), None),
            P("dp", None),
            P("dp", None),
            P(None, "dp", "tp"),
            P("tp", "dp"),
            P(None, "dp", "tp"),
            P("tp", "dp"),
            P("dp", "tp"),
            P("tp", "dp"),
            P(None, "dp"),
            P(None, "dp"),
        ),
        out_specs=(
            P(("dp", "ctx"), None),
            P(("dp", "ctx"), None),
            P(("dp", "ctx"), None),
            P(None, "dp", "tp"),
            P("tp", "dp"),
            P(None, "dp", "tp"),
            P("tp", "dp"),
            P("dp", "tp"),
            P("tp", "dp"),
            P(None, "dp"),
            P(None, "dp"),
        ),
        check_vma=False,
    )
```
